32 devices in a mesh: dp: 8 (over z, y), fsdp: 4 (over x, core).
Axes of the slice: x: 2, y: 2, z: 4, core: 2. Of those that a mesh axis runs over, the one named last changes fastest.
Arguments:
- tokens: bfloat16 [6144, 768], P(('dp', 'fsdp')), may hold values from -6 to 6
- lengths: int32 [32, 4], P(('dp', 'fsdp')), may hold values from 1 to 168, 192 in all within a row
- cotangent: bfloat16 [6144, 768], P(('dp', 'fsdp')), may hold values from -6 to 6
- w_qkv: bfloat16 [768, 2304], P(('dp', 'fsdp')), may hold values from -0.21875 to 0.21875
- bias_q: bfloat16 [768], P(('dp', 'fsdp')), may hold values from -3 to 3
- bias_v: bfloat16 [768], P(('dp', 'fsdp')), may hold values from -3 to 3
- w_out: bfloat16 [768, 768], P(('dp', 'fsdp')), may hold values from -0.625 to 0.625
- bias_out: bfloat16 [768], P(('dp', 'fsdp')), may hold values from -2 to 2
- gain_attn: bfloat16 [768], P(('dp', 'fsdp')), may hold values from 0.25 to 1.75
- shift_attn: bfloat16 [768], P(('dp', 'fsdp')), may hold values from -2 to 2
- gain_mlp: bfloat16 [768], P(('dp', 'fsdp')), may hold values from 0.25 to 1.75
- shift_mlp: bfloat16 [768], P(('dp', 'fsdp')), may hold values from -2 to 2
- w_up: bfloat16 [768, 3072], P(('dp', 'fsdp')), may hold values from -0.21875 to 0.21875
- bias_up: bfloat16 [3072], P(('dp', 'fsdp')), may hold values from -2 to 2
- w_down: bfloat16 [3072, 768], P(('dp', 'fsdp')), may hold values from -0.109375 to 0.109375
- bias_down: bfloat16 [768], P(('dp', 'fsdp')), may hold values from -2 to 2
- pass_embed: bfloat16 [3, 768], P(None, ('dp', 'fsdp')), may hold values from -3 to 3
Outputs:
- output: bfloat16 [6144, 768], P(('dp', 'fsdp'))
- token_grad: bfloat16 [6144, 768], P(('dp', 'fsdp'))
- grad_w_qkv: float32 [768, 2304], P(('dp', 'fsdp'))
- grad_bias_q: float32 [768], P(('dp', 'fsdp'))
- grad_bias_v: float32 [768], P(('dp', 'fsdp'))
- grad_w_out: float32 [768, 768], P(('dp', 'fsdp'))
- grad_bias_out: float32 [768], P(('dp', 'fsdp'))
- grad_gain_attn: float32 [768], P(('dp', 'fsdp'))
- grad_shift_attn: float32 [768], P(('dp', 'fsdp'))
- grad_gain_mlp: float32 [768], P(('dp', 'fsdp'))
- grad_shift_mlp: float32 [768], P(('dp', 'fsdp'))
- grad_w_up: float32 [768, 3072], P(('dp', 'fsdp'))
- grad_bias_up: float32 [3072], P(('dp', 'fsdp'))
- grad_w_down: float32 [3072, 768], P(('dp', 'fsdp'))
- grad_bias_down: float32 [768], P(('dp', 'fsdp'))
- grad_pass_embed: float32 [3, 768], P(None, ('dp', 'fsdp'))
The draws below stay inside these ranges and needn't reach their ends.
Inputs may be any that keep to these rules, and one draw needn't show every extreme that they name: The 4 lengths of each row sum to 192; in every row the longest is exactly 168.
All inputs are finite; a program needn't handle non-finite values.
Results may differ from the reference program's by a relative error of at most 0.015.
Values may be sent and summed in bfloat16 or wider, within the bound.
No kernel may reach another device: no remote copies, remote signals or barrier semaphores. Data moves between devices by JAX's collectives and lax.ppermute only.
A program may use at most 192 MiB of HBM per device.

```python
import math
import jax
import jax.numpy as jnp
import numpy as np
from jax import lax

D = 768
HEAD_DIM = 64
FF = 3072
PASSES = 3
DOCS = 4
TOK_DEV = 192
MAX_DOC = 168
ROWS = 32
TOKENS = 6144


def with_spikes(values, key, source, target, parts, factor):
    owner, partner = [(jnp.arange(values.shape[axis_at]) // (values.shape[axis_at] // parts)).reshape([-1 if axis == axis_at else 1 for axis in range(values.ndim)]) for axis_at in (source, target)]
    chosen = jax.random.permutation(key, parts)[partner]
    strong = (owner == chosen) | (owner == (partner + parts // 2) % parts)
    return jnp.where(strong, factor * values, values)


def block_scale(stream_key, extent, pieces, least, top_value):
    gain = 1.0
    for dim, blocks in pieces:
        steps = jax.random.uniform(jax.random.fold_in(jax.random.fold_in(stream_key, 6), dim), (blocks,), jnp.float32, least / len(pieces), top_value / len(pieces))
        gain = gain * jnp.repeat(jnp.exp(steps), extent[dim] // blocks).reshape((-1,) + (1,) * (len(extent) - 1 - dim))
    return gain


def profile(count, total, reach, lean):
    portions = [(1 << 20) // math.isqrt(standing ** lean) + 1 for standing in range(2, count + 1)]
    surplus, counts = total - reach - (count - 1), [1] * (count - 1)
    while surplus > 0:
        free = [i for i in range(count - 1) if counts[i] < reach]
        pool, budget = sum([portions[i] for i in free]), surplus
        for i in free:
            more = min(reach - counts[i], max(1, budget * portions[i] // pool), surplus)
            counts[i] = counts[i] + more
            surplus = surplus - more
    return np.array([reach] + counts)


def ragged_sizes(stream_key, count, total, most, slope):
    if count == 2:
        one = jax.random.randint(stream_key, (), max(1, total - most), min(most, total - 1) + 1)
        return jnp.stack([one, total - one])
    sizes = jnp.asarray(profile(count, total, most, slope), jnp.int32)
    pairs = (count - 1) // 2
    donor, sink = sizes[1:1 + 2 * pairs:2], sizes[2:2 + 2 * pairs:2]
    margin = jnp.minimum(donor - 1, most - sink)
    shifted = jax.random.randint(jax.random.fold_in(stream_key, 1), (pairs,), 0, 1 << 20) % (margin + 1)
    sizes = sizes.at[1:1 + 2 * pairs:2].set(donor - shifted).at[2:2 + 2 * pairs:2].set(sink + shifted)
    return sizes[jax.random.permutation(jax.random.fold_in(stream_key, 2), count)]


def bell_draw(rng, extent, scale, bound, cuts=(), held_as=jnp.bfloat16):
    values = jax.random.normal(rng, extent, jnp.float32) * scale
    if len(cuts) > 0:
        values = block_scale(rng, extent, cuts, -0.22, 0.18) * values
    return jnp.clip(values, min=-bound, max=bound).astype(held_as)


def bell_draw_with(stream_key, shape, deviation, bound, split, heavy, kind=jnp.bfloat16):
    values = deviation * jax.random.normal(stream_key, shape, jnp.float32)
    if split:
        values = values * block_scale(stream_key, shape, split, -0.22, 0.18)
    return jnp.clip(with_spikes(values, jax.random.fold_in(stream_key, 3), *heavy), -bound, bound).astype(kind)


def setup_inputs(seed: int = 0) -> dict:
    seeds = jax.random.split(jax.random.key(seed), 18)
    tokens = bell_draw(seeds[0], (TOKENS, D), 1.0, 6.0, ((0, 32),))
    lengths = jax.vmap(lambda own: ragged_sizes(own, DOCS, TOK_DEV, MAX_DOC, 2))(jax.random.split(seeds[1], ROWS)).reshape((ROWS, DOCS)).astype(jnp.int32)
    cotangent = bell_draw_with(seeds[2], (TOKENS, D), 1.0, 6.0, ((0, 32),), (0, 1, 32, 2.75))
    w_qkv = bell_draw(seeds[3], (D, 3 * D), D ** -0.5, 0.21875, ((0, 32),))
    bias_q = bell_draw(seeds[4], (D,), 0.5, 3.0, ((0, 32),))
    bias_v = bell_draw(seeds[5], (D,), 0.5, 3.0, ((0, 32),))
    w_out = bell_draw(seeds[6], (D, D), (D // 8) ** -0.5, 0.625, ((0, 32),))
    bias_out = bell_draw(seeds[7], (D,), 0.3, 2.0, ((0, 32),))
    gain_attn = jnp.clip(1.0 + 0.15 * jax.random.normal(seeds[8], (D,), jnp.float32), 0.25, 1.75).astype(jnp.bfloat16)
    shift_attn = bell_draw(seeds[9], (D,), 0.3, 2.0, ((0, 32),))
    gain_mlp = jnp.clip(1.0 + 0.15 * jax.random.normal(seeds[10], (D,), jnp.float32), 0.25, 1.75).astype(jnp.bfloat16)
    shift_mlp = bell_draw(seeds[11], (D,), 0.3, 2.0, ((0, 32),))
    w_up = bell_draw(seeds[12], (D, FF), D ** -0.5, 0.21875, ((0, 32),))
    bias_up = bell_draw(seeds[13], (FF,), 0.3, 2.0, ((0, 32),))
    w_down = bell_draw(seeds[14], (FF, D), FF ** -0.5, 0.109375, ((0, 32),))
    bias_down = bell_draw(seeds[15], (D,), 0.3, 2.0, ((0, 32),))
    pass_embed = bell_draw(seeds[16], (PASSES, D), 0.5, 3.0, ((1, 32),))
    return {"tokens": tokens, "lengths": lengths, "cotangent": cotangent, "w_qkv": w_qkv, "bias_q": bias_q, "bias_v": bias_v, "w_out": w_out, "bias_out": bias_out, "gain_attn": gain_attn, "shift_attn": shift_attn, "gain_mlp": gain_mlp, "shift_mlp": shift_mlp, "w_up": w_up, "bias_up": bias_up, "w_down": w_down, "bias_down": bias_down, "pass_embed": pass_embed}


HIGHEST = lax.Precision.HIGHEST
EPSILON = 1e-05

@jax.custom_vjp
def low(v):
    return lax.optimization_barrier(v.astype(jnp.bfloat16)).astype(jnp.float32)

@jax.custom_vjp
def low_back(v):
    return v

def low_keep(v):
    return (low(v), None)

def low_pass(kept, grad):
    return (grad,)

def back_keep(v):
    return (v, None)

def back_low(kept, grad):
    return (low(grad),)
low.defvjp(low_keep, low_pass)
low_back.defvjp(back_keep, back_low)

def layer_norm(values, gain_vec, shift_vec):
    average = lax.optimization_barrier(jnp.mean(values, axis=-1, keepdims=True))
    centred = values - average
    spread = lax.optimization_barrier(jnp.mean(centred * centred, axis=-1, keepdims=True))
    return centred * lax.rsqrt(spread + EPSILON) * gain_vec + shift_vec

def attend_row(queries, key_stack, value_stack, doc_ids):
    length = queries.shape[0]
    copies = key_stack.shape[0] // length
    raw_scores = jnp.einsum('thd,shd->hts', queries, key_stack, precision=HIGHEST) * HEAD_DIM ** (-0.5)
    scores = low_back(raw_scores)
    position = jnp.arange(length, dtype=jnp.int32)
    same_doc = (doc_ids[:, None] == doc_ids[None, :]) & (position[None, :] <= position[:, None])
    allowed = jnp.tile(same_doc, (1, copies))
    masked = jnp.where(allowed[None], scores, -1e+30)
    row_top = lax.optimization_barrier(jnp.max(masked, axis=-1, keepdims=True))
    weights = jnp.exp(masked - row_top)
    prob_full = low(weights / lax.optimization_barrier(jnp.sum(weights, axis=-1, keepdims=True)))
    return jnp.einsum('hts,shd->thd', prob_full, value_stack, precision=HIGHEST)

def forward_rows(tokens, params, doc_ids):
    w_qkv, bias_q, bias_v, w_out, bias_out, gain_attn, shift_attn, gain_mlp, shift_mlp, w_up, bias_up, w_down, bias_down, pass_embed = params
    group_rows, length, model_width = tokens.shape
    head_count = model_width // HEAD_DIM
    attend = jax.checkpoint(attend_row)
    residual = tokens
    key_list = []
    value_list = []
    for repeat in range(PASSES):
        entry_state = residual + pass_embed[repeat]
        normed = low(layer_norm(entry_state, gain_attn, shift_attn))
        mixed_qkv = jnp.einsum('gtd,de->gte', normed, w_qkv, precision=HIGHEST)
        queries = low(low_back(mixed_qkv[..., :model_width] + bias_q))
        key_list.append(low(low_back(mixed_qkv[..., model_width:2 * model_width])))
        value_list.append(low(low_back(mixed_qkv[..., 2 * model_width:] + bias_v)))
        key_stack = jnp.concatenate(key_list, axis=1).reshape(group_rows, -1, head_count, HEAD_DIM)
        value_stack = jnp.concatenate(value_list, axis=1).reshape(group_rows, -1, head_count, HEAD_DIM)

        def one_row(row_item):
            return attend(row_item[0], row_item[1], row_item[2], row_item[3])
        attended = lax.map(one_row, (queries.reshape(group_rows, length, head_count, HEAD_DIM), key_stack, value_stack, doc_ids))
        context = low(low_back(attended.reshape(group_rows, length, model_width)))
        branch = low_back(jnp.einsum('gte,ed->gtd', context, w_out, precision=HIGHEST) + bias_out)
        middle = entry_state + branch
        normed_mlp = low(layer_norm(middle, gain_mlp, shift_mlp))
        hidden = low_back(jnp.einsum('gtd,df->gtf', normed_mlp, w_up, precision=HIGHEST) + bias_up)
        active = low(jax.nn.gelu(hidden, approximate=True))
        update = low_back(jnp.einsum('gtf,fd->gtd', active, w_down, precision=HIGHEST) + bias_down)
        residual = middle + update
    return residual

def reference(tokens, lengths, cotangent, w_qkv, bias_q, bias_v, w_out, bias_out, gain_attn, shift_attn, gain_mlp, shift_mlp, w_up, bias_up, w_down, bias_down, pass_embed):
    params = tuple((weight_arg.astype(jnp.float32) for weight_arg in (w_qkv, bias_q, bias_v, w_out, bias_out, gain_attn, shift_attn, gain_mlp, shift_mlp, w_up, bias_up, w_down, bias_down, pass_embed)))
    row_count = lengths.shape[0]
    row_limit = max(1, 4096 // TOK_DEV)
    group_rows = max((divisor for divisor in range(1, min(row_count, row_limit) + 1) if row_count % divisor == 0))
    blocks = row_count // group_rows
    position = jnp.arange(TOK_DEV, dtype=jnp.int32)
    doc_ends = jnp.cumsum(lengths, axis=1).astype(jnp.int32)
    doc_ids = lax.optimization_barrier(jnp.sum((position[None, :, None] >= doc_ends[:, None, :]).astype(jnp.int32), axis=2)).astype(jnp.int32)
    sources = tokens.astype(jnp.float32).reshape(blocks, group_rows, TOK_DEV, D)
    cotangents = cotangent.astype(jnp.float32).reshape(blocks, group_rows, TOK_DEV, D)
    doc_blocks = doc_ids.reshape(blocks, group_rows, TOK_DEV)

    def block_step(totals, block_item):
        block_tokens, block_cotangent, block_docs = block_item

        def forward_block(inputs, weight_set):
            return forward_rows(inputs, weight_set, block_docs)
        result, pull_back = jax.vjp(forward_block, block_tokens, params)
        input_grad, weight_grads = pull_back(block_cotangent)
        totals = tuple((running + fresh for running, fresh in zip(totals, weight_grads)))
        return (totals, (result, input_grad))
    zero_grads = tuple((jnp.zeros_like(weight_arg) for weight_arg in params))
    totals, (results, input_grads) = lax.scan(block_step, zero_grads, (sources, cotangents, doc_blocks))
    output = results.reshape(row_count * TOK_DEV, D).astype(jnp.bfloat16)
    token_grad = input_grads.reshape(row_count * TOK_DEV, D).astype(jnp.bfloat16)
    return (output, token_grad, totals[0], totals[1], totals[2], totals[3], totals[4], totals[5], totals[6], totals[7], totals[8], totals[9], totals[10], totals[11], totals[12], totals[13])
```

```python
import functools

import jax
import jax.numpy as jnp
from jax import lax
from jax.experimental import pallas as pl
from jax.experimental.pallas import tpu as pltpu
from jax.sharding import PartitionSpec as P

HEAD_DIM = 64
PASSES = 3
EPSILON = 1e-05
AXES = ("dp", "fsdp")
F32 = jnp.float32
BF16 = jnp.bfloat16


def pairs(partner):
    return [(i, partner(i)) for i in range(32)]


TO_MATE = pairs(lambda i: i ^ 1)
TO_Z = [pairs(lambda i, k=k: i ^ (8 * k)) for k in range(4)]
TO_NEAR = pairs(lambda i: i ^ (2 if i & 1 else 4))
TO_FAR = pairs(lambda i: i ^ (4 if i & 1 else 2))


def send(x, route):
    return lax.ppermute(x, AXES, route)


def after(x, *earlier):
    earlier = tuple(e for e in earlier if e is not None)
    return lax.optimization_barrier((x, earlier))[0] if earlier else x


def in_core_order(core, mine, other, axis):
    return jnp.where(
        core == 0,
        jnp.concatenate([mine, other], axis=axis),
        jnp.concatenate([other, mine], axis=axis),
    )


def gather_chunks(blocks):
    pieces, crossed, far = [], [], []
    for n, block in enumerate(blocks):
        if n >= 1:
            block = after(block, crossed[n - 1])
        z = [send(block, TO_Z[k]) for k in (1, 2, 3)]
        crossed.append(z)
        stack = jnp.stack([block] + z)
        if n >= 2:
            stack = after(stack, far[n - 2])
        both = jnp.stack([stack, send(stack, TO_NEAR)])
        distant = send(both, TO_FAR)
        far.append(distant)
        pieces.append([both, distant, send(both, TO_MATE), send(distant, TO_MATE)])
    return pieces


def chip_of(place, swapped, far, near, z):
    chip, core = place
    order = core ^ swapped
    near_bit = 2 - order
    far_bit = 1 + order
    return chip ^ (far * far_bit) ^ (near * near_bit) ^ (z * 4)


def run_copies(copies):
    for copy in copies:
        copy.start()
    for copy in copies:
        copy.wait()


def assemble_kernel(widths, place_ref, both, distant, mate_both, mate_distant, *rest):
    outs, sem = rest[:-1], rest[-1]
    place = (place_ref[0], place_ref[1])
    rows = both.shape[2]
    copies = []
    for source, swapped, far in (
        (both, 0, 0),
        (distant, 0, 1),
        (mate_both, 1, 0),
        (mate_distant, 1, 1),
    ):
        half = place[1] ^ swapped
        for near in range(2):
            for z in range(4):
                chip = chip_of(place, swapped, far, near, z)
                first = 0
                for out, width in zip(outs, widths):
                    copies.append(
                        pltpu.make_async_copy(
                            source.at[near, z, :, pl.ds(first, width)],
                            out.at[
                                pl.ds(pl.multiple_of(chip * rows, 16), rows),
                                pl.ds(pl.multiple_of(half * width, 128), width),
                            ],
                            sem,
                        )
                    )
                    first += width
    run_copies(copies)


def assemble(place, pieces, widths):
    rows = pieces[0].shape[2] * 16
    anywhere = pl.BlockSpec(memory_space=pl.ANY)
    return pl.pallas_call(
        functools.partial(assemble_kernel, widths),
        out_shape=[jax.ShapeDtypeStruct((rows, 2 * w), BF16) for w in widths],
        in_specs=[pl.BlockSpec(memory_space=pltpu.SMEM)] + [anywhere] * 4,
        out_specs=[anywhere] * len(widths),
        scratch_shapes=[pltpu.SemaphoreType.DMA(())],
    )(place, *pieces)


def spread_kernel(widths, place_ref, *refs):
    count = len(widths)
    sources, (give, keep), sem = refs[:count], refs[count : count + 2], refs[-1]
    place = (place_ref[0], place_ref[1])
    rows = give.shape[3]
    copies = []
    for target, swapped in ((give, 1), (keep, 0)):
        half = place[1] ^ swapped
        for far in range(2):
            for near in range(2):
                for z in range(4):
                    chip = chip_of(place, swapped, far, near, z)
                    first = 0
                    for source, width in zip(sources, widths):
                        copies.append(
                            pltpu.make_async_copy(
                                source.at[
                                    pl.ds(pl.multiple_of(chip * rows, 16), rows),
                                    pl.ds(pl.multiple_of(half * width, 128), width),
                                ],
                                target.at[far, near, z, :, pl.ds(first, width)],
                                sem,
                            )
                        )
                        first += width
    run_copies(copies)


def spread(place, grads):
    widths = [g.shape[1] // 2 for g in grads]
    rows = grads[0].shape[0] // 16
    anywhere = pl.BlockSpec(memory_space=pl.ANY)
    shape = jax.ShapeDtypeStruct((2, 2, 4, rows, sum(widths)), BF16)
    return pl.pallas_call(
        functools.partial(spread_kernel, widths),
        out_shape=[shape, shape],
        in_specs=[pl.BlockSpec(memory_space=pltpu.SMEM)] + [anywhere] * len(grads),
        out_specs=[anywhere] * 2,
        scratch_shapes=[pltpu.SemaphoreType.DMA(())],
    )(place, *grads)


def add_low(a, b):
    return (a.astype(F32) + b.astype(F32)).astype(BF16)


def scatter_chunk(core, give, keep, earlier):
    got = send(give, TO_MATE)
    give, keep = add_low(keep[1], got[1]), add_low(keep[0], got[0])
    got = send(after(give, earlier.get("near")), TO_FAR)
    give, keep = add_low(keep[1], got[1]), add_low(keep[0], got[0])
    got = send(give, TO_NEAR)
    near = got
    give = [add_low(keep[k], got[k]) for k in (1, 2, 3)]
    total = keep[0].astype(F32) + got[0].astype(F32)
    give = after(give, earlier.get("z"))
    z = [send(give[k - 1], TO_Z[k]) for k in (1, 2, 3)]
    for part in z:
        total = total + part.astype(F32)
    rows = total.shape[0] // 2
    total = total.reshape(2, rows, total.shape[1])
    mine = jnp.where(core == 0, total[0], total[1])
    other = send(jnp.where(core == 0, total[1], total[0]), TO_MATE)
    return (
        jnp.where(core == 0, mine, other),
        jnp.where(core == 0, other, mine),
    ), {"near": near, "z": z}


SMALL = 256


def pack_small(vectors, bias_up, pass_embed):
    rows = vectors[0].shape[0]
    first = jnp.stack(vectors, axis=1)
    second = jnp.concatenate([bias_up.reshape(rows, -1), pass_embed.T], axis=1)
    pad = lambda a: jnp.pad(a, ((0, 0), (0, SMALL // 2 - a.shape[1])))
    return jnp.concatenate([pad(first), pad(second)], axis=1)


def unpack_small(small):
    half = SMALL // 2
    vectors = [small[:, k] for k in range(8)]
    return vectors, small[:, half : half + 4].reshape(-1), small[:, half + 4 : half + 4 + PASSES].T


def is_known_slice():
    return lax.axis_size("dp") == 8 and lax.axis_size("fsdp") == 4


def place_of():
    index = lax.axis_index("dp") * 4 + lax.axis_index("fsdp")
    return jnp.stack([index >> 1, index & 1]).astype(jnp.int32)


def halves(*arrays):
    return [
        jnp.concatenate([a[:, h * (a.shape[1] // 2) : (h + 1) * (a.shape[1] // 2)] for a in arrays], axis=1)
        for h in range(2)
    ]


def gather_all(w_qkv, w_out, small, w_up, w_down):
    if not is_known_slice():
        return [lax.all_gather(a, AXES, axis=0, tiled=True) for a in (w_qkv, w_out, small, w_up, w_down)]
    place = place_of()
    core = place[1]
    blocks = []
    for arrays in ((w_qkv, w_out, small), (w_up,), (w_down,)):
        low, high = halves(*arrays)
        mine = jnp.where(core == 0, low, high)
        other = send(jnp.where(core == 0, high, low), TO_MATE)
        blocks.append(in_core_order(core, mine, other, 0))
    pieces = gather_chunks(blocks)
    full = assemble(place, pieces[0], [a.shape[1] // 2 for a in (w_qkv, w_out, small)])
    full += assemble(place, pieces[1], [w_up.shape[1] // 2])
    full += assemble(place, pieces[2], [w_down.shape[1] // 2])
    return full


def scatter_all(chunks):
    if not is_known_slice():
        return [
            [lax.psum_scatter(g.astype(F32), AXES, scatter_dimension=0, tiled=True) for g in grads]
            for grads in chunks
        ]
    place = place_of()
    core = place[1]
    results, earlier = [], {}
    for grads in chunks:
        give, keep = spread(place, grads)
        (low, high), earlier = scatter_chunk(core, give, keep, earlier)
        first, out = 0, []
        for g in grads:
            width = g.shape[1] // 2
            out.append(jnp.concatenate([low[:, first : first + width], high[:, first : first + width]], axis=1))
            first += width
        results.append(out)
    return results


def layer_norm(values, gain_vec, shift_vec):
    average = jnp.mean(values, axis=-1, keepdims=True)
    centred = values - average
    spread_ = jnp.mean(centred * centred, axis=-1, keepdims=True)
    return centred * lax.rsqrt(spread_ + EPSILON) * gain_vec + shift_vec


def gelu_tanh(values):
    return jax.nn.gelu(values, approximate=True)


def masked_scores(queries, key_stack, allowed):
    length, model_width = queries.shape
    head_count = model_width // HEAD_DIM
    query_heads = queries.reshape(length, head_count, HEAD_DIM)
    key_heads = key_stack.reshape(-1, head_count, HEAD_DIM)
    raw_scores = jnp.einsum(
        "thd,shd->hts", query_heads, key_heads, preferred_element_type=jnp.float32
    ) * HEAD_DIM ** (-0.5)
    return (jnp.where(allowed[None], raw_scores, -1e30), query_heads, key_heads)


def attend_forward(queries, key_stack, value_stack, allowed):
    length, model_width = queries.shape
    head_count = model_width // HEAD_DIM
    masked, query_heads, key_heads = masked_scores(queries, key_stack, allowed)
    row_top = jnp.max(masked, axis=-1, keepdims=True)
    weights = jnp.exp(masked - row_top)
    row_total = jnp.sum(weights, axis=-1, keepdims=True)
    prob_low = (weights / row_total).astype(jnp.bfloat16)
    value_heads = value_stack.reshape(-1, head_count, HEAD_DIM)
    context = jnp.einsum("hts,shd->thd", prob_low, value_heads, preferred_element_type=jnp.float32)
    return (context.reshape(length, model_width).astype(jnp.bfloat16), row_top + jnp.log(row_total))


def attend_backward(queries, key_stack, value_stack, grad_context, log_total, allowed):
    length, model_width = queries.shape
    head_count = model_width // HEAD_DIM
    masked, query_heads, key_heads = masked_scores(queries, key_stack, allowed)
    prob_full = jnp.exp(masked - log_total)
    value_heads = value_stack.reshape(-1, head_count, HEAD_DIM)
    grad_heads = grad_context.reshape(length, head_count, HEAD_DIM)
    grad_probs = jnp.einsum(
        "thd,shd->hts", grad_heads, value_heads, preferred_element_type=jnp.float32
    )
    row_inner = jnp.sum(prob_full * grad_probs, axis=-1, keepdims=True)
    grad_scores = (prob_full * (grad_probs - row_inner)).astype(jnp.bfloat16)
    score_scale = HEAD_DIM ** (-0.5)
    grad_queries = (
        jnp.einsum("hts,shd->thd", grad_scores, key_heads, preferred_element_type=jnp.float32)
        * score_scale
    )
    grad_keys = (
        jnp.einsum("hts,thd->shd", grad_scores, query_heads, preferred_element_type=jnp.float32)
        * score_scale
    )
    grad_values = jnp.einsum(
        "hts,thd->shd",
        prob_full.astype(jnp.bfloat16),
        grad_heads,
        preferred_element_type=jnp.float32,
    )
    return (
        grad_queries.reshape(length, model_width),
        grad_keys.reshape(-1, model_width),
        grad_values.reshape(-1, model_width),
    )


def forward_pass(residual, gathered, repeat, key_list, value_list, allowed_base):
    (
        w_qkv,
        bias_q,
        bias_v,
        w_out,
        bias_out,
        gain_attn,
        shift_attn,
        gain_mlp,
        shift_mlp,
        w_up,
        bias_up,
        w_down,
        bias_down,
        pass_embed,
    ) = gathered
    model_width = residual.shape[1]
    entry_state = residual + pass_embed[repeat].astype(jnp.float32)
    normed = layer_norm(
        entry_state, gain_attn.astype(jnp.float32), shift_attn.astype(jnp.float32)
    ).astype(jnp.bfloat16)
    qkv_bias = jnp.concatenate(
        [
            bias_q.astype(jnp.float32),
            jnp.zeros((model_width,), jnp.float32),
            bias_v.astype(jnp.float32),
        ]
    )
    mixed_qkv = (jnp.dot(normed, w_qkv, preferred_element_type=jnp.float32) + qkv_bias).astype(
        jnp.bfloat16
    )
    queries = mixed_qkv[:, :model_width]
    key_list.append(mixed_qkv[:, model_width : 2 * model_width])
    value_list.append(mixed_qkv[:, 2 * model_width :])
    allowed = jnp.tile(allowed_base, (1, repeat + 1))
    context, log_total = attend_forward(
        queries, jnp.concatenate(key_list, axis=0), jnp.concatenate(value_list, axis=0), allowed
    )
    middle = entry_state + (
        jnp.dot(context, w_out, preferred_element_type=jnp.float32) + bias_out.astype(jnp.float32)
    )
    normed_mlp = layer_norm(
        middle, gain_mlp.astype(jnp.float32), shift_mlp.astype(jnp.float32)
    ).astype(jnp.bfloat16)
    hidden = jnp.dot(normed_mlp, w_up, preferred_element_type=jnp.float32) + bias_up.astype(
        jnp.float32
    )
    active = gelu_tanh(hidden).astype(jnp.bfloat16)
    residual = middle + (
        jnp.dot(active, w_down, preferred_element_type=jnp.float32) + bias_down.astype(jnp.float32)
    )
    return (residual, (entry_state, queries, context, log_total, middle, hidden))


def backward_pass(
    grad_state,
    gathered,
    repeat,
    saved_pass,
    key_list,
    value_list,
    key_grads,
    value_grads,
    allowed_base,
):
    (
        w_qkv,
        bias_q,
        bias_v,
        w_out,
        bias_out,
        gain_attn,
        shift_attn,
        gain_mlp,
        shift_mlp,
        w_up,
        bias_up,
        w_down,
        bias_down,
        pass_embed,
    ) = gathered
    entry_state, queries, context, log_total, middle, hidden = saved_pass
    length, model_width = queries.shape
    update_grad = grad_state.astype(jnp.bfloat16)
    active, gelu_pull = jax.vjp(gelu_tanh, hidden)
    grad_w_down = jnp.einsum(
        "tf,td->fd", active.astype(jnp.bfloat16), update_grad, preferred_element_type=jnp.float32
    )
    grad_bias_down = jnp.sum(update_grad.astype(jnp.float32), axis=0)
    (grad_hidden,) = gelu_pull(
        jnp.einsum("td,fd->tf", update_grad, w_down, preferred_element_type=jnp.float32)
    )
    grad_hidden = grad_hidden.astype(jnp.bfloat16)
    normed_mlp, mlp_pull = jax.vjp(
        layer_norm, middle, gain_mlp.astype(jnp.float32), shift_mlp.astype(jnp.float32)
    )
    grad_w_up = jnp.einsum(
        "td,tf->df",
        normed_mlp.astype(jnp.bfloat16),
        grad_hidden,
        preferred_element_type=jnp.float32,
    )
    grad_bias_up = jnp.sum(grad_hidden.astype(jnp.float32), axis=0)
    grad_middle, grad_gain_mlp, grad_shift_mlp = mlp_pull(
        jnp.einsum("tf,df->td", grad_hidden, w_up, preferred_element_type=jnp.float32)
    )
    grad_middle = grad_state + grad_middle
    branch_grad = grad_middle.astype(jnp.bfloat16)
    grad_w_out = jnp.einsum("te,td->ed", context, branch_grad, preferred_element_type=jnp.float32)
    grad_bias_out = jnp.sum(branch_grad.astype(jnp.float32), axis=0)
    grad_context = jnp.einsum(
        "td,ed->te", branch_grad, w_out, preferred_element_type=jnp.float32
    ).astype(jnp.bfloat16)
    allowed = jnp.tile(allowed_base, (1, repeat + 1))
    grad_queries, grad_keys, grad_values = attend_backward(
        queries,
        jnp.concatenate(key_list[: repeat + 1], axis=0),
        jnp.concatenate(value_list[: repeat + 1], axis=0),
        grad_context,
        log_total,
        allowed,
    )
    for earlier in range(repeat + 1):
        key_grads[earlier] = (
            key_grads[earlier] + grad_keys[earlier * length : (earlier + 1) * length]
        )
        value_grads[earlier] = (
            value_grads[earlier] + grad_values[earlier * length : (earlier + 1) * length]
        )
    grad_mixed = jnp.concatenate(
        [grad_queries, key_grads[repeat], value_grads[repeat]], axis=1
    ).astype(jnp.bfloat16)
    grad_bias_q = jnp.sum(grad_mixed[:, :model_width].astype(jnp.float32), axis=0)
    grad_bias_v = jnp.sum(grad_mixed[:, 2 * model_width :].astype(jnp.float32), axis=0)
    normed, attn_pull = jax.vjp(
        layer_norm, entry_state, gain_attn.astype(jnp.float32), shift_attn.astype(jnp.float32)
    )
    grad_w_qkv = jnp.einsum(
        "td,te->de", normed.astype(jnp.bfloat16), grad_mixed, preferred_element_type=jnp.float32
    )
    grad_entry, grad_gain_attn, grad_shift_attn = attn_pull(
        jnp.einsum("te,de->td", grad_mixed, w_qkv, preferred_element_type=jnp.float32)
    )
    grad_entry = grad_middle + grad_entry
    grad_embed = (
        jnp.zeros((PASSES, model_width), jnp.float32).at[repeat].set(jnp.sum(grad_entry, axis=0))
    )
    return (
        grad_entry,
        (
            grad_w_qkv,
            grad_bias_q,
            grad_bias_v,
            grad_w_out,
            grad_bias_out,
            grad_gain_attn,
            grad_shift_attn,
            grad_gain_mlp,
            grad_shift_mlp,
            grad_w_up,
            grad_bias_up,
            grad_w_down,
            grad_bias_down,
            grad_embed,
        ),
    )


def per_device(
    tokens,
    lengths,
    cotangent,
    w_qkv,
    bias_q,
    bias_v,
    w_out,
    bias_out,
    gain_attn,
    shift_attn,
    gain_mlp,
    shift_mlp,
    w_up,
    bias_up,
    w_down,
    bias_down,
    pass_embed,
):
    length, model_width = tokens.shape
    position = jnp.arange(length, dtype=jnp.int32)
    docs = lengths.shape[1]
    upto = jnp.arange(docs)[:, None] <= jnp.arange(docs)[None, :]
    doc_ends = jnp.sum(jnp.where(upto, lengths[0][:, None], 0), axis=0)
    doc_ids = jnp.sum((position[:, None] >= doc_ends[None, :]).astype(jnp.int32), axis=1)
    allowed_base = (doc_ids[:, None] == doc_ids[None, :]) & (position[None, :] <= position[:, None])
    small = pack_small(
        [bias_q, bias_v, bias_out, gain_attn, shift_attn, gain_mlp, shift_mlp, bias_down], bias_up, pass_embed
    )
    w_qkv, w_out, small, w_up, w_down = gather_all(w_qkv, w_out, small, w_up, w_down)
    (bias_q, bias_v, bias_out, gain_attn, shift_attn, gain_mlp, shift_mlp, bias_down), bias_up, pass_embed = unpack_small(
        small
    )
    gathered = (
        w_qkv,
        bias_q,
        bias_v,
        w_out,
        bias_out,
        gain_attn,
        shift_attn,
        gain_mlp,
        shift_mlp,
        w_up,
        bias_up,
        w_down,
        bias_down,
        pass_embed,
    )
    residual = tokens.astype(jnp.float32)
    key_list = []
    value_list = []
    saved_list = []
    for repeat in range(PASSES):
        residual, saved_pass = forward_pass(
            residual, gathered, repeat, key_list, value_list, allowed_base
        )
        saved_list.append(saved_pass)
    output = residual.astype(jnp.bfloat16)
    grad_state = cotangent.astype(jnp.float32)
    key_grads = [jnp.zeros((length, model_width), jnp.float32) for repeat in range(PASSES)]
    value_grads = [jnp.zeros((length, model_width), jnp.float32) for repeat in range(PASSES)]
    totals = None
    for repeat in reversed(range(PASSES)):
        grad_state, pass_grads = backward_pass(
            grad_state,
            gathered,
            repeat,
            saved_list[repeat],
            key_list,
            value_list,
            key_grads,
            value_grads,
            allowed_base,
        )
        totals = (
            pass_grads
            if totals is None
            else tuple((running + extra for running, extra in zip(totals, pass_grads)))
        )
    (g_qkv, g_bq, g_bv, g_out, g_bo, g_ga, g_sa, g_gm, g_sm, g_up, g_bu, g_down, g_bd, g_pe) = totals
    g_small = pack_small([g_bq, g_bv, g_bo, g_ga, g_sa, g_gm, g_sm, g_bd], g_bu, g_pe)
    (g_down,), (g_up,), (g_qkv, g_out, g_small) = scatter_all(
        [[g_down.astype(BF16)], [g_up.astype(BF16)], [g_qkv.astype(BF16), g_out.astype(BF16), g_small.astype(BF16)]]
    )
    (g_bq, g_bv, g_bo, g_ga, g_sa, g_gm, g_sm, g_bd), g_bu, g_pe = unpack_small(g_small)
    return (
        output,
        grad_state.astype(jnp.bfloat16),
        g_qkv,
        g_bq,
        g_bv,
        g_out,
        g_bo,
        g_ga,
        g_sa,
        g_gm,
        g_sm,
        g_up,
        g_bu,
        g_down,
        g_bd,
        g_pe,
    )


def solution(mesh):
    placed = (
        P(("dp", "fsdp"), None),
        P(("dp", "fsdp"), None),
        P(("dp", "fsdp"), None),
        P(("dp", "fsdp"), None),
        P(("dp", "fsdp")),
        P(("dp", "fsdp")),
        P(("dp", "fsdp"), None),
        P(("dp", "fsdp")),
        P(("dp", "fsdp")),
        P(("dp", "fsdp")),
        P(("dp", "fsdp")),
        P(("dp", "fsdp")),
        P(("dp", "fsdp"), None),
        P(("dp", "fsdp")),
        P(("dp", "fsdp"), None),
        P(("dp", "fsdp")),
        P(None, ("dp", "fsdp")),
    )
    return jax.shard_map(
        per_device,
        mesh=mesh,
        in_specs=placed,
        out_specs=(
            P(("dp", "fsdp"), None),
            P(("dp", "fsdp"), None),
            P(("dp", "fsdp"), None),
            P(("dp", "fsdp")),
            P(("dp", "fsdp")),
            P(("dp", "fsdp"), None),
            P(("dp", "fsdp")),
            P(("dp", "fsdp")),
            P(("dp", "fsdp")),
            P(("dp", "fsdp")),
            P(("dp", "fsdp")),
            P(("dp", "fsdp"), None),
            P(("dp", "fsdp")),
            P(("dp", "fsdp"), None),
            P(("dp", "fsdp")),
            P(None, ("dp", "fsdp")),
        ),
        check_vma=False,
    )
```

```python
import functools

import jax
import jax.numpy as jnp
from jax import lax
from jax.experimental import pallas as pl
from jax.experimental.pallas import tpu as pltpu
from jax.sharding import PartitionSpec as P

HEAD_DIM = 64
PASSES = 3
EPSILON = 1e-05
AXES = ("dp", "fsdp")
F32 = jnp.float32
BF16 = jnp.bfloat16


def pairs(partner):
    return [(i, partner(i)) for i in range(32)]


TO_MATE = pairs(lambda i: i ^ 1)
TO_Z = [pairs(lambda i, k=k: i ^ (8 * k)) for k in range(4)]
TO_NEAR = pairs(lambda i: i ^ (2 if i & 1 else 4))
TO_FAR = pairs(lambda i: i ^ (4 if i & 1 else 2))


def send(x, route):
    return lax.ppermute(x, AXES, route)


def after(x, *earlier):
    earlier = tuple(e for e in earlier if e is not None)
    return lax.optimization_barrier((x, earlier))[0] if earlier else x


def in_core_order(core, mine, other, axis):
    return jnp.where(
        core == 0,
        jnp.concatenate([mine, other], axis=axis),
        jnp.concatenate([other, mine], axis=axis),
    )


def gather_chunks(blocks):
    pieces, crossed, far = [], [], []
    for n, block in enumerate(blocks):
        if n >= 1:
            block = after(block, crossed[n - 1])
        z = [send(block, TO_Z[k]) for k in (1, 2, 3)]
        crossed.append(z)
        stack = jnp.stack([block] + z)
        if n >= 2:
            stack = after(stack, far[n - 2])
        both = jnp.stack([stack, send(stack, TO_NEAR)])
        distant = send(both, TO_FAR)
        far.append(distant)
        pieces.append([both, distant, send(both, TO_MATE), send(distant, TO_MATE)])
    return pieces


def chip_of(place, swapped, far, near, z):
    chip, core = place
    order = core ^ swapped
    near_bit = 2 - order
    far_bit = 1 + order
    return chip ^ (far * far_bit) ^ (near * near_bit) ^ (z * 4)


def run_copies(copies):
    for copy in copies:
        copy.start()
    for copy in copies:
        copy.wait()


def assemble_kernel(widths, place_ref, both, distant, mate_both, mate_distant, *rest):
    outs, sem = rest[:-1], rest[-1]
    place = (place_ref[0], place_ref[1])
    rows = both.shape[2]
    copies = []
    for source, swapped, far in (
        (both, 0, 0),
        (distant, 0, 1),
        (mate_both, 1, 0),
        (mate_distant, 1, 1),
    ):
        half = place[1] ^ swapped
        for near in range(2):
            for z in range(4):
                chip = chip_of(place, swapped, far, near, z)
                first = 0
                for out, width in zip(outs, widths):
                    copies.append(
                        pltpu.make_async_copy(
                            source.at[near, z, :, pl.ds(first, width)],
                            out.at[
                                pl.ds(pl.multiple_of(chip * rows, 16), rows),
                                pl.ds(pl.multiple_of(half * width, 128), width),
                            ],
                            sem,
                        )
                    )
                    first += width
    run_copies(copies)


def assemble(place, pieces, widths):
    rows = pieces[0].shape[2] * 16
    anywhere = pl.BlockSpec(memory_space=pl.ANY)
    return pl.pallas_call(
        functools.partial(assemble_kernel, widths),
        out_shape=[jax.ShapeDtypeStruct((rows, 2 * w), BF16) for w in widths],
        in_specs=[pl.BlockSpec(memory_space=pltpu.SMEM)] + [anywhere] * 4,
        out_specs=[pl.BlockSpec(memory_space=pltpu.VMEM)] * len(widths),
        scratch_shapes=[pltpu.SemaphoreType.DMA(())],
    )(place, *pieces)


def spread_kernel(widths, place_ref, *refs):
    count = len(widths)
    sources, (give, keep), sem = refs[:count], refs[count : count + 2], refs[-1]
    place = (place_ref[0], place_ref[1])
    rows = give.shape[3]
    copies = []
    for target, swapped in ((give, 1), (keep, 0)):
        half = place[1] ^ swapped
        for far in range(2):
            for near in range(2):
                for z in range(4):
                    chip = chip_of(place, swapped, far, near, z)
                    first = 0
                    for source, width in zip(sources, widths):
                        copies.append(
                            pltpu.make_async_copy(
                                source.at[
                                    pl.ds(pl.multiple_of(chip * rows, 16), rows),
                                    pl.ds(pl.multiple_of(half * width, 128), width),
                                ],
                                target.at[far, near, z, :, pl.ds(first, width)],
                                sem,
                            )
                        )
                        first += width
    run_copies(copies)


def spread(place, grads):
    widths = [g.shape[1] // 2 for g in grads]
    rows = grads[0].shape[0] // 16
    anywhere = pl.BlockSpec(memory_space=pl.ANY)
    shape = jax.ShapeDtypeStruct((2, 2, 4, rows, sum(widths)), BF16)
    return pl.pallas_call(
        functools.partial(spread_kernel, widths),
        out_shape=[shape, shape],
        in_specs=[pl.BlockSpec(memory_space=pltpu.SMEM)] + [pl.BlockSpec(memory_space=pltpu.VMEM)] * len(grads),
        out_specs=[anywhere] * 2,
        scratch_shapes=[pltpu.SemaphoreType.DMA(())],
    )(place, *grads)


def add_low(a, b):
    return (a.astype(F32) + b.astype(F32)).astype(BF16)


def scatter_chunk(core, give, keep, earlier):
    got = send(give, TO_MATE)
    give, keep = add_low(keep[1], got[1]), add_low(keep[0], got[0])
    got = send(after(give, earlier.get("near")), TO_FAR)
    give, keep = add_low(keep[1], got[1]), add_low(keep[0], got[0])
    got = send(give, TO_NEAR)
    near = got
    give = [add_low(keep[k], got[k]) for k in (1, 2, 3)]
    total = keep[0].astype(F32) + got[0].astype(F32)
    give = after(give, earlier.get("z"))
    z = [send(give[k - 1], TO_Z[k]) for k in (1, 2, 3)]
    for part in z:
        total = total + part.astype(F32)
    rows = total.shape[0] // 2
    total = total.reshape(2, rows, total.shape[1])
    mine = jnp.where(core == 0, total[0], total[1])
    other = send(jnp.where(core == 0, total[1], total[0]), TO_MATE)
    return (
        jnp.where(core == 0, mine, other),
        jnp.where(core == 0, other, mine),
    ), {"near": near, "z": z}


SMALL = 256


def pack_small(vectors, bias_up, pass_embed):
    rows = vectors[0].shape[0]
    first = jnp.stack(vectors, axis=1)
    second = jnp.concatenate([bias_up.reshape(rows, -1), pass_embed.T], axis=1)
    pad = lambda a: jnp.pad(a, ((0, 0), (0, SMALL // 2 - a.shape[1])))
    return jnp.concatenate([pad(first), pad(second)], axis=1)


def unpack_small(small):
    half = SMALL // 2
    vectors = [small[:, k] for k in range(8)]
    return vectors, small[:, half : half + 4].reshape(-1), small[:, half + 4 : half + 4 + PASSES].T


def is_known_slice():
    return lax.axis_size("dp") == 8 and lax.axis_size("fsdp") == 4


def place_of():
    index = lax.axis_index("dp") * 4 + lax.axis_index("fsdp")
    return jnp.stack([index >> 1, index & 1]).astype(jnp.int32)


def halves(*arrays):
    return [
        jnp.concatenate([a[:, h * (a.shape[1] // 2) : (h + 1) * (a.shape[1] // 2)] for a in arrays], axis=1)
        for h in range(2)
    ]


def gather_all(w_qkv, w_out, small, w_up, w_down):
    if not is_known_slice():
        return [lax.all_gather(a, AXES, axis=0, tiled=True) for a in (w_qkv, w_out, small, w_up, w_down)]
    place = place_of()
    core = place[1]
    blocks = []
    for arrays in ((w_qkv, w_out, small), (w_up,), (w_down,)):
        low, high = halves(*arrays)
        mine = jnp.where(core == 0, low, high)
        other = send(jnp.where(core == 0, high, low), TO_MATE)
        blocks.append(in_core_order(core, mine, other, 0))
    pieces = gather_chunks(blocks)
    full = assemble(place, pieces[0], [a.shape[1] // 2 for a in (w_qkv, w_out, small)])
    full += assemble(place, pieces[1], [w_up.shape[1] // 2])
    full += assemble(place, pieces[2], [w_down.shape[1] // 2])
    return full


def scatter_all(chunks):
    if not is_known_slice():
        return [
            [lax.psum_scatter(g.astype(F32), AXES, scatter_dimension=0, tiled=True) for g in grads]
            for grads in chunks
        ]
    place = place_of()
    core = place[1]
    results, earlier = [], {}
    for grads in chunks:
        give, keep = spread(place, grads)
        (low, high), earlier = scatter_chunk(core, give, keep, earlier)
        first, out = 0, []
        for g in grads:
            width = g.shape[1] // 2
            out.append(jnp.concatenate([low[:, first : first + width], high[:, first : first + width]], axis=1))
            first += width
        results.append(out)
    return results


def layer_norm(values, gain_vec, shift_vec):
    average = jnp.mean(values, axis=-1, keepdims=True)
    centred = values - average
    spread_ = jnp.mean(centred * centred, axis=-1, keepdims=True)
    return centred * lax.rsqrt(spread_ + EPSILON) * gain_vec + shift_vec


def gelu_tanh(values):
    return jax.nn.gelu(values, approximate=True)


def masked_scores(queries, key_stack, allowed):
    length, model_width = queries.shape
    head_count = model_width // HEAD_DIM
    query_heads = queries.reshape(length, head_count, HEAD_DIM)
    key_heads = key_stack.reshape(-1, head_count, HEAD_DIM)
    raw_scores = jnp.einsum(
        "thd,shd->hts", query_heads, key_heads, preferred_element_type=jnp.float32
    ) * HEAD_DIM ** (-0.5)
    return (jnp.where(allowed[None], raw_scores, -1e30), query_heads, key_heads)


def attend_forward(queries, key_stack, value_stack, allowed):
    length, model_width = queries.shape
    head_count = model_width // HEAD_DIM
    masked, query_heads, key_heads = masked_scores(queries, key_stack, allowed)
    row_top = jnp.max(masked, axis=-1, keepdims=True)
    weights = jnp.exp(masked - row_top)
    row_total = jnp.sum(weights, axis=-1, keepdims=True)
    prob_low = (weights / row_total).astype(jnp.bfloat16)
    value_heads = value_stack.reshape(-1, head_count, HEAD_DIM)
    context = jnp.einsum("hts,shd->thd", prob_low, value_heads, preferred_element_type=jnp.float32)
    return (context.reshape(length, model_width).astype(jnp.bfloat16), row_top + jnp.log(row_total))


def attend_backward(queries, key_stack, value_stack, grad_context, log_total, allowed):
    length, model_width = queries.shape
    head_count = model_width // HEAD_DIM
    masked, query_heads, key_heads = masked_scores(queries, key_stack, allowed)
    prob_full = jnp.exp(masked - log_total)
    value_heads = value_stack.reshape(-1, head_count, HEAD_DIM)
    grad_heads = grad_context.reshape(length, head_count, HEAD_DIM)
    grad_probs = jnp.einsum(
        "thd,shd->hts", grad_heads, value_heads, preferred_element_type=jnp.float32
    )
    row_inner = jnp.sum(prob_full * grad_probs, axis=-1, keepdims=True)
    grad_scores = (prob_full * (grad_probs - row_inner)).astype(jnp.bfloat16)
    score_scale = HEAD_DIM ** (-0.5)
    grad_queries = (
        jnp.einsum("hts,shd->thd", grad_scores, key_heads, preferred_element_type=jnp.float32)
        * score_scale
    )
    grad_keys = (
        jnp.einsum("hts,thd->shd", grad_scores, query_heads, preferred_element_type=jnp.float32)
        * score_scale
    )
    grad_values = jnp.einsum(
        "hts,thd->shd",
        prob_full.astype(jnp.bfloat16),
        grad_heads,
        preferred_element_type=jnp.float32,
    )
    return (
        grad_queries.reshape(length, model_width),
        grad_keys.reshape(-1, model_width),
        grad_values.reshape(-1, model_width),
    )


def forward_pass(residual, gathered, repeat, key_list, value_list, allowed_base):
    (
        w_qkv,
        bias_q,
        bias_v,
        w_out,
        bias_out,
        gain_attn,
        shift_attn,
        gain_mlp,
        shift_mlp,
        w_up,
        bias_up,
        w_down,
        bias_down,
        pass_embed,
    ) = gathered
    model_width = residual.shape[1]
    entry_state = residual + pass_embed[repeat].astype(jnp.float32)
    normed = layer_norm(
        entry_state, gain_attn.astype(jnp.float32), shift_attn.astype(jnp.float32)
    ).astype(jnp.bfloat16)
    qkv_bias = jnp.concatenate(
        [
            bias_q.astype(jnp.float32),
            jnp.zeros((model_width,), jnp.float32),
            bias_v.astype(jnp.float32),
        ]
    )
    mixed_qkv = (jnp.dot(normed, w_qkv, preferred_element_type=jnp.float32) + qkv_bias).astype(
        jnp.bfloat16
    )
    queries = mixed_qkv[:, :model_width]
    key_list.append(mixed_qkv[:, model_width : 2 * model_width])
    value_list.append(mixed_qkv[:, 2 * model_width :])
    allowed = jnp.tile(allowed_base, (1, repeat + 1))
    context, log_total = attend_forward(
        queries, jnp.concatenate(key_list, axis=0), jnp.concatenate(value_list, axis=0), allowed
    )
    middle = entry_state + (
        jnp.dot(context, w_out, preferred_element_type=jnp.float32) + bias_out.astype(jnp.float32)
    )
    normed_mlp = layer_norm(
        middle, gain_mlp.astype(jnp.float32), shift_mlp.astype(jnp.float32)
    ).astype(jnp.bfloat16)
    hidden = jnp.dot(normed_mlp, w_up, preferred_element_type=jnp.float32) + bias_up.astype(
        jnp.float32
    )
    active = gelu_tanh(hidden).astype(jnp.bfloat16)
    residual = middle + (
        jnp.dot(active, w_down, preferred_element_type=jnp.float32) + bias_down.astype(jnp.float32)
    )
    return (residual, (entry_state, queries, context, log_total, middle, hidden))


def backward_pass(
    grad_state,
    gathered,
    repeat,
    saved_pass,
    key_list,
    value_list,
    key_grads,
    value_grads,
    allowed_base,
):
    (
        w_qkv,
        bias_q,
        bias_v,
        w_out,
        bias_out,
        gain_attn,
        shift_attn,
        gain_mlp,
        shift_mlp,
        w_up,
        bias_up,
        w_down,
        bias_down,
        pass_embed,
    ) = gathered
    entry_state, queries, context, log_total, middle, hidden = saved_pass
    length, model_width = queries.shape
    update_grad = grad_state.astype(jnp.bfloat16)
    active, gelu_pull = jax.vjp(gelu_tanh, hidden)
    grad_w_down = jnp.einsum(
        "tf,td->fd", active.astype(jnp.bfloat16), update_grad, preferred_element_type=jnp.float32
    )
    grad_bias_down = jnp.sum(update_grad.astype(jnp.float32), axis=0)
    (grad_hidden,) = gelu_pull(
        jnp.einsum("td,fd->tf", update_grad, w_down, preferred_element_type=jnp.float32)
    )
    grad_hidden = grad_hidden.astype(jnp.bfloat16)
    normed_mlp, mlp_pull = jax.vjp(
        layer_norm, middle, gain_mlp.astype(jnp.float32), shift_mlp.astype(jnp.float32)
    )
    grad_w_up = jnp.einsum(
        "td,tf->df",
        normed_mlp.astype(jnp.bfloat16),
        grad_hidden,
        preferred_element_type=jnp.float32,
    )
    grad_bias_up = jnp.sum(grad_hidden.astype(jnp.float32), axis=0)
    grad_middle, grad_gain_mlp, grad_shift_mlp = mlp_pull(
        jnp.einsum("tf,df->td", grad_hidden, w_up, preferred_element_type=jnp.float32)
    )
    grad_middle = grad_state + grad_middle
    branch_grad = grad_middle.astype(jnp.bfloat16)
    grad_w_out = jnp.einsum("te,td->ed", context, branch_grad, preferred_element_type=jnp.float32)
    grad_bias_out = jnp.sum(branch_grad.astype(jnp.float32), axis=0)
    grad_context = jnp.einsum(
        "td,ed->te", branch_grad, w_out, preferred_element_type=jnp.float32
    ).astype(jnp.bfloat16)
    allowed = jnp.tile(allowed_base, (1, repeat + 1))
    grad_queries, grad_keys, grad_values = attend_backward(
        queries,
        jnp.concatenate(key_list[: repeat + 1], axis=0),
        jnp.concatenate(value_list[: repeat + 1], axis=0),
        grad_context,
        log_total,
        allowed,
    )
    for earlier in range(repeat + 1):
        key_grads[earlier] = (
            key_grads[earlier] + grad_keys[earlier * length : (earlier + 1) * length]
        )
        value_grads[earlier] = (
            value_grads[earlier] + grad_values[earlier * length : (earlier + 1) * length]
        )
    grad_mixed = jnp.concatenate(
        [grad_queries, key_grads[repeat], value_grads[repeat]], axis=1
    ).astype(jnp.bfloat16)
    grad_bias_q = jnp.sum(grad_mixed[:, :model_width].astype(jnp.float32), axis=0)
    grad_bias_v = jnp.sum(grad_mixed[:, 2 * model_width :].astype(jnp.float32), axis=0)
    normed, attn_pull = jax.vjp(
        layer_norm, entry_state, gain_attn.astype(jnp.float32), shift_attn.astype(jnp.float32)
    )
    grad_w_qkv = jnp.einsum(
        "td,te->de", normed.astype(jnp.bfloat16), grad_mixed, preferred_element_type=jnp.float32
    )
    grad_entry, grad_gain_attn, grad_shift_attn = attn_pull(
        jnp.einsum("te,de->td", grad_mixed, w_qkv, preferred_element_type=jnp.float32)
    )
    grad_entry = grad_middle + grad_entry
    grad_embed = (
        jnp.zeros((PASSES, model_width), jnp.float32).at[repeat].set(jnp.sum(grad_entry, axis=0))
    )
    return (
        grad_entry,
        (
            grad_w_qkv,
            grad_bias_q,
            grad_bias_v,
            grad_w_out,
            grad_bias_out,
            grad_gain_attn,
            grad_shift_attn,
            grad_gain_mlp,
            grad_shift_mlp,
            grad_w_up,
            grad_bias_up,
            grad_w_down,
            grad_bias_down,
            grad_embed,
        ),
    )


def per_device(
    tokens,
    lengths,
    cotangent,
    w_qkv,
    bias_q,
    bias_v,
    w_out,
    bias_out,
    gain_attn,
    shift_attn,
    gain_mlp,
    shift_mlp,
    w_up,
    bias_up,
    w_down,
    bias_down,
    pass_embed,
):
    length, model_width = tokens.shape
    position = jnp.arange(length, dtype=jnp.int32)
    docs = lengths.shape[1]
    upto = jnp.arange(docs)[:, None] <= jnp.arange(docs)[None, :]
    doc_ends = jnp.sum(jnp.where(upto, lengths[0][:, None], 0), axis=0)
    doc_ids = jnp.sum((position[:, None] >= doc_ends[None, :]).astype(jnp.int32), axis=1)
    allowed_base = (doc_ids[:, None] == doc_ids[None, :]) & (position[None, :] <= position[:, None])
    small = pack_small(
        [bias_q, bias_v, bias_out, gain_attn, shift_attn, gain_mlp, shift_mlp, bias_down], bias_up, pass_embed
    )
    w_qkv, w_out, small, w_up, w_down = gather_all(w_qkv, w_out, small, w_up, w_down)
    (bias_q, bias_v, bias_out, gain_attn, shift_attn, gain_mlp, shift_mlp, bias_down), bias_up, pass_embed = unpack_small(
        small
    )
    gathered = (
        w_qkv,
        bias_q,
        bias_v,
        w_out,
        bias_out,
        gain_attn,
        shift_attn,
        gain_mlp,
        shift_mlp,
        w_up,
        bias_up,
        w_down,
        bias_down,
        pass_embed,
    )
    residual = tokens.astype(jnp.float32)
    key_list = []
    value_list = []
    saved_list = []
    for repeat in range(PASSES):
        residual, saved_pass = forward_pass(
            residual, gathered, repeat, key_list, value_list, allowed_base
        )
        saved_list.append(saved_pass)
    output = residual.astype(jnp.bfloat16)
    grad_state = cotangent.astype(jnp.float32)
    key_grads = [jnp.zeros((length, model_width), jnp.float32) for repeat in range(PASSES)]
    value_grads = [jnp.zeros((length, model_width), jnp.float32) for repeat in range(PASSES)]
    totals = None
    for repeat in reversed(range(PASSES)):
        grad_state, pass_grads = backward_pass(
            grad_state,
            gathered,
            repeat,
            saved_list[repeat],
            key_list,
            value_list,
            key_grads,
            value_grads,
            allowed_base,
        )
        totals = (
            pass_grads
            if totals is None
            else tuple((running + extra for running, extra in zip(totals, pass_grads)))
        )
    (g_qkv, g_bq, g_bv, g_out, g_bo, g_ga, g_sa, g_gm, g_sm, g_up, g_bu, g_down, g_bd, g_pe) = totals
    g_small = pack_small([g_bq, g_bv, g_bo, g_ga, g_sa, g_gm, g_sm, g_bd], g_bu, g_pe)
    (g_down,), (g_up,), (g_qkv, g_out, g_small) = scatter_all(
        [[g_down.astype(BF16)], [g_up.astype(BF16)], [g_qkv.astype(BF16), g_out.astype(BF16), g_small.astype(BF16)]]
    )
    (g_bq, g_bv, g_bo, g_ga, g_sa, g_gm, g_sm, g_bd), g_bu, g_pe = unpack_small(g_small)
    return (
        output,
        grad_state.astype(jnp.bfloat16),
        g_qkv,
        g_bq,
        g_bv,
        g_out,
        g_bo,
        g_ga,
        g_sa,
        g_gm,
        g_sm,
        g_up,
        g_bu,
        g_down,
        g_bd,
        g_pe,
    )


def solution(mesh):
    placed = (
        P(("dp", "fsdp"), None),
        P(("dp", "fsdp"), None),
        P(("dp", "fsdp"), None),
        P(("dp", "fsdp"), None),
        P(("dp", "fsdp")),
        P(("dp", "fsdp")),
        P(("dp", "fsdp"), None),
        P(("dp", "fsdp")),
        P(("dp", "fsdp")),
        P(("dp", "fsdp")),
        P(("dp", "fsdp")),
        P(("dp", "fsdp")),
        P(("dp", "fsdp"), None),
        P(("dp", "fsdp")),
        P(("dp", "fsdp"), None),
        P(("dp", "fsdp")),
        P(None, ("dp", "fsdp")),
    )
    return jax.shard_map(
        per_device,
        mesh=mesh,
        in_specs=placed,
        out_specs=(
            P(("dp", "fsdp"), None),
            P(("dp", "fsdp"), None),
            P(("dp", "fsdp"), None),
            P(("dp", "fsdp")),
            P(("dp", "fsdp")),
            P(("dp", "fsdp"), None),
            P(("dp", "fsdp")),
            P(("dp", "fsdp")),
            P(("dp", "fsdp")),
            P(("dp", "fsdp")),
            P(("dp", "fsdp")),
            P(("dp", "fsdp"), None),
            P(("dp", "fsdp")),
            P(("dp", "fsdp"), None),
            P(("dp", "fsdp")),
            P(None, ("dp", "fsdp")),
        ),
        check_vma=False,
    )
```

```python
import functools

import jax
import jax.numpy as jnp
from jax import lax
from jax.experimental import pallas as pl
from jax.experimental.pallas import tpu as pltpu
from jax.sharding import PartitionSpec as P

HEAD_DIM = 64
PASSES = 3
EPSILON = 1e-05
AXES = ("dp", "fsdp")
F32 = jnp.float32
BF16 = jnp.bfloat16


def pairs(partner):
    return [(i, partner(i)) for i in range(32)]


TO_MATE = pairs(lambda i: i ^ 1)
TO_Z = [pairs(lambda i, k=k: i ^ (8 * k)) for k in range(4)]
TO_NEAR = pairs(lambda i: i ^ (2 if i & 1 else 4))
TO_FAR = pairs(lambda i: i ^ (4 if i & 1 else 2))


def send(x, route):
    return lax.ppermute(x, AXES, route)


def after(x, *earlier):
    earlier = tuple(e for e in earlier if e is not None)
    return lax.optimization_barrier((x, earlier))[0] if earlier else x


def in_core_order(core, mine, other, axis):
    return jnp.where(
        core == 0,
        jnp.concatenate([mine, other], axis=axis),
        jnp.concatenate([other, mine], axis=axis),
    )


def gather_chunks(blocks):
    pieces, crossed, far = [], [], []
    for n, block in enumerate(blocks):
        if n >= 1:
            block = after(block, crossed[n - 1])
        z = [send(block, TO_Z[k]) for k in (1, 2, 3)]
        crossed.append(z)
        stack = jnp.stack([block] + z)
        if n >= 2:
            stack = after(stack, far[n - 2])
        both = jnp.stack([stack, send(stack, TO_NEAR)])
        distant = send(both, TO_FAR)
        far.append(distant)
        pieces.append([both, distant, send(both, TO_MATE), send(distant, TO_MATE)])
    return pieces


def chip_of(place, swapped, far, near, z):
    chip, core = place
    order = core ^ swapped
    near_bit = 2 - order
    far_bit = 1 + order
    return chip ^ (far * far_bit) ^ (near * near_bit) ^ (z * 4)


def run_copies(copies):
    for copy in copies:
        copy.start()
    for copy in copies:
        copy.wait()


def assemble_kernel(widths, place_ref, both, distant, mate_both, mate_distant, *rest):
    outs, sem = rest[:-1], rest[-1]
    place = (place_ref[0], place_ref[1])
    rows = both.shape[2]
    copies = []
    for source, swapped, far in (
        (both, 0, 0),
        (distant, 0, 1),
        (mate_both, 1, 0),
        (mate_distant, 1, 1),
    ):
        half = place[1] ^ swapped
        for near in range(2):
            for z in range(4):
                chip = chip_of(place, swapped, far, near, z)
                first = 0
                for out, width in zip(outs, widths):
                    copies.append(
                        pltpu.make_async_copy(
                            source.at[near, z, :, pl.ds(first, width)],
                            out.at[
                                pl.ds(pl.multiple_of(chip * rows, 16), rows),
                                pl.ds(pl.multiple_of(half * width, 128), width),
                            ],
                            sem,
                        )
                    )
                    first += width
    run_copies(copies)


def assemble(place, pieces, widths):
    rows = pieces[0].shape[2] * 16
    anywhere = pl.BlockSpec(memory_space=pl.ANY)
    return pl.pallas_call(
        functools.partial(assemble_kernel, widths),
        out_shape=[jax.ShapeDtypeStruct((rows, 2 * w), BF16) for w in widths],
        in_specs=[pl.BlockSpec(memory_space=pltpu.SMEM)] + [anywhere] * 4,
        out_specs=[pl.BlockSpec(memory_space=pltpu.VMEM)] * len(widths),
        scratch_shapes=[pltpu.SemaphoreType.DMA(())],
    )(place, *pieces)


def spread_kernel(widths, place_ref, *refs):
    count = len(widths)
    sources, (give, keep), sem = refs[:count], refs[count : count + 2], refs[-1]
    place = (place_ref[0], place_ref[1])
    rows = give.shape[3]
    copies = []
    for target, swapped in ((give, 1), (keep, 0)):
        half = place[1] ^ swapped
        for far in range(2):
            for near in range(2):
                for z in range(4):
                    chip = chip_of(place, swapped, far, near, z)
                    first = 0
                    for source, width in zip(sources, widths):
                        copies.append(
                            pltpu.make_async_copy(
                                source.at[
                                    pl.ds(pl.multiple_of(chip * rows, 16), rows),
                                    pl.ds(pl.multiple_of(half * width, 128), width),
                                ],
                                target.at[far, near, z, :, pl.ds(first, width)],
                                sem,
                            )
                        )
                        first += width
    run_copies(copies)


def spread(place, grads):
    widths = [g.shape[1] // 2 for g in grads]
    rows = grads[0].shape[0] // 16
    anywhere = pl.BlockSpec(memory_space=pl.ANY)
    shape = jax.ShapeDtypeStruct((2, 2, 4, rows, sum(widths)), BF16)
    return pl.pallas_call(
        functools.partial(spread_kernel, widths),
        out_shape=[shape, shape],
        in_specs=[pl.BlockSpec(memory_space=pltpu.SMEM)] + [pl.BlockSpec(memory_space=pltpu.VMEM)] * len(grads),
        out_specs=[anywhere] * 2,
        scratch_shapes=[pltpu.SemaphoreType.DMA(())],
    )(place, *grads)


def add_low(a, b):
    return (a.astype(F32) + b.astype(F32)).astype(BF16)


def scatter_chunk(core, give, keep, extra, earlier):
    parts = [(send(give, TO_MATE), keep)]
    if extra is not None:
        parts.append((send(extra[0], TO_MATE), extra[1]))
    give, keep = (
        jnp.concatenate([add_low(kept[far], got[far]) for got, kept in parts], axis=-1) for far in (1, 0)
    )
    got = send(after(give, earlier.get("near")), TO_FAR)
    give, keep = add_low(keep[1], got[1]), add_low(keep[0], got[0])
    got = send(give, TO_NEAR)
    near = got
    give = [add_low(keep[k], got[k]) for k in (1, 2, 3)]
    total = keep[0].astype(F32) + got[0].astype(F32)
    give = after(give, earlier.get("z"))
    z = [send(give[k - 1], TO_Z[k]) for k in (1, 2, 3)]
    for part in z:
        total = total + part.astype(F32)
    rows = total.shape[0] // 2
    total = total.reshape(2, rows, total.shape[1])
    mine = jnp.where(core == 0, total[0], total[1])
    other = send(jnp.where(core == 0, total[1], total[0]), TO_MATE)
    return (
        jnp.where(core == 0, mine, other),
        jnp.where(core == 0, other, mine),
    ), {"near": near, "z": z}


SMALL = 256


def pack_small(vectors, bias_up, pass_embed):
    rows = vectors[0].shape[0]
    first = jnp.stack(vectors, axis=1)
    second = jnp.concatenate([bias_up.reshape(rows, -1), pass_embed.T], axis=1)
    pad = lambda a: jnp.pad(a, ((0, 0), (0, SMALL // 2 - a.shape[1])))
    return jnp.concatenate([pad(first), pad(second)], axis=1)


def unpack_small(small):
    half = SMALL // 2
    vectors = [small[:, k] for k in range(8)]
    return vectors, small[:, half : half + 4].reshape(-1), small[:, half + 4 : half + 4 + PASSES].T


def is_known_slice():
    return lax.axis_size("dp") == 8 and lax.axis_size("fsdp") == 4


def place_of():
    index = lax.axis_index("dp") * 4 + lax.axis_index("fsdp")
    return jnp.stack([index >> 1, index & 1]).astype(jnp.int32)


def halves(*arrays):
    return [
        jnp.concatenate([a[:, h * (a.shape[1] // 2) : (h + 1) * (a.shape[1] // 2)] for a in arrays], axis=1)
        for h in range(2)
    ]


def gather_all(w_qkv, w_out, small, w_up, w_down):
    if not is_known_slice():
        whole = [lax.all_gather(a, AXES, axis=0, tiled=True) for a in (w_qkv, w_out, w_up, w_down, small)]
        return whole[:4], whole[4]
    place = place_of()
    core = place[1]
    blocks = []
    for arrays in ((w_qkv, w_out, small), (w_up,), (w_down,)):
        low, high = halves(*arrays)
        mine = jnp.where(core == 0, low, high)
        other = send(jnp.where(core == 0, high, low), TO_MATE)
        blocks.append(in_core_order(core, mine, other, 0))
    pieces = gather_chunks(blocks)
    first = (w_qkv.shape[1] + w_out.shape[1]) // 2
    (small,) = assemble(place, [p[..., first:] for p in pieces[0]], [small.shape[1] // 2])
    return pieces[0] + pieces[1] + pieces[2], small


def scatter_all(grads, small):
    if not is_known_slice():
        total = lambda g: lax.psum_scatter(g.astype(F32), AXES, scatter_dimension=0, tiled=True)
        return [total(g) for g in (*grads, small)]
    place = place_of()
    core = place[1]
    small_give, small_keep = spread(place, [small])
    sums, earlier = [], {}
    for n in range(3):
        give, keep = grads[2 * n], grads[2 * n + 1]
        extra = (small_give, small_keep) if n == 2 else None
        (low, high), earlier = scatter_chunk(core, give, keep, extra, earlier)
        sums.append((low, high))
    join = lambda n, first, width: jnp.concatenate([s[:, first : first + width] for s in sums[n]], axis=1)
    down_half, up_half, last = sums[0][0].shape[1], sums[1][0].shape[1], sums[2][0].shape[1]
    small_half = small.shape[1] // 2
    out_half = (last - small_half) // 4
    return [
        join(2, 0, 3 * out_half),
        join(2, 3 * out_half, out_half),
        join(1, 0, up_half),
        join(0, 0, down_half),
        join(2, 4 * out_half, small_half),
    ]


BIAS_Q, BIAS_V, BIAS_OUT, GAIN_ATTN, SHIFT_ATTN, GAIN_MLP, SHIFT_MLP, BIAS_DOWN, EMBED = range(9)
VECTORS = 16
PAIR = 2 * HEAD_DIM
SCALE = HEAD_DIM**-0.5
LOG2_E = 1.4426950408889634
GELU_A = 0.7978845608028654
GELU_B = 0.044715


def dot(a, b, a_dim, b_dim):
    return lax.dot_general(a, b, (((a_dim,), (b_dim,)), ((), ())), preferred_element_type=F32)


def nn(a, b):
    return dot(a, b, 1, 0)


def nt(a, b):
    return dot(a, b, 1, 1)


def tn(a, b):
    return dot(a, b, 0, 0)


def row_mean(x):
    return jnp.sum(x, axis=1, keepdims=True) * (1.0 / x.shape[1])


def normalized(x):
    centred = x - row_mean(x)
    inverse = lax.rsqrt(row_mean(centred * centred) + EPSILON)
    return centred * inverse, inverse


def gelu_and_slope(v):
    square = v * v
    t = jnp.tanh(v * (GELU_A + (GELU_A * GELU_B) * square))
    half = 0.5 * (1.0 + t)
    slope = half + v * (1.0 - t * t) * (0.5 * GELU_A + (1.5 * GELU_A * GELU_B) * square)
    return v * half, slope


def block_copies(place, arrays, targets, sems, out_of_full):
    copies = []
    for array, swapped, far in arrays:
        half = place[1] ^ swapped
        rows = array.shape[2]
        for near in range(2):
            for z in range(4):
                chip = chip_of(place, swapped, far, near, z)
                first = 0
                for (full, width), sem in zip(targets, sems):
                    inside = full.at[
                        pl.ds(pl.multiple_of(chip * rows, 16), rows),
                        pl.ds(pl.multiple_of(half * width, 128), width),
                    ]
                    block = array.at[near, z, :, pl.ds(first, width)]
                    source, target = (inside, block) if out_of_full else (block, inside)
                    copies.append(pltpu.make_async_copy(source, target, sem))
                    first += width
    return copies


def start_all(copies):
    for copy in copies:
        copy.start()


def wait_whole(full, sem):
    pltpu.make_async_copy(full, full, sem).wait()


def layer_kernel(known, *refs):
    place_ref, lengths_ref, tokens, cotangent, vec, bias_up = refs[:6]
    sources, refs = (refs[6:18], refs[18:]) if known else (refs[6:10], refs[10:])
    output, token_grad, g_vec, g_bias_up = refs[:4]
    results, refs = (refs[4:10], refs[10:]) if known else (refs[4:8], refs[8:])
    (
        w_qkv,
        w_out,
        w_up,
        w_down,
        x_norm,
        x_context,
        x_mlp,
        x_active,
        d_z,
        d_y,
        d_hidden,
        d_mixed,
        q_all,
        k_all,
        v_all,
        probs_0,
        probs_1,
        probs_2,
        entry,
        middle,
        k_grad,
        v_grad,
        state,
        extra,
        d_context,
        scores,
        d_scores,
        mask,
        in_sems,
        out_sems,
    ) = refs
    probs = (probs_0, probs_1, probs_2)
    length, width = state.shape
    inner = w_up.shape[1]
    pair_count = width // PAIR
    place = (place_ref[0], place_ref[1])

    weights = (w_qkv, w_out, w_up, w_down)
    if known:
        chunks = (
            (sources[0:4], (w_qkv, w_out), (0, 1)),
            (sources[4:8], (w_up,), (2,)),
            (sources[8:12], (w_down,), (3,)),
        )
        for pieces, targets, numbers in chunks:
            start_all(
                block_copies(
                    place,
                    list(zip(pieces, (0, 0, 1, 1), (0, 1, 0, 1))),
                    [(t, t.shape[1] // 2) for t in targets],
                    [in_sems.at[n] for n in numbers],
                    False,
                )
            )
    else:
        for n in range(4):
            pltpu.make_async_copy(sources[n], weights[n], in_sems.at[n]).start()

    def cols(n, size):
        return pl.ds(pl.multiple_of(n * size, size), size)

    rows_at = lax.broadcasted_iota(jnp.int32, (length, PASSES * length), 0)
    keys_at = lax.broadcasted_iota(jnp.int32, (length, PASSES * length), 1)
    for _ in range(PASSES - 1):
        keys_at = jnp.where(keys_at >= length, keys_at - length, keys_at)
    same = keys_at <= rows_at
    end = 0
    for n in range(lengths_ref.shape[0]):
        end = end + lengths_ref[n]
        same = same & ((rows_at >= end) == (keys_at >= end))
    mask[...] = jnp.where(same, 0.0, -1e30)

    lane = lax.broadcasted_iota(jnp.int32, (1, PAIR), 1)
    first_head = (lane < HEAD_DIM).astype(F32).astype(BF16)
    second_head = (lane >= HEAD_DIM).astype(F32).astype(BF16)

    def stacked(x):
        return jnp.concatenate([x * first_head, x * second_head], axis=0)

    def unstacked(x):
        return jnp.where(lane < HEAD_DIM, x[:length], x[length:])

    def vector(n):
        return vec[n : n + 1, :]

    LN_ROWS = 32
    SOFT_ROWS = 64
    g_vec[...] = jnp.zeros(g_vec.shape, F32)

    for b in range(0, length, 64):
        state[b : b + 64, :] = tokens[b : b + 64, :].astype(F32)

    for r in range(PASSES):
        at = r * length
        mine = pl.ds(at, length)
        seen = (r + 1) * length
        for b in range(0, length, LN_ROWS):
            x = state[b : b + LN_ROWS, :] + vector(EMBED + r)
            entry[at + b : at + b + LN_ROWS, :] = x
            n, _ = normalized(x)
            x_norm[at + b : at + b + LN_ROWS, :] = (n * vector(GAIN_ATTN) + vector(SHIFT_ATTN)).astype(BF16)
        if r == 0:
            wait_whole(w_qkv, in_sems.at[0])
        for part, (target, bias) in enumerate(((q_all, BIAS_Q), (k_all, None), (v_all, BIAS_V))):
            for c in range(0, width, 256):
                acc = nn(x_norm[mine, :], w_qkv[:, part * width + c : part * width + c + 256])
                if bias is not None:
                    acc = acc + vec[bias : bias + 1, c : c + 256]
                target[mine, c : c + 256] = acc.astype(BF16)

        def attend(j, _):
            c = cols(j, PAIR)
            scores[:, :seen] = nt(stacked(q_all[mine, c]), k_all[:seen, c])
            for b in range(0, 2 * length, SOFT_ROWS):
                part = slice(b, b + SOFT_ROWS)
                m = b % length
                s = scores[part, :seen] + mask[m : m + SOFT_ROWS, :seen]
                p = jnp.exp2((s - jnp.max(s, axis=1, keepdims=True)) * (SCALE * LOG2_E))
                p = p * (1.0 / jnp.sum(p, axis=1, keepdims=True))
                probs[r][j, part, :] = p.astype(BF16)
            x_context[mine, c] = unstacked(nn(probs[r][j], v_all[:seen, c])).astype(BF16)

        lax.fori_loop(0, pair_count, attend, None)
        if r == 0:
            wait_whole(w_out, in_sems.at[1])
        for c in range(0, width, 256):
            acc = nn(x_context[mine, :], w_out[:, c : c + 256])
            middle[mine, c : c + 256] = entry[mine, c : c + 256] + acc + vec[BIAS_OUT : BIAS_OUT + 1, c : c + 256]
        for b in range(0, length, LN_ROWS):
            n, _ = normalized(middle[at + b : at + b + LN_ROWS, :])
            x_mlp[at + b : at + b + LN_ROWS, :] = (n * vector(GAIN_MLP) + vector(SHIFT_MLP)).astype(BF16)
        if r == 0:
            wait_whole(w_up, in_sems.at[2])

        def up(j, _):
            c = cols(j, 256)
            value, slope = gelu_and_slope(nn(x_mlp[mine, :], w_up[:, c]) + bias_up[:, c])
            x_active[mine, c] = value.astype(BF16)
            d_hidden[mine, c] = slope.astype(BF16)

        lax.fori_loop(0, inner // 256, up, None, unroll=6)
        if r == 0:
            wait_whole(w_down, in_sems.at[3])
        for c in range(0, width, 256):
            acc = nn(x_active[mine, :], w_down[:, c : c + 256])
            state[:, c : c + 256] = middle[mine, c : c + 256] + acc + vec[BIAS_DOWN : BIAS_DOWN + 1, c : c + 256]

    for b in range(0, length, 64):
        output[b : b + 64, :] = state[b : b + 64, :].astype(BF16)
        state[b : b + 64, :] = cotangent[b : b + 64, :].astype(F32)

    def norm_backward(source, at, gain, g_gain, g_shift, rounded, g_embed):
        for b in range(0, length, LN_ROWS):
            part = slice(b, b + LN_ROWS)
            n, inverse = normalized(source[at + b : at + b + LN_ROWS, :])
            e = extra[part, :]
            g_vec[g_gain : g_gain + 1, :] += jnp.sum(e * n, axis=0, keepdims=True)
            g_vec[g_shift : g_shift + 1, :] += jnp.sum(e, axis=0, keepdims=True)
            eg = e * vector(gain)
            back = state[part, :] + inverse * (eg - row_mean(eg) - n * row_mean(eg * n))
            state[part, :] = back
            if rounded is not None:
                rounded[at + b : at + b + LN_ROWS, :] = back.astype(BF16)
            if g_embed is not None:
                g_vec[g_embed : g_embed + 1, :] += jnp.sum(back, axis=0, keepdims=True)

    ones = jnp.ones((16, PASSES * length), BF16)

    def send_out(n, targets):
        if known:
            give, keep = results[2 * n], results[2 * n + 1]
            arrays = []
            for array, swapped in ((give, 1), (keep, 0)):
                arrays += [(array.at[0], swapped, 0), (array.at[1], swapped, 1)]
            start_all(
                block_copies(
                    place,
                    arrays,
                    [(weights[t], weights[t].shape[1] // 2) for t in targets],
                    [out_sems.at[t] for t in targets],
                    True,
                )
            )
        else:
            for t in targets:
                pltpu.make_async_copy(weights[t], results[t], out_sems.at[t]).start()

    for r in reversed(range(PASSES)):
        at = r * length
        mine = pl.ds(at, length)
        seen = (r + 1) * length
        for b in range(0, length, 64):
            d_z[at + b : at + b + 64, :] = state[b : b + 64, :].astype(BF16)

        def down_back(j, _):
            c = cols(j, 256)
            acc = nt(d_z[mine, :], w_down[c, :])
            d_hidden[mine, c] = (acc * d_hidden[mine, c].astype(F32)).astype(BF16)

        lax.fori_loop(0, inner // 256, down_back, None, unroll=6)
        if r == 0:

            def down_grad(j, _):
                c = cols(j, 256)
                w_down[c, :] = tn(x_active[:, c], d_z[...]).astype(BF16)

            lax.fori_loop(0, inner // 256, down_grad, None, unroll=2)
            send_out(0, (3,))
            g_vec[BIAS_DOWN : BIAS_DOWN + 1, :] = nn(ones, d_z[...])[:1]
        for c in range(0, width, 256):
            extra[:, c : c + 256] = nt(d_hidden[mine, :], w_up[c : c + 256, :])
        if r == 0:

            def up_grad(j, _):
                c = cols(j, 768)
                w_up[:, c] = tn(x_mlp[...], d_hidden[:, c]).astype(BF16)
                g_bias_up[:, c] = nn(ones, d_hidden[:, c])[:1]

            lax.fori_loop(0, inner // 768, up_grad, None)
            send_out(1, (2,))
        norm_backward(middle, at, GAIN_MLP, GAIN_MLP, SHIFT_MLP, d_y, None)
        for c in range(0, width, 256):
            d_context[:, c : c + 256] = nt(d_y[mine, :], w_out[c : c + 256, :]).astype(BF16)

        def attend_back(j, _):
            c = cols(j, PAIR)
            dc = d_context[:, c]
            both = stacked(dc)
            scores[:, :seen] = nt(both, v_all[:seen, c])
            product = dc.astype(F32) * x_context[mine, c].astype(F32)
            inner_0 = jnp.sum(jnp.where(lane < HEAD_DIM, product, 0.0), axis=1, keepdims=True)
            inner_1 = jnp.sum(jnp.where(lane < HEAD_DIM, 0.0, product), axis=1, keepdims=True)
            for b in range(0, 2 * length, SOFT_ROWS):
                part = slice(b, b + SOFT_ROWS)
                m = b % length
                shift = (inner_0 if b < length else inner_1)[m : m + SOFT_ROWS]
                d_scores[part, :seen] = (
                    probs[r][j, part, :].astype(F32) * (scores[part, :seen] - shift)
                ).astype(BF16)
            ds = d_scores[:, :seen]
            d_mixed[mine, c] = (unstacked(nn(ds, k_all[:seen, c])) * SCALE).astype(BF16)
            k_more = tn(ds, stacked(q_all[mine, c]))
            v_more = tn(probs[r][j], both)
            if r == PASSES - 1:
                k_grad[:seen, c] = k_more
                v_grad[:seen, c] = v_more
            else:
                k_grad[:seen, c] += k_more
                v_grad[:seen, c] += v_more

        lax.fori_loop(0, pair_count, attend_back, None)
        for b in range(0, length, 64):
            part = slice(at + b, at + b + 64)
            d_mixed[part, width : 2 * width] = (k_grad[part, :] * SCALE).astype(BF16)
            d_mixed[part, 2 * width :] = v_grad[part, :].astype(BF16)
        for c in range(0, width, 256):
            extra[:, c : c + 256] = nt(d_mixed[mine, :], w_qkv[c : c + 256, :])
        norm_backward(entry, at, GAIN_ATTN, GAIN_ATTN, SHIFT_ATTN, None, EMBED + r)

    for b in range(0, length, 64):
        token_grad[b : b + 64, :] = state[b : b + 64, :].astype(BF16)
    w_out[...] = tn(x_context[...], d_y[...]).astype(BF16)
    for c in range(0, 3 * width, width):
        w_qkv[:, c : c + width] = tn(x_norm[...], d_mixed[:, c : c + width]).astype(BF16)
    send_out(2, (0, 1))
    g_vec[BIAS_Q : BIAS_Q + 1, :] = nn(ones, d_mixed[:, :width])[:1]
    g_vec[BIAS_V : BIAS_V + 1, :] = nn(ones, d_mixed[:, 2 * width :])[:1]
    g_vec[BIAS_OUT : BIAS_OUT + 1, :] = nn(ones, d_y[...])[:1]
    for n in range(4):
        wait_whole(weights[n], out_sems.at[n])


def layer(place, lengths, tokens, cotangent, vec, bias_up, sources, known):
    length, width = tokens.shape
    inner = bias_up.shape[1]
    total = PASSES * length
    anywhere = pl.BlockSpec(memory_space=pl.ANY)
    local = pl.BlockSpec(memory_space=pltpu.VMEM)
    scalars = pl.BlockSpec(memory_space=pltpu.SMEM)
    struct = jax.ShapeDtypeStruct
    full = [(width, 3 * width), (width, width), (width, inner), (inner, width)]
    if known:
        results = []
        for rows, half in ((inner // 16, width // 2), (width // 16, inner // 2), (width // 16, 2 * width)):
            results += [struct((2, 2, 4, rows, half), BF16)] * 2
    else:
        results = [struct(shape, BF16) for shape in full]
    low = lambda *shape: pltpu.VMEM(shape, BF16)
    wide = lambda *shape: pltpu.VMEM(shape, F32)
    pairs_ = width // PAIR
    return pl.pallas_call(
        functools.partial(layer_kernel, known),
        out_shape=[
            struct((length, width), BF16),
            struct((length, width), BF16),
            struct((VECTORS, width), F32),
            struct((1, inner), F32),
        ]
        + results,
        in_specs=[scalars, scalars] + [local] * 4 + [anywhere] * len(sources),
        out_specs=[local] * 4 + [anywhere] * len(results),
        scratch_shapes=[low(*shape) for shape in full]
        + [low(total, width)] * 3
        + [low(total, inner)]
        + [low(total, width)] * 2
        + [low(total, inner), low(total, 3 * width)]
        + [low(total, width)] * 3
        + [low(pairs_, 2 * length, (r + 1) * length) for r in range(PASSES)]
        + [wide(total, width)] * 4
        + [wide(length, width)] * 2
        + [low(length, width), wide(2 * length, total), low(2 * length, total), wide(length, total)]
        + [pltpu.SemaphoreType.DMA((4,)), pltpu.SemaphoreType.DMA((4,))],
        compiler_params=pltpu.CompilerParams(vmem_limit_bytes=60 * 2**20),
        name="layer",
    )(place, lengths, tokens, cotangent, vec, bias_up, *sources)


def per_device(
    tokens,
    lengths,
    cotangent,
    w_qkv,
    bias_q,
    bias_v,
    w_out,
    bias_out,
    gain_attn,
    shift_attn,
    gain_mlp,
    shift_mlp,
    w_up,
    bias_up,
    w_down,
    bias_down,
    pass_embed,
):
    known = is_known_slice()
    place = place_of()
    small = pack_small(
        [bias_q, bias_v, bias_out, gain_attn, shift_attn, gain_mlp, shift_mlp, bias_down], bias_up, pass_embed
    )
    sources, small = gather_all(w_qkv, w_out, small, w_up, w_down)
    vectors, bias_up, pass_embed = unpack_small(small)
    vec = jnp.concatenate([jnp.stack(vectors), pass_embed], axis=0).astype(F32)
    vec = jnp.pad(vec, ((0, VECTORS - vec.shape[0]), (0, 0)))
    output, token_grad, g_vec, g_bias_up, *results = layer(
        place, lengths[0], tokens, cotangent, vec, bias_up.astype(F32)[None, :], sources, known
    )
    g_small = pack_small([g_vec[n] for n in range(8)], g_bias_up[0], g_vec[8 : 8 + PASSES]).astype(BF16)
    g_qkv, g_out, g_up, g_down, g_small = scatter_all(results, g_small)
    (g_bq, g_bv, g_bo, g_ga, g_sa, g_gm, g_sm, g_bd), g_bu, g_pe = unpack_small(g_small)
    return (
        output,
        token_grad,
        g_qkv,
        g_bq,
        g_bv,
        g_out,
        g_bo,
        g_ga,
        g_sa,
        g_gm,
        g_sm,
        g_up,
        g_bu,
        g_down,
        g_bd,
        g_pe,
    )


def solution(mesh):
    placed = (
        P(("dp", "fsdp"), None),
        P(("dp", "fsdp"), None),
        P(("dp", "fsdp"), None),
        P(("dp", "fsdp"), None),
        P(("dp", "fsdp")),
        P(("dp", "fsdp")),
        P(("dp", "fsdp"), None),
        P(("dp", "fsdp")),
        P(("dp", "fsdp")),
        P(("dp", "fsdp")),
        P(("dp", "fsdp")),
        P(("dp", "fsdp")),
        P(("dp", "fsdp"), None),
        P(("dp", "fsdp")),
        P(("dp", "fsdp"), None),
        P(("dp", "fsdp")),
        P(None, ("dp", "fsdp")),
    )
    return jax.shard_map(
        per_device,
        mesh=mesh,
        in_specs=placed,
        out_specs=(
            P(("dp", "fsdp"), None),
            P(("dp", "fsdp"), None),
            P(("dp", "fsdp"), None),
            P(("dp", "fsdp")),
            P(("dp", "fsdp")),
            P(("dp", "fsdp"), None),
            P(("dp", "fsdp")),
            P(("dp", "fsdp")),
            P(("dp", "fsdp")),
            P(("dp", "fsdp")),
            P(("dp", "fsdp")),
            P(("dp", "fsdp"), None),
            P(("dp", "fsdp")),
            P(("dp", "fsdp"), None),
            P(("dp", "fsdp")),
            P(None, ("dp", "fsdp")),
        ),
        check_vma=False,
    )
```

```python
import functools
import math

import jax
import jax.numpy as jnp
from jax import lax
from jax.experimental import pallas as pl
from jax.experimental.pallas import tpu as pltpu
from jax.sharding import PartitionSpec as P

HEAD_DIM = 64
PASSES = 3
EPSILON = 1e-05
AXES = ("dp", "fsdp")
F32 = jnp.float32
BF16 = jnp.bfloat16


def pairs(partner):
    return [(i, partner(i)) for i in range(32)]


TO_MATE = pairs(lambda i: i ^ 1)
TO_Z = [pairs(lambda i, k=k: i ^ (8 * k)) for k in range(4)]
TO_NEAR = pairs(lambda i: i ^ (2 if i & 1 else 4))
TO_FAR = pairs(lambda i: i ^ (4 if i & 1 else 2))


def send(x, route):
    return lax.ppermute(x, AXES, route)


def after(x, *earlier):
    earlier = tuple(e for e in earlier if e is not None)
    return lax.optimization_barrier((x, earlier))[0] if earlier else x


def in_core_order(core, mine, other, axis):
    return jnp.where(
        core == 0,
        jnp.concatenate([mine, other], axis=axis),
        jnp.concatenate([other, mine], axis=axis),
    )


def stack_kernel(*refs):
    for n, ref in enumerate(refs[:-1]):
        refs[-1][n] = ref[...]


def stack_blocks(blocks, weight):
    if not weight:
        return jnp.stack(blocks)
    return pl.pallas_call(
        stack_kernel,
        out_shape=jax.ShapeDtypeStruct((len(blocks), *blocks[0].shape), BF16),
        in_specs=[pl.BlockSpec(memory_space=pltpu.VMEM)] * len(blocks),
        out_specs=pl.BlockSpec(memory_space=pltpu.VMEM),
        compiler_params=pltpu.CompilerParams(vmem_limit_bytes=8 * 2**20),
        cost_estimate=pl.CostEstimate(flops=weight * 10**9, bytes_accessed=weight * 35 * 10**5, transcendentals=0),
        name="stack",
    )(*blocks)


STACK_WEIGHTS = (0, 0, 10)
BOTH_WEIGHTS = (10, 0, 0)


def gather_chunks(blocks):
    chunks, earlier = [], None
    for n, block in enumerate(blocks):
        block = after(block, earlier)
        earlier = [send(block, TO_Z[k]) for k in (1, 2, 3)]
        stack = stack_blocks([block] + earlier, STACK_WEIGHTS[n])
        both = stack_blocks([stack, send(stack, TO_NEAR)], BOTH_WEIGHTS[n])
        chunks.append([both, None, send(both, TO_MATE), None])
    return chunks, earlier


def far_pieces(pieces, *earlier):
    if pieces[1] is None:
        pieces[1] = send(after(pieces[0], *earlier), TO_FAR)


def mate_pieces(pieces, *earlier):
    if pieces[3] is None:
        pieces[3] = send(after(pieces[1], *earlier), TO_MATE)


def chip_of(place, swapped, far, near, z):
    chip, core = place
    order = core ^ swapped
    near_bit = 2 - order
    far_bit = 1 + order
    return chip ^ (far * far_bit) ^ (near * near_bit) ^ (z * 4)


def add_low(a, b):
    return (a.astype(F32) + b.astype(F32)).astype(BF16)


def add_kernel(got, keep, give_out, keep_out):
    for n in range(got.shape[1]):
        give_out[n] = (keep[1, n].astype(F32) + got[1, n].astype(F32)).astype(BF16)
        keep_out[n] = (keep[0, n].astype(F32) + got[0, n].astype(F32)).astype(BF16)


def add_halves(got, keep, weight):
    if not weight:
        return add_low(keep[1], got[1]), add_low(keep[0], got[0])
    shape, merged = keep.shape[1:], (2, -1, keep.shape[-2], keep.shape[-1])
    got, keep = got.reshape(merged), keep.reshape(merged)
    give, keep = pl.pallas_call(
        add_kernel,
        out_shape=[jax.ShapeDtypeStruct(keep.shape[1:], BF16)] * 2,
        in_specs=[pl.BlockSpec(memory_space=pltpu.VMEM)] * 2,
        out_specs=[pl.BlockSpec(memory_space=pltpu.VMEM)] * 2,
        compiler_params=pltpu.CompilerParams(vmem_limit_bytes=8 * 2**20),
        cost_estimate=pl.CostEstimate(flops=weight * 10**9, bytes_accessed=weight * 35 * 10**5, transcendentals=0),
        name="add",
    )(got, keep)
    return give.reshape(shape), keep.reshape(shape)


def begin_scatter(give, keep, weight):
    if not is_known_slice():
        return give, keep
    split = lambda a: a.reshape(2, 2, 4, *a.shape[1:])
    return add_halves(split(send(give, TO_MATE)), split(keep), weight)


def far_step(part):
    give, keep = part
    if not is_known_slice():
        return part
    return send(give, TO_FAR), keep


def near_step(part, weight):
    got, keep = part
    if not is_known_slice():
        return part
    give, keep = add_halves(got, keep, weight)
    return send(give, TO_NEAR), keep


def end_scatter(core, begun):
    begun = [begun[0]] + [near_step(begun[n], FAR_WEIGHTS[n]) for n in (1, 2)]
    results, earlier = [], None
    for n in range(len(begun)):
        near, keep = begun[n]
        z = [add_low(keep[k], near[k]) for k in (1, 2, 3)]
        z = [send(give, TO_Z[k + 1]) for k, give in enumerate(after(z, earlier))]
        earlier = z if n == 0 else None
        total = keep[0].astype(F32) + near[0].astype(F32)
        for part in z:
            total = total + part.astype(F32)
        total = total.reshape(2, total.shape[0] // 2, total.shape[1])
        mine = jnp.where(core == 0, total[0], total[1])
        other = send(jnp.where(core == 0, total[1], total[0]), TO_MATE)
        results.append((jnp.where(core == 0, mine, other), jnp.where(core == 0, other, mine)))
    return results


MATE_WEIGHTS = (0, 15, 0)
FAR_WEIGHTS = (0, 0, 0)
SMALL = 256


def pack_small(vectors, bias_up, pass_embed):
    rows = vectors[0].shape[0]
    first = jnp.stack(vectors, axis=1)
    second = jnp.concatenate([bias_up.reshape(rows, -1), pass_embed.T], axis=1)
    pad = lambda a: jnp.pad(a, ((0, 0), (0, SMALL // 2 - a.shape[1])))
    return jnp.concatenate([pad(first), pad(second)], axis=1)


def unpack_small(small):
    half = SMALL // 2
    vectors = [small[:, k] for k in range(8)]
    return vectors, small[:, half : half + 4].reshape(-1), small[:, half + 4 : half + 4 + PASSES].T


def is_known_slice():
    return lax.axis_size("dp") == 8 and lax.axis_size("fsdp") == 4


def place_of():
    if not is_known_slice():
        return jnp.zeros((2,), jnp.int32)
    index = lax.axis_index("dp") * 4 + lax.axis_index("fsdp")
    return jnp.stack([index >> 1, index & 1]).astype(jnp.int32)


def halves(*arrays):
    return [
        jnp.concatenate([a[:, h * (a.shape[1] // 2) : (h + 1) * (a.shape[1] // 2)] for a in arrays], axis=1)
        for h in range(2)
    ]


def slots(swapped):
    return [chip_of((0, 0), swapped, far, near, z) for far in range(2) for near in range(2) for z in range(4)]


def gather_all(w_qkv, w_out, small, w_up, w_down):
    place = place_of()
    groups = ((w_qkv, small), (w_up, w_out), (w_down,))
    if not is_known_slice():
        chunks = []
        for arrays in groups:
            whole = [lax.all_gather(a, AXES, axis=0, tiled=True) for a in arrays]
            pieces = []
            for swapped, part in enumerate(halves(*whole)):
                blocks = part.reshape(16, -1, part.shape[1])
                blocks = jnp.stack([blocks[chip] for chip in slots(swapped)])
                pieces += list(blocks.reshape(2, 2, 4, *blocks.shape[1:]))
            chunks.append(pieces)
        return place, chunks, ()
    core = place[1]
    blocks = []
    for arrays in groups:
        low, high = halves(*arrays)
        mine = jnp.where(core == 0, low, high)
        other = send(jnp.where(core == 0, high, low), TO_MATE)
        blocks.append(in_core_order(core, mine, other, 0))
    chunks, last_z = gather_chunks(blocks)
    return place, chunks, last_z


def scatter_all(parts):
    if is_known_slice():
        sums = end_scatter(place_of()[1], list(parts))
    else:
        sums = []
        for give, keep in parts:
            both = []
            for blocks, swapped in ((keep, 0), (give, 1)):
                order = slots(swapped)
                whole = jnp.concatenate([blocks[order.index(chip)] for chip in range(16)], axis=0)
                both.append(lax.psum_scatter(whole.astype(F32), AXES, scatter_dimension=0, tiled=True))
            sums.append(both)
    join = lambda n, first, width: jnp.concatenate([s[:, first : first + width] for s in sums[n]], axis=1)
    small_half = SMALL // 2
    qkv_half = sums[2][0].shape[1] - small_half
    out_half = qkv_half // 3
    up_half_ = sums[1][0].shape[1] - out_half
    return [
        join(2, 0, qkv_half),
        join(1, up_half_, out_half),
        join(1, 0, up_half_),
        join(0, 0, sums[0][0].shape[1]),
        join(2, qkv_half, small_half),
    ]


BIAS_Q, BIAS_V, BIAS_OUT, GAIN_ATTN, SHIFT_ATTN, GAIN_MLP, SHIFT_MLP, BIAS_DOWN, EMBED = range(9)
VECTORS = 16
PAIR = 2 * HEAD_DIM
SCALE = HEAD_DIM**-0.5
LOG2_E = 1.4426950408889634
GELU_A = 0.7978845608028654
GELU_B = 0.044715
LN_ROWS = 32
COST = (10 * 10**9, 35 * 2**20)
SOFT_ROWS = 64
WIDE = 256


def dot(a, b, a_dim, b_dim):
    return lax.dot_general(a, b, (((a_dim,), (b_dim,)), ((), ())), preferred_element_type=F32)


def nn(a, b):
    return dot(a, b, 1, 0)


def nt(a, b):
    return dot(a, b, 1, 1)


def tn(a, b):
    return dot(a, b, 0, 0)


def cols(n, size):
    return pl.ds(pl.multiple_of(n * size, size), size)


def row_mean(x):
    return jnp.sum(x, axis=1, keepdims=True) * (1.0 / x.shape[1])


def normalized(x):
    centred = x - row_mean(x)
    inverse = lax.rsqrt(row_mean(centred * centred) + EPSILON)
    return centred * inverse, inverse


def gelu_and_slope(v):
    square = v * v
    t = jnp.tanh(v * (GELU_A + (GELU_A * GELU_B) * square))
    half = 0.5 * (1.0 + t)
    slope = half + v * (1.0 - t * t) * (0.5 * GELU_A + (1.5 * GELU_A * GELU_B) * square)
    return v * half, slope


def iota(shape, dim):
    return lax.broadcasted_iota(jnp.int32, shape, dim)


def first_lanes():
    return iota((1, PAIR), 1) < HEAD_DIM


def stacked(x):
    low = first_lanes().astype(F32)
    return jnp.concatenate([x * low.astype(BF16), x * (1.0 - low).astype(BF16)], axis=0)


def unstacked(x):
    length = x.shape[0] // 2
    return jnp.where(first_lanes(), x[:length], x[length:])


def fetch(place_ref, pieces, targets, sems):
    place = (place_ref[0], place_ref[1])
    for source, swapped, far in zip(pieces, (0, 0, 1, 1), (0, 1, 0, 1)):
        half = place[1] ^ swapped
        rows = source.shape[2]
        for near in range(2):
            for z in range(4):
                chip = chip_of(place, swapped, far, near, z)
                first = 0
                for n, full in enumerate(targets):
                    width = full.shape[1] // 2
                    pltpu.make_async_copy(
                        source.at[near, z, :, pl.ds(first, width)],
                        full.at[
                            pl.ds(pl.multiple_of(chip * rows, 16), rows),
                            pl.ds(pl.multiple_of(half * width, 128), width),
                        ],
                        sems.at[n],
                    ).start()
                    first += width


def wait_whole(full, sem):
    pltpu.make_async_copy(full, full, sem).wait()


def slot_of(place_ref, swapped, chip):
    apart = chip ^ place_ref[0]
    order = place_ref[1] ^ swapped
    x, y = apart & 1, (apart >> 1) & 1
    far = x + order * (y - x)
    near = y + order * (x - y)
    return far * 8 + near * 4 + (apart >> 2)


def put_blocks(place_ref, swapped, target, value, first_chip, first_col):
    rows = target.shape[1]
    for n in range(value.shape[0] // rows):
        slot = slot_of(place_ref, swapped, first_chip + n)
        target[slot, :, first_col : first_col + value.shape[1]] = value[n * rows : (n + 1) * rows, :]


def half_start(place_ref, swapped, width):
    return pl.multiple_of((place_ref[1] ^ swapped) * width, 128)


def pick_vectors(offset, first, last):
    row, col = iota((VECTORS, SMALL // 2), 0), iota((VECTORS, SMALL // 2), 1)
    return ((col == row + offset) & (row >= first) & (row < last)).astype(F32).astype(BF16)


def spread_four():
    row, col = iota((SMALL // 2, WIDE), 0), iota((SMALL // 2, WIDE), 1)
    return ((row < 4) & ((col & 3) == row)).astype(F32).astype(BF16)


def own_lanes():
    return (iota((WIDE // 4, WIDE), 1) >> 2) == iota((WIDE // 4, WIDE), 0)


def norm_forward(source, at, length, vec, gain, shift, target, to):
    for b in range(0, length, LN_ROWS):
        n, _ = normalized(source[at + b : at + b + LN_ROWS, :])
        target[to + b : to + b + LN_ROWS, :] = (n * vec[gain : gain + 1, :] + vec[shift : shift + 1, :]).astype(BF16)


def norm_backward(source, at, extra, state, vec, gain, shift, g_vec, rounded, to, embed):
    for b in range(0, state.shape[0], LN_ROWS):
        part = slice(b, b + LN_ROWS)
        n, inverse = normalized(source[at + b : at + b + LN_ROWS, :])
        e = extra[part, :]
        g_vec[gain : gain + 1, :] += jnp.sum(e * n, axis=0, keepdims=True)
        g_vec[shift : shift + 1, :] += jnp.sum(e, axis=0, keepdims=True)
        eg = e * vec[gain : gain + 1, :]
        back = state[part, :] + inverse * (eg - row_mean(eg) - n * row_mean(eg * n))
        state[part, :] = back
        if rounded is not None:
            rounded[to + b : to + b + LN_ROWS, :] = back.astype(BF16)
        if embed is not None:
            g_vec[embed : embed + 1, :] += jnp.sum(back, axis=0, keepdims=True)


def attend(j, q, k, v, probs, scores, mask, context, at, seen):
    length = mask.shape[0]
    mine = pl.ds(at, length)
    c = cols(j, PAIR)
    scores[:, :seen] = nt(stacked(q[mine, c]), k[:seen, c])
    for b in range(0, 2 * length, SOFT_ROWS):
        part = slice(b, b + SOFT_ROWS)
        m = b % length
        s = scores[part, :seen] + mask[m : m + SOFT_ROWS, :seen]
        p = jnp.exp2((s - jnp.max(s, axis=1, keepdims=True)) * (SCALE * LOG2_E))
        p = p * (1.0 / jnp.sum(p, axis=1, keepdims=True))
        probs[j, part, :] = p.astype(BF16)
    context[mine, c] = unstacked(nn(probs[j], v[:seen, c])).astype(BF16)


def attend_back(j, q, k, v, probs, scores, d_scores, d_context, context, at, seen, d_query, k_grad, v_grad, fresh):
    length = d_context.shape[0]
    mine = pl.ds(at, length)
    c = cols(j, PAIR)
    dc = d_context[:, c]
    both = stacked(dc)
    scores[:, :seen] = nt(both, v[:seen, c])
    product = dc.astype(F32) * context[mine, c].astype(F32)
    inner_0 = jnp.sum(jnp.where(first_lanes(), product, 0.0), axis=1, keepdims=True)
    inner_1 = jnp.sum(jnp.where(first_lanes(), 0.0, product), axis=1, keepdims=True)
    for b in range(0, 2 * length, SOFT_ROWS):
        part = slice(b, b + SOFT_ROWS)
        m = b % length
        shift = (inner_0 if b < length else inner_1)[m : m + SOFT_ROWS]
        d_scores[part, :seen] = (probs[j, part, :].astype(F32) * (scores[part, :seen] - shift)).astype(BF16)
    ds = d_scores[:, :seen]
    d_query[mine, c] = (unstacked(nn(ds, k[:seen, c])) * SCALE).astype(BF16)
    k_more = tn(ds, stacked(q[mine, c]))
    v_more = tn(probs[j], both)
    if fresh:
        k_grad[:seen, c] = k_more
        v_grad[:seen, c] = v_more
    else:
        k_grad[:seen, c] += k_more
        v_grad[:seen, c] += v_more


def feed_up(x_mlp, at, length, w_up, bias_up, active, slope, to):
    def step(j, _):
        c = cols(j, WIDE)
        value, rise = gelu_and_slope(nn(x_mlp[pl.ds(at, length), :], w_up[:, c]) + bias_up[:, c])
        active[pl.ds(to, length), c] = value.astype(BF16)
        slope[pl.ds(to, length), c] = rise.astype(BF16)

    lax.fori_loop(0, w_up.shape[1] // WIDE, step, None, unroll=6)


def project_in(x_norm, at, length, w_qkv, vec, targets, to):
    width = w_qkv.shape[0]
    for part, (target, bias) in enumerate(zip(targets, (BIAS_Q, None, BIAS_V))):
        for c in range(0, width, WIDE):
            acc = nn(x_norm[at : at + length, :], w_qkv[:, part * width + c : part * width + c + WIDE])
            if bias is not None:
                acc = acc + vec[bias : bias + 1, c : c + WIDE]
            target[to[part] : to[part] + length, c : c + WIDE] = acc.astype(BF16)


def project_out(context, at, length, w_out, vec, entry, middle):
    for c in range(0, w_out.shape[1], WIDE):
        acc = nn(context[at : at + length, :], w_out[:, c : c + WIDE])
        middle[at : at + length, c : c + WIDE] = (
            entry[at : at + length, c : c + WIDE] + acc + vec[BIAS_OUT : BIAS_OUT + 1, c : c + WIDE]
        )


def feed_down(active, at, length, w_down, vec, middle, middle_at, state):
    for c in range(0, w_down.shape[1], WIDE):
        acc = nn(active[at : at + length, :], w_down[:, c : c + WIDE])
        state[:, c : c + WIDE] = (
            middle[middle_at : middle_at + length, c : c + WIDE] + acc + vec[BIAS_DOWN : BIAS_DOWN + 1, c : c + WIDE]
        )


def enter(state, r, vec, entry, at):
    for b in range(0, state.shape[0], LN_ROWS):
        entry[at + b : at + b + LN_ROWS, :] = state[b : b + LN_ROWS, :].astype(F32) + vec[EMBED + r : EMBED + r + 1, :]


def start_kernel(
    place_ref, lengths_ref, tokens, p0, p1, p2, p3,
    w_qkv, vec, bias_up, mask, x_norm, q, k, v, probs, context, entry,
    small, scores, sems,
):
    length, width = tokens.shape
    fetch(place_ref, (p0, p1, p2, p3), (w_qkv, small), sems)

    rows_at, keys_at = iota(mask.shape, 0), iota(mask.shape, 1)
    for _ in range(PASSES - 1):
        keys_at = jnp.where(keys_at >= length, keys_at - length, keys_at)
    same = keys_at <= rows_at
    end = 0
    for n in range(lengths_ref.shape[0]):
        end = end + lengths_ref[n]
        same = same & ((rows_at >= end) == (keys_at >= end))
    mask[...] = jnp.where(same, 0.0, -1e30)

    wait_whole(small, sems.at[1])
    side = SMALL // 2
    vec[...] = nt(pick_vectors(0, 0, EMBED), small[:, :side]) + nt(
        pick_vectors(4 - EMBED, EMBED, EMBED + PASSES), small[:, side:]
    )
    repeated = nn(small[:, side:], spread_four())
    for b in range(bias_up.shape[1] // WIDE):
        rows = repeated[b * (WIDE // 4) : (b + 1) * (WIDE // 4), :]
        bias_up[:, b * WIDE : (b + 1) * WIDE] = jnp.sum(jnp.where(own_lanes(), rows, 0.0), axis=0, keepdims=True)

    enter(tokens, 0, vec, entry, 0)
    norm_forward(entry, 0, length, vec, GAIN_ATTN, SHIFT_ATTN, x_norm, 0)
    wait_whole(w_qkv, sems.at[0])
    project_in(x_norm, 0, length, w_qkv, vec, (q, k, v), (0, 0, 0))

    def pair(j, _):
        attend(j, q, k, v, probs, scores, mask, context, 0, length)

    lax.fori_loop(0, width // PAIR, pair, None)


def up_kernel(
    place_ref, context, vec, bias_up, entry, p0, p1, p2, p3, w_up, w_out, middle, x_mlp, active, slope, sems
):
    length = context.shape[0]
    fetch(place_ref, (p0, p1, p2, p3), (w_up, w_out), sems)
    wait_whole(w_out, sems.at[1])
    project_out(context, 0, length, w_out, vec, entry, middle)
    norm_forward(middle, 0, length, vec, GAIN_MLP, SHIFT_MLP, x_mlp, 0)
    wait_whole(w_up, sems.at[0])
    feed_up(x_mlp, 0, length, w_up, bias_up, active, slope, 0)


def down_half(place_ref, swapped, active_0, active, d_z, target):
    length = active_0.shape[0]
    width = target.shape[2]
    step = 2 * target.shape[1]
    half = pl.ds(half_start(place_ref, swapped, width), width)

    def some(j, _):
        c = cols(j, step)
        grad = tn(active_0[:, c], d_z[:length, half]) + tn(active[:, c], d_z[length:, half])
        put_blocks(place_ref, swapped, target, grad.astype(BF16), 2 * j, 0)

    lax.fori_loop(0, active_0.shape[1] // step, some, None, unroll=2)


def main_kernel(
    place_ref, cotangent, vec, bias_up, mask, w_qkv, w_out, w_up, k_0, v_0, middle_0, active_0, slope_0, p0, p1, p2, p3,
    output, state, g_vec, x_norm, context, x_mlp, active, d_hidden_0, d_hidden, d_z, d_y, d_mixed, k_grad_0, v_grad_0,
    w_down, q, k_all, v_all, probs_1, probs_2, entry, middle, k_grad, v_grad, extra, d_context, scores, d_scores, sems,
):
    probs = (None, probs_1, probs_2)
    length, width = state.shape
    inner = w_up.shape[1]
    pair_count = width // PAIR
    fetch(place_ref, (p0, p1, p2, p3), (w_down,), sems)
    g_vec[...] = jnp.zeros(g_vec.shape, F32)
    k_all[:length, :] = k_0[...]
    v_all[:length, :] = v_0[...]
    wait_whole(w_down, sems.at[0])
    feed_down(active_0, 0, length, w_down, vec, middle_0, 0, state)

    for r in range(1, PASSES):
        at, seen = (r - 1) * length, (r + 1) * length
        enter(state, r, vec, entry, at)
        norm_forward(entry, at, length, vec, GAIN_ATTN, SHIFT_ATTN, x_norm, at)
        project_in(x_norm, at, length, w_qkv, vec, (q, k_all, v_all), (at, r * length, r * length))

        def pair(j, _):
            attend(j, q, k_all, v_all, probs[r], scores, mask, context, at, seen)

        lax.fori_loop(0, pair_count, pair, None)
        project_out(context, at, length, w_out, vec, entry, middle)
        norm_forward(middle, at, length, vec, GAIN_MLP, SHIFT_MLP, x_mlp, at)
        feed_up(x_mlp, at, length, w_up, bias_up, active, d_hidden, at)
        feed_down(active, at, length, w_down, vec, middle, at, state)

    for b in range(0, length, 64):
        output[b : b + 64, :] = state[b : b + 64, :].astype(BF16)
        state[b : b + 64, :] = cotangent[b : b + 64, :].astype(F32)

    def through_down(r, slope, target, to):
        for b in range(0, length, 64):
            d_z[r * length + b : r * length + b + 64, :] = state[b : b + 64, :].astype(BF16)

        def step(j, _):
            c = cols(j, WIDE)
            acc = nt(d_z[r * length : (r + 1) * length, :], w_down[c, :])
            rows = pl.ds(to, length)
            target[rows, c] = (acc * slope[rows, c].astype(F32)).astype(BF16)

        lax.fori_loop(0, inner // WIDE, step, None, unroll=6)

    for r in reversed(range(1, PASSES)):
        at, seen = (r - 1) * length, (r + 1) * length
        mine = pl.ds(at, length)
        through_down(r, d_hidden, d_hidden, at)
        for c in range(0, width, WIDE):
            extra[:, c : c + WIDE] = nt(d_hidden[mine, :], w_up[c : c + WIDE, :])
        norm_backward(middle, at, extra, state, vec, GAIN_MLP, SHIFT_MLP, g_vec, d_y, at, None)
        for c in range(0, width, WIDE):
            d_context[:, c : c + WIDE] = nt(d_y[mine, :], w_out[c : c + WIDE, :]).astype(BF16)

        def pair_back(j, _):
            attend_back(
                j, q, k_all, v_all, probs[r], scores, d_scores, d_context, context, at, seen, d_mixed, k_grad, v_grad,
                r == PASSES - 1,
            )

        lax.fori_loop(0, pair_count, pair_back, None)
        for b in range(0, length, 64):
            part = slice(at + b, at + b + 64)
            made = slice(r * length + b, r * length + b + 64)
            d_mixed[part, width : 2 * width] = (k_grad[made, :] * SCALE).astype(BF16)
            d_mixed[part, 2 * width :] = v_grad[made, :].astype(BF16)
        for c in range(0, width, WIDE):
            extra[:, c : c + WIDE] = nt(d_mixed[mine, :], w_qkv[c : c + WIDE, :])
        norm_backward(entry, at, extra, state, vec, GAIN_ATTN, SHIFT_ATTN, g_vec, None, 0, EMBED + r)

    k_grad_0[...] = k_grad[:length, :]
    v_grad_0[...] = v_grad[:length, :]
    through_down(0, slope_0, d_hidden_0, 0)
    g_vec[BIAS_DOWN : BIAS_DOWN + 1, :] = nn(jnp.ones((16, PASSES * length), BF16), d_z[...])[:1]


def give_down_kernel(place_ref, active_0, active, d_z, give):
    down_half(place_ref, 1, active_0, active, d_z, give)


def keep_down_kernel(place_ref, active_0, active, d_z, keep):
    down_half(place_ref, 0, active_0, active, d_z, keep)


def up_half(place_ref, swapped, x_0, x, d_0, d, target, first_col, source_col, width):
    size = 384 if width % 384 == 0 else width
    start = half_start(place_ref, swapped, width)
    for c in range(0, width, size):
        part = pl.ds(pl.multiple_of(start + (source_col + c), 128), size)
        grad = tn(x_0[...], d_0[:, part]) + tn(x[...], d[:, part])
        put_blocks(place_ref, swapped, target, grad.astype(BF16), 0, first_col + c)


def give_up_kernel(
    place_ref, vec, w_up, w_out, x_mlp_0, x_mlp, d_hidden_0, d_hidden, middle_0, state_in, g_vec_in, context_0, context, d_y_1,
    give, state, g_vec, d_y, d_context,
    extra,
):
    width, inner = state.shape[1], w_up.shape[1]
    up_half(place_ref, 1, x_mlp_0, x_mlp, d_hidden_0, d_hidden, give, 0, 0, inner // 2)
    for c in range(0, width, WIDE):
        extra[:, c : c + WIDE] = nt(d_hidden_0[...], w_up[c : c + WIDE, :])
    state[...] = state_in[...]
    g_vec[...] = g_vec_in[...]
    norm_backward(middle_0, 0, extra, state, vec, GAIN_MLP, SHIFT_MLP, g_vec, d_y, 0, None)
    for c in range(0, width, WIDE):
        d_context[:, c : c + WIDE] = nt(d_y[...], w_out[c : c + WIDE, :]).astype(BF16)
    up_half(place_ref, 1, context_0, context, d_y, d_y_1, give, inner // 2, 0, width // 2)


def keep_up_kernel(
    place_ref, x_mlp_0, x_mlp, d_hidden_0, d_hidden, context_0, context, d_y_0, d_y, keep, g_bias_up
):
    width, inner = x_mlp.shape[1], d_hidden.shape[1]
    up_half(place_ref, 0, x_mlp_0, x_mlp, d_hidden_0, d_hidden, keep, 0, 0, inner // 2)
    up_half(place_ref, 0, context_0, context, d_y_0, d_y, keep, inner // 2, 0, width // 2)
    ones = jnp.ones((16, x_mlp.shape[0]), BF16)
    length = x_mlp_0.shape[0]

    def step(j, _):
        c = cols(j, 768)
        g_bias_up[:, c] = (nn(ones[:, :length], d_hidden_0[:, c]) + nn(ones, d_hidden[:, c]))[:1]

    lax.fori_loop(0, g_bias_up.shape[1] // 768, step, None)


def last_kernel(
    place_ref, vec, w_qkv, q, k, v, probs, context_0, d_context, d_y_0, d_y, d_mixed, entry, k_grad_0, v_grad_0, state_in,
    g_vec_in, g_bias_up,
    token_grad, d_mixed_0, small,
    k_grad, v_grad, state, g_vec, extra, scores, d_scores,
):
    length, width = state.shape
    k_grad[...] = k_grad_0[...]
    v_grad[...] = v_grad_0[...]
    state[...] = state_in[...]
    g_vec[...] = g_vec_in[...]

    def pair_back(j, _):
        attend_back(
            j, q, k, v, probs, scores, d_scores, d_context, context_0, 0, length, d_mixed_0, k_grad, v_grad, False
        )

    lax.fori_loop(0, width // PAIR, pair_back, None)
    for b in range(0, length, 64):
        part = slice(b, b + 64)
        d_mixed_0[part, width : 2 * width] = (k_grad[part, :] * SCALE).astype(BF16)
        d_mixed_0[part, 2 * width :] = v_grad[part, :].astype(BF16)
    for c in range(0, width, WIDE):
        extra[:, c : c + WIDE] = nt(d_mixed_0[...], w_qkv[c : c + WIDE, :])
    norm_backward(entry, 0, extra, state, vec, GAIN_ATTN, SHIFT_ATTN, g_vec, None, 0, EMBED)
    for b in range(0, length, 64):
        token_grad[b : b + 64, :] = state[b : b + 64, :].astype(BF16)

    ones = jnp.ones((16, 2 * length), BF16)

    def sums(d_0, d):
        return (nn(ones[:, :length], d_0) + nn(ones, d))[:1]

    g_vec[BIAS_Q : BIAS_Q + 1, :] = sums(d_mixed_0[:, :width], d_mixed[:, :width])
    g_vec[BIAS_V : BIAS_V + 1, :] = sums(d_mixed_0[:, 2 * width :], d_mixed[:, 2 * width :])
    g_vec[BIAS_OUT : BIAS_OUT + 1, :] = sums(d_y_0[...], d_y[...])
    vectors = g_vec[...].astype(BF16)
    four = []
    for b in range(g_bias_up.shape[1] // WIDE):
        four.append(jnp.where(own_lanes(), g_bias_up[:, b * WIDE : (b + 1) * WIDE], 0.0).astype(BF16))
    second = tn(vectors, pick_vectors(4 - EMBED, EMBED, EMBED + PASSES)) + nt(
        jnp.concatenate(four, axis=0), spread_four()
    )
    small[:, : SMALL // 2] = tn(vectors, pick_vectors(0, 0, EMBED)).astype(BF16)
    small[:, SMALL // 2 :] = second.astype(BF16)


def qkv_kernel(swapped, place_ref, x_norm_0, x_norm, d_mixed_0, d_mixed, small, target):
    wide = d_mixed.shape[1] // 2
    up_half(place_ref, swapped, x_norm_0, x_norm, d_mixed_0, d_mixed, target, 0, 0, wide)
    side = SMALL // 2
    put_blocks(place_ref, swapped, target, small[:, pl.ds(half_start(place_ref, swapped, side), side)], 0, wide)


def call(kernel, name, inputs, outputs, scratch, flops, touched):
    size = lambda shape, dtype: math.prod(shape) * jnp.dtype(dtype).itemsize
    need = sum(size(*s) for s in scratch if isinstance(s, tuple))
    results = [pltpu.VMEM(shape, dtype) if stays else jax.ShapeDtypeStruct(shape, dtype) for shape, dtype, stays in outputs]
    extra = sum(size(shape, dtype) for shape, dtype, stays in outputs if not stays)
    return pl.pallas_call(
        kernel,
        out_shape=results,
        in_specs=[pl.BlockSpec(memory_space=memory) for _, memory in inputs],
        out_specs=[pl.BlockSpec(memory_space=pltpu.VMEM)] * len(outputs),
        scratch_shapes=[pltpu.VMEM(*s) if isinstance(s, tuple) else s for s in scratch],
        compiler_params=pltpu.CompilerParams(vmem_limit_bytes=need + extra + 13 * 2**20),
        cost_estimate=pl.CostEstimate(flops=flops, bytes_accessed=touched, transcendentals=0),
        name=name,
    )(*[array for array, _ in inputs])


def layer(place, lengths, tokens, cotangent, chunks):
    length, width = tokens.shape
    inner = 16 * chunks[2][0].shape[2]
    rest = (PASSES - 1) * length
    heads = width // PAIR
    anywhere, local, scalars = pl.ANY, pltpu.VMEM, pltpu.SMEM
    place = (place, scalars)
    L = lambda *arrays: [(a, local) for a in arrays]

    G = lambda n: [(a, anywhere) for a in chunks[n]]
    low = lambda *shape: (shape, BF16)
    full = lambda *shape: (shape, F32)
    kept = lambda *specs: [(*s, True) for s in specs]
    out = lambda *specs: [(*s, False) for s in specs]
    semaphores = lambda n: pltpu.SemaphoreType.DMA((n,))
    row, row32 = low(length, width), full(length, width)
    part = 2 * length * width

    far_pieces(chunks[0])
    mate_pieces(chunks[0])
    far_pieces(chunks[1])
    w_qkv, vec, bias_up, mask, x_norm_0, q_0, k_0, v_0, probs_0, context_0, entry_0 = call(
        start_kernel, "start",
        [place, (lengths, scalars)] + L(tokens) + G(0),
        kept(
            low(width, 3 * width), full(VECTORS, width), full(1, inner), full(length, PASSES * length), row, row, row, row,
            low(heads, 2 * length, length), row, row32,
        ),
        [low(width, SMALL), full(2 * length, length), semaphores(2)],
        20 * 10**9, 70 * 2**20,
    )
    far_pieces(chunks[2])
    mate_pieces(chunks[1])
    w_up, w_out, middle_0, x_mlp_0, active_0, slope_0 = call(
        up_kernel, "up",
        [place] + L(context_0, vec, bias_up, entry_0) + G(1),
        kept(low(width, inner), low(width, width), row32, row, low(length, inner), low(length, inner)),
        [semaphores(2)],
        12 * 10**9, 40 * 2**20,
    )
    mate_pieces(chunks[2], context_0)
    (
        output, state, g_vec, x_norm, context, x_mlp, active, d_hidden_0, d_hidden, d_z, d_y, d_mixed, k_grad, v_grad,
    ) = call(
        main_kernel, "main",
        [place] + L(cotangent, vec, bias_up, mask, w_qkv, w_out, w_up, k_0, v_0, middle_0, active_0, slope_0) + G(2),
        out(row) + kept(
            row32, full(VECTORS, width), low(rest, width), low(rest, width), low(rest, width), low(rest, inner),
            low(length, inner), low(rest, inner), low(rest + length, width), low(rest, width), low(rest, 3 * width),
            row32, row32,
        ),
        [
            low(inner, width), low(rest, width), low(rest + length, width), low(rest + length, width),
            low(heads, 2 * length, 2 * length), low(heads, 2 * length, 3 * length), full(rest, width), full(rest, width),
            full(rest + length, width), full(rest + length, width), row32, row, full(2 * length, PASSES * length),
            low(2 * length, PASSES * length), semaphores(1),
        ],
        40 * part * inner, 60 * 2**20,
    )
    halves_ = []
    for kernel, name in ((give_down_kernel, "give_down"), (keep_down_kernel, "keep_down")):
        halves_ += call(
            kernel, name, [place] + L(active_0, active, after(d_z, *halves_)), kept(low(16, inner // 16, width // 2)), [],
            *COST,
        )
    begun = [begin_scatter(*halves_, MATE_WEIGHTS[0])]
    state = after(state, begun[0][0])
    begun[0] = far_step(begun[0])
    up_shape = low(16, width // 16, inner // 2 + width // 2)
    give_up, state, g_vec, d_y_0, d_context = call(
        give_up_kernel, "give_up",
        [place]
        + L(vec, w_up, w_out, x_mlp_0, x_mlp, d_hidden_0, d_hidden, middle_0, state, g_vec, context_0, context, d_y),
        kept(up_shape, row32, full(VECTORS, width), row, row), [row32],
        *COST,
    )
    keep_up, g_bias_up = call(
        keep_up_kernel, "keep_up",
        [place] + L(x_mlp_0, x_mlp, d_hidden_0, d_hidden, context_0, context, d_y_0, d_y),
        kept(up_shape, full(1, inner)), [],
        *COST,
    )
    begun.append(begin_scatter(give_up, keep_up, MATE_WEIGHTS[1]))
    state = after(state, begun[0][0])
    token_grad, d_mixed_0, g_small = call(
        last_kernel, "last",
        [place]
        + L(
            vec, w_qkv, q_0, k_0, v_0, probs_0, context_0, d_context, d_y_0, d_y, d_mixed, entry_0, k_grad, v_grad, state,
            g_vec, g_bias_up,
        ),
        out(row) + kept(low(length, 3 * width), low(width, SMALL)),
        [
            row32, row32, row32, full(VECTORS, width), row32, full(2 * length, length), low(2 * length, length),
        ],
        *COST,
    )
    begun[1] = far_step((after(begun[1][0], g_small), begun[1][1]))
    near_0 = near_step(begun[0], FAR_WEIGHTS[0])
    last_shape = low(16, width // 16, 3 * width // 2 + SMALL // 2)
    ends = []
    for name, swapped in (("give_qkv", 1), ("keep_qkv", 0)):
        earlier = ends if ends else near_0[:1]
        ends += call(
            functools.partial(qkv_kernel, swapped), name,
            [place] + L(x_norm_0, x_norm, d_mixed_0, d_mixed, after(g_small, *earlier)), kept(last_shape), [], *COST,
        )
    return output, token_grad, (near_0, begun[1], far_step(begin_scatter(*ends, MATE_WEIGHTS[2])))


def per_device(
    tokens,
    lengths,
    cotangent,
    w_qkv,
    bias_q,
    bias_v,
    w_out,
    bias_out,
    gain_attn,
    shift_attn,
    gain_mlp,
    shift_mlp,
    w_up,
    bias_up,
    w_down,
    bias_down,
    pass_embed,
):
    small = pack_small(
        [bias_q, bias_v, bias_out, gain_attn, shift_attn, gain_mlp, shift_mlp, bias_down], bias_up, pass_embed
    )
    place, chunks, last_z = gather_all(w_qkv, w_out, small, w_up, w_down)
    output, token_grad, parts = layer(place, lengths[0], tokens, cotangent, chunks)
    g_qkv, g_out, g_up, g_down, g_small = scatter_all(parts)
    (g_bq, g_bv, g_bo, g_ga, g_sa, g_gm, g_sm, g_bd), g_bu, g_pe = unpack_small(g_small)
    return (
        output,
        token_grad,
        g_qkv,
        g_bq,
        g_bv,
        g_out,
        g_bo,
        g_ga,
        g_sa,
        g_gm,
        g_sm,
        g_up,
        g_bu,
        g_down,
        g_bd,
        g_pe,
    )


def solution(mesh):
    placed = (
        P(("dp", "fsdp"), None),
        P(("dp", "fsdp"), None),
        P(("dp", "fsdp"), None),
        P(("dp", "fsdp"), None),
        P(("dp", "fsdp")),
        P(("dp", "fsdp")),
        P(("dp", "fsdp"), None),
        P(("dp", "fsdp")),
        P(("dp", "fsdp")),
        P(("dp", "fsdp")),
        P(("dp", "fsdp")),
        P(("dp", "fsdp")),
        P(("dp", "fsdp"), None),
        P(("dp", "fsdp")),
        P(("dp", "fsdp"), None),
        P(("dp", "fsdp")),
        P(None, ("dp", "fsdp")),
    )
    return jax.shard_map(
        per_device,
        mesh=mesh,
        in_specs=placed,
        out_specs=(
            P(("dp", "fsdp"), None),
            P(("dp", "fsdp"), None),
            P(("dp", "fsdp"), None),
            P(("dp", "fsdp")),
            P(("dp", "fsdp")),
            P(("dp", "fsdp"), None),
            P(("dp", "fsdp")),
            P(("dp", "fsdp")),
            P(("dp", "fsdp")),
            P(("dp", "fsdp")),
            P(("dp", "fsdp")),
            P(("dp", "fsdp"), None),
            P(("dp", "fsdp")),
            P(("dp", "fsdp"), None),
            P(("dp", "fsdp")),
            P(None, ("dp", "fsdp")),
        ),
        check_vma=False,
    )
```

```python
import functools
import math

import jax
import jax.numpy as jnp
from jax import lax
from jax.experimental import pallas as pl
from jax.experimental.pallas import tpu as pltpu
from jax.sharding import PartitionSpec as P

HEAD_DIM = 64
PASSES = 3
EPSILON = 1e-05
AXES = ("dp", "fsdp")
F32 = jnp.float32
BF16 = jnp.bfloat16


def pairs(partner):
    return [(i, partner(i)) for i in range(32)]


TO_MATE = pairs(lambda i: i ^ 1)
TO_Z = [pairs(lambda i, k=k: i ^ (8 * k)) for k in range(4)]
TO_NEAR = pairs(lambda i: i ^ (2 if i & 1 else 4))
TO_FAR = pairs(lambda i: i ^ (4 if i & 1 else 2))


def send(x, route):
    return lax.ppermute(x, AXES, route)


def after(x, *earlier):
    earlier = tuple(e for e in earlier if e is not None)
    return lax.optimization_barrier((x, earlier))[0] if earlier else x


def in_core_order(core, mine, other, axis):
    return jnp.where(
        core == 0,
        jnp.concatenate([mine, other], axis=axis),
        jnp.concatenate([other, mine], axis=axis),
    )


def stack_kernel(*refs):
    for n, ref in enumerate(refs[:-1]):
        refs[-1][n] = ref[...]


def stack_blocks(blocks, weight):
    if not weight:
        return jnp.stack(blocks)
    return pl.pallas_call(
        stack_kernel,
        out_shape=jax.ShapeDtypeStruct((len(blocks), *blocks[0].shape), BF16),
        in_specs=[pl.BlockSpec(memory_space=pltpu.VMEM)] * len(blocks),
        out_specs=pl.BlockSpec(memory_space=pltpu.VMEM),
        compiler_params=pltpu.CompilerParams(vmem_limit_bytes=8 * 2**20),
        cost_estimate=pl.CostEstimate(flops=weight * 10**9, bytes_accessed=weight * 35 * 10**5, transcendentals=0),
        name="stack",
    )(*blocks)


STACK_WEIGHTS = (0, 0, 10)
BOTH_WEIGHTS = (10, 0, 0)


def gather_chunks(blocks):
    chunks, earlier = [], None
    for n, block in enumerate(blocks):
        block = after(block, earlier)
        earlier = [send(block, TO_Z[k]) for k in (1, 2, 3)]
        stack = stack_blocks([block] + earlier, STACK_WEIGHTS[n])
        both = stack_blocks([stack, send(stack, TO_NEAR)], BOTH_WEIGHTS[n])
        chunks.append([both, None, send(both, TO_MATE), None])
    return chunks, earlier


def far_pieces(pieces, *earlier):
    if pieces[1] is None:
        pieces[1] = send(after(pieces[0], *earlier), TO_FAR)


def mate_pieces(pieces, *earlier):
    if pieces[3] is None:
        pieces[3] = send(after(pieces[1], *earlier), TO_MATE)


def chip_of(place, swapped, far, near, z):
    chip, core = place
    order = core ^ swapped
    near_bit = 2 - order
    far_bit = 1 + order
    return chip ^ (far * far_bit) ^ (near * near_bit) ^ (z * 4)


def add_low(a, b):
    return (a.astype(F32) + b.astype(F32)).astype(BF16)


def add_kernel(got, keep, give_out, keep_out):
    for n in range(got.shape[1]):
        give_out[n] = (keep[1, n].astype(F32) + got[1, n].astype(F32)).astype(BF16)
        keep_out[n] = (keep[0, n].astype(F32) + got[0, n].astype(F32)).astype(BF16)


def add_halves(got, keep, weight):
    if not weight:
        return add_low(keep[1], got[1]), add_low(keep[0], got[0])
    shape, merged = keep.shape[1:], (2, -1, keep.shape[-2], keep.shape[-1])
    got, keep = got.reshape(merged), keep.reshape(merged)
    give, keep = pl.pallas_call(
        add_kernel,
        out_shape=[jax.ShapeDtypeStruct(keep.shape[1:], BF16)] * 2,
        in_specs=[pl.BlockSpec(memory_space=pltpu.VMEM)] * 2,
        out_specs=[pl.BlockSpec(memory_space=pltpu.VMEM)] * 2,
        compiler_params=pltpu.CompilerParams(vmem_limit_bytes=8 * 2**20),
        cost_estimate=pl.CostEstimate(flops=weight * 10**9, bytes_accessed=weight * 35 * 10**5, transcendentals=0),
        name="add",
    )(got, keep)
    return give.reshape(shape), keep.reshape(shape)


def mate_step(give):
    return send(give, TO_MATE) if is_known_slice() else give


def begin_scatter(got, give, keep, weight):
    if not is_known_slice():
        return give, keep
    split = lambda a: a.reshape(2, 2, 4, *a.shape[1:])
    return add_halves(split(got), split(keep), weight)


def far_step(part):
    give, keep = part
    if not is_known_slice():
        return part
    return send(give, TO_FAR), keep


def near_step(part, weight):
    got, keep = part
    if not is_known_slice():
        return part
    give, keep = add_halves(got, keep, weight)
    return send(give, TO_NEAR), keep


def end_scatter(core, begun):
    begun = [begun[0]] + [near_step(begun[n], FAR_WEIGHTS[n]) for n in (1, 2)]
    results, earlier = [], None
    for n in range(len(begun)):
        near, keep = begun[n]
        z = [add_low(keep[k], near[k]) for k in (1, 2, 3)]
        z = [send(give, TO_Z[k + 1]) for k, give in enumerate(after(z, earlier))]
        earlier = z if n == 0 else None
        total = keep[0].astype(F32) + near[0].astype(F32)
        for part in z:
            total = total + part.astype(F32)
        total = total.reshape(2, total.shape[0] // 2, total.shape[1])
        mine = jnp.where(core == 0, total[0], total[1])
        other = send(jnp.where(core == 0, total[1], total[0]), TO_MATE)
        results.append((jnp.where(core == 0, mine, other), jnp.where(core == 0, other, mine)))
    return results


MATE_WEIGHTS = (0, 15, 0)
FAR_WEIGHTS = (0, 0, 0)
SMALL = 256


def pack_small(vectors, bias_up, pass_embed):
    rows = vectors[0].shape[0]
    first = jnp.stack(vectors, axis=1)
    second = jnp.concatenate([bias_up.reshape(rows, -1), pass_embed.T], axis=1)
    pad = lambda a: jnp.pad(a, ((0, 0), (0, SMALL // 2 - a.shape[1])))
    return jnp.concatenate([pad(first), pad(second)], axis=1)


def unpack_small(small):
    half = SMALL // 2
    vectors = [small[:, k] for k in range(8)]
    return vectors, small[:, half : half + 4].reshape(-1), small[:, half + 4 : half + 4 + PASSES].T


def is_known_slice():
    return lax.axis_size("dp") == 8 and lax.axis_size("fsdp") == 4


def place_of():
    if not is_known_slice():
        return jnp.zeros((2,), jnp.int32)
    index = lax.axis_index("dp") * 4 + lax.axis_index("fsdp")
    return jnp.stack([index >> 1, index & 1]).astype(jnp.int32)


def halves(*arrays):
    return [
        jnp.concatenate([a[:, h * (a.shape[1] // 2) : (h + 1) * (a.shape[1] // 2)] for a in arrays], axis=1)
        for h in range(2)
    ]


def slots(swapped):
    return [chip_of((0, 0), swapped, far, near, z) for far in range(2) for near in range(2) for z in range(4)]


def gather_all(w_qkv, w_out, small, w_up, w_down):
    place = place_of()
    groups = ((w_qkv, small), (w_up, w_out), (w_down,))
    if not is_known_slice():
        chunks = []
        for arrays in groups:
            whole = [lax.all_gather(a, AXES, axis=0, tiled=True) for a in arrays]
            pieces = []
            for swapped, part in enumerate(halves(*whole)):
                blocks = part.reshape(16, -1, part.shape[1])
                blocks = jnp.stack([blocks[chip] for chip in slots(swapped)])
                pieces += list(blocks.reshape(2, 2, 4, *blocks.shape[1:]))
            chunks.append(pieces)
        return place, chunks, ()
    core = place[1]
    blocks = []
    for arrays in groups:
        low, high = halves(*arrays)
        mine = jnp.where(core == 0, low, high)
        other = send(jnp.where(core == 0, high, low), TO_MATE)
        blocks.append(in_core_order(core, mine, other, 0))
    chunks, last_z = gather_chunks(blocks)
    return place, chunks, last_z


def scatter_all(parts):
    if is_known_slice():
        sums = end_scatter(place_of()[1], list(parts))
    else:
        sums = []
        for give, keep in parts:
            both = []
            for blocks, swapped in ((keep, 0), (give, 1)):
                order = slots(swapped)
                whole = jnp.concatenate([blocks[order.index(chip)] for chip in range(16)], axis=0)
                both.append(lax.psum_scatter(whole.astype(F32), AXES, scatter_dimension=0, tiled=True))
            sums.append(both)
    join = lambda n, first, width: jnp.concatenate([s[:, first : first + width] for s in sums[n]], axis=1)
    small_half = SMALL // 2
    qkv_half = sums[2][0].shape[1] - small_half
    out_half = qkv_half // 3
    up_half_ = sums[1][0].shape[1] - out_half
    return [
        join(2, 0, qkv_half),
        join(1, up_half_, out_half),
        join(1, 0, up_half_),
        join(0, 0, sums[0][0].shape[1]),
        join(2, qkv_half, small_half),
    ]


BIAS_Q, BIAS_V, BIAS_OUT, GAIN_ATTN, SHIFT_ATTN, GAIN_MLP, SHIFT_MLP, BIAS_DOWN, EMBED = range(9)
VECTORS = 16
PAIR = 2 * HEAD_DIM
SCALE = HEAD_DIM**-0.5
LOG2_E = 1.4426950408889634
GELU_A = 0.7978845608028654
GELU_B = 0.044715
LN_ROWS = 32
COST = (10 * 10**9, 35 * 2**20)
TINY = 1000
SOFT_ROWS = 64
WIDE = 256


def dot(a, b, a_dim, b_dim):
    return lax.dot_general(a, b, (((a_dim,), (b_dim,)), ((), ())), preferred_element_type=F32)


def nn(a, b):
    return dot(a, b, 1, 0)


def nt(a, b):
    return dot(a, b, 1, 1)


def tn(a, b):
    return dot(a, b, 0, 0)


def cols(n, size):
    return pl.ds(pl.multiple_of(n * size, size), size)


def row_mean(x):
    return jnp.sum(x, axis=1, keepdims=True) * (1.0 / x.shape[1])


def normalized(x):
    centred = x - row_mean(x)
    inverse = lax.rsqrt(row_mean(centred * centred) + EPSILON)
    return centred * inverse, inverse


def gelu_and_slope(v):
    square = v * v
    t = jnp.tanh(v * (GELU_A + (GELU_A * GELU_B) * square))
    half = 0.5 * (1.0 + t)
    slope = half + v * (1.0 - t * t) * (0.5 * GELU_A + (1.5 * GELU_A * GELU_B) * square)
    return v * half, slope


def iota(shape, dim):
    return lax.broadcasted_iota(jnp.int32, shape, dim)


def first_lanes():
    return iota((1, PAIR), 1) < HEAD_DIM


def stacked(x):
    low = first_lanes().astype(F32)
    return jnp.concatenate([x * low.astype(BF16), x * (1.0 - low).astype(BF16)], axis=0)


def unstacked(x):
    length = x.shape[0] // 2
    return jnp.where(first_lanes(), x[:length], x[length:])


def fetch(place_ref, pieces, targets, sems):
    place = (place_ref[0], place_ref[1])
    for source, swapped, far in zip(pieces, (0, 0, 1, 1), (0, 1, 0, 1)):
        half = place[1] ^ swapped
        rows = source.shape[2]
        for near in range(2):
            for z in range(4):
                chip = chip_of(place, swapped, far, near, z)
                first = 0
                for n, full in enumerate(targets):
                    width = full.shape[1] // 2
                    pltpu.make_async_copy(
                        source.at[near, z, :, pl.ds(first, width)],
                        full.at[
                            pl.ds(pl.multiple_of(chip * rows, 16), rows),
                            pl.ds(pl.multiple_of(half * width, 128), width),
                        ],
                        sems.at[n],
                    ).start()
                    first += width


def wait_whole(full, sem):
    pltpu.make_async_copy(full, full, sem).wait()


def slot_of(place_ref, swapped, chip):
    apart = chip ^ place_ref[0]
    order = place_ref[1] ^ swapped
    x, y = apart & 1, (apart >> 1) & 1
    far = x + order * (y - x)
    near = y + order * (x - y)
    return far * 8 + near * 4 + (apart >> 2)


def put_blocks(place_ref, swapped, target, value, first_chip, first_col):
    rows = target.shape[1]
    for n in range(value.shape[0] // rows):
        slot = slot_of(place_ref, swapped, first_chip + n)
        target[slot, :, first_col : first_col + value.shape[1]] = value[n * rows : (n + 1) * rows, :]


def half_start(place_ref, swapped, width):
    return pl.multiple_of((place_ref[1] ^ swapped) * width, 128)


def pick_vectors(offset, first, last):
    row, col = iota((VECTORS, SMALL // 2), 0), iota((VECTORS, SMALL // 2), 1)
    return ((col == row + offset) & (row >= first) & (row < last)).astype(F32).astype(BF16)


def spread_four():
    row, col = iota((SMALL // 2, WIDE), 0), iota((SMALL // 2, WIDE), 1)
    return ((row < 4) & ((col & 3) == row)).astype(F32).astype(BF16)


def own_lanes():
    return (iota((WIDE // 4, WIDE), 1) >> 2) == iota((WIDE // 4, WIDE), 0)


def norm_forward(source, at, length, vec, gain, shift, target, to):
    for b in range(0, length, LN_ROWS):
        n, _ = normalized(source[at + b : at + b + LN_ROWS, :])
        target[to + b : to + b + LN_ROWS, :] = (n * vec[gain : gain + 1, :] + vec[shift : shift + 1, :]).astype(BF16)


def norm_backward(source, at, extra, state, vec, gain, shift, g_vec, rounded, to, embed):
    for b in range(0, state.shape[0], LN_ROWS):
        part = slice(b, b + LN_ROWS)
        n, inverse = normalized(source[at + b : at + b + LN_ROWS, :])
        e = extra[part, :]
        g_vec[gain : gain + 1, :] += jnp.sum(e * n, axis=0, keepdims=True)
        g_vec[shift : shift + 1, :] += jnp.sum(e, axis=0, keepdims=True)
        eg = e * vec[gain : gain + 1, :]
        back = state[part, :] + inverse * (eg - row_mean(eg) - n * row_mean(eg * n))
        state[part, :] = back
        if rounded is not None:
            rounded[to + b : to + b + LN_ROWS, :] = back.astype(BF16)
        if embed is not None:
            g_vec[embed : embed + 1, :] += jnp.sum(back, axis=0, keepdims=True)


def attend(j, q, k, v, probs, scores, mask, context, at, seen):
    length = mask.shape[0]
    mine = pl.ds(at, length)
    c = cols(j, PAIR)
    scores[:, :seen] = nt(stacked(q[mine, c]), k[:seen, c])
    for b in range(0, 2 * length, SOFT_ROWS):
        part = slice(b, b + SOFT_ROWS)
        m = b % length
        s = scores[part, :seen] + mask[m : m + SOFT_ROWS, :seen]
        p = jnp.exp2((s - jnp.max(s, axis=1, keepdims=True)) * (SCALE * LOG2_E))
        p = p * (1.0 / jnp.sum(p, axis=1, keepdims=True))
        probs[j, part, :] = p.astype(BF16)
    context[mine, c] = unstacked(nn(probs[j], v[:seen, c])).astype(BF16)


def attend_back(j, q, k, v, probs, scores, d_scores, d_context, context, at, seen, d_query, k_grad, v_grad, fresh):
    length = d_context.shape[0]
    mine = pl.ds(at, length)
    c = cols(j, PAIR)
    dc = d_context[:, c]
    both = stacked(dc)
    scores[:, :seen] = nt(both, v[:seen, c])
    product = dc.astype(F32) * context[mine, c].astype(F32)
    inner_0 = jnp.sum(jnp.where(first_lanes(), product, 0.0), axis=1, keepdims=True)
    inner_1 = jnp.sum(jnp.where(first_lanes(), 0.0, product), axis=1, keepdims=True)
    for b in range(0, 2 * length, SOFT_ROWS):
        part = slice(b, b + SOFT_ROWS)
        m = b % length
        shift = (inner_0 if b < length else inner_1)[m : m + SOFT_ROWS]
        d_scores[part, :seen] = (probs[j, part, :].astype(F32) * (scores[part, :seen] - shift)).astype(BF16)
    ds = d_scores[:, :seen]
    d_query[mine, c] = (unstacked(nn(ds, k[:seen, c])) * SCALE).astype(BF16)
    k_more = tn(ds, stacked(q[mine, c]))
    v_more = tn(probs[j], both)
    if fresh:
        k_grad[:seen, c] = k_more
        v_grad[:seen, c] = v_more
    else:
        k_grad[:seen, c] += k_more
        v_grad[:seen, c] += v_more


def feed_up(x_mlp, at, length, w_up, bias_up, active, slope, to):
    def step(j, _):
        c = cols(j, WIDE)
        value, rise = gelu_and_slope(nn(x_mlp[pl.ds(at, length), :], w_up[:, c]) + bias_up[:, c])
        active[pl.ds(to, length), c] = value.astype(BF16)
        slope[pl.ds(to, length), c] = rise.astype(BF16)

    lax.fori_loop(0, w_up.shape[1] // WIDE, step, None, unroll=6)


def project_in(x_norm, at, length, w_qkv, vec, targets, to):
    width = w_qkv.shape[0]
    for part, (target, bias) in enumerate(zip(targets, (BIAS_Q, None, BIAS_V))):
        for c in range(0, width, WIDE):
            acc = nn(x_norm[at : at + length, :], w_qkv[:, part * width + c : part * width + c + WIDE])
            if bias is not None:
                acc = acc + vec[bias : bias + 1, c : c + WIDE]
            target[to[part] : to[part] + length, c : c + WIDE] = acc.astype(BF16)


def project_out(context, at, length, w_out, vec, entry, middle):
    for c in range(0, w_out.shape[1], WIDE):
        acc = nn(context[at : at + length, :], w_out[:, c : c + WIDE])
        middle[at : at + length, c : c + WIDE] = (
            entry[at : at + length, c : c + WIDE] + acc + vec[BIAS_OUT : BIAS_OUT + 1, c : c + WIDE]
        )


def feed_down(active, at, length, w_down, vec, middle, middle_at, state):
    for c in range(0, w_down.shape[1], WIDE):
        acc = nn(active[at : at + length, :], w_down[:, c : c + WIDE])
        state[:, c : c + WIDE] = (
            middle[middle_at : middle_at + length, c : c + WIDE] + acc + vec[BIAS_DOWN : BIAS_DOWN + 1, c : c + WIDE]
        )


def enter(state, r, vec, entry, at):
    for b in range(0, state.shape[0], LN_ROWS):
        entry[at + b : at + b + LN_ROWS, :] = state[b : b + LN_ROWS, :].astype(F32) + vec[EMBED + r : EMBED + r + 1, :]


def start_kernel(
    place_ref, lengths_ref, tokens, p0, p1, p2, p3,
    w_qkv, vec, bias_up, mask, x_norm, q, k, v, probs, context, entry,
    small, scores, sems,
):
    length, width = tokens.shape
    fetch(place_ref, (p0, p1, p2, p3), (w_qkv, small), sems)

    rows_at, keys_at = iota(mask.shape, 0), iota(mask.shape, 1)
    for _ in range(PASSES - 1):
        keys_at = jnp.where(keys_at >= length, keys_at - length, keys_at)
    same = keys_at <= rows_at
    end = 0
    for n in range(lengths_ref.shape[0]):
        end = end + lengths_ref[n]
        same = same & ((rows_at >= end) == (keys_at >= end))
    mask[...] = jnp.where(same, 0.0, -1e30)

    wait_whole(small, sems.at[1])
    side = SMALL // 2
    vec[...] = nt(pick_vectors(0, 0, EMBED), small[:, :side]) + nt(
        pick_vectors(4 - EMBED, EMBED, EMBED + PASSES), small[:, side:]
    )
    repeated = nn(small[:, side:], spread_four())
    for b in range(bias_up.shape[1] // WIDE):
        rows = repeated[b * (WIDE // 4) : (b + 1) * (WIDE // 4), :]
        bias_up[:, b * WIDE : (b + 1) * WIDE] = jnp.sum(jnp.where(own_lanes(), rows, 0.0), axis=0, keepdims=True)

    enter(tokens, 0, vec, entry, 0)
    norm_forward(entry, 0, length, vec, GAIN_ATTN, SHIFT_ATTN, x_norm, 0)
    wait_whole(w_qkv, sems.at[0])
    project_in(x_norm, 0, length, w_qkv, vec, (q, k, v), (0, 0, 0))

    def pair(j, _):
        attend(j, q, k, v, probs, scores, mask, context, 0, length)

    lax.fori_loop(0, width // PAIR, pair, None, unroll=2)


def up_kernel(
    place_ref, context, vec, bias_up, entry, p0, p1, p2, p3, w_up, w_out, middle, x_mlp, active, slope, sems
):
    length = context.shape[0]
    fetch(place_ref, (p0, p1, p2, p3), (w_up, w_out), sems)
    wait_whole(w_out, sems.at[1])
    project_out(context, 0, length, w_out, vec, entry, middle)
    norm_forward(middle, 0, length, vec, GAIN_MLP, SHIFT_MLP, x_mlp, 0)
    wait_whole(w_up, sems.at[0])
    feed_up(x_mlp, 0, length, w_up, bias_up, active, slope, 0)


def down_half(place_ref, swapped, active_0, active, d_z, target):
    length = active_0.shape[0]
    width = target.shape[2]
    step = 2 * target.shape[1]
    half = pl.ds(half_start(place_ref, swapped, width), width)

    def some(j, _):
        c = cols(j, step)
        grad = tn(active_0[:, c], d_z[:length, half]) + tn(active[:, c], d_z[length:, half])
        put_blocks(place_ref, swapped, target, grad.astype(BF16), 2 * j, 0)

    lax.fori_loop(0, active_0.shape[1] // step, some, None, unroll=2)


def main_kernel(
    place_ref, cotangent, vec, bias_up, mask, w_qkv, w_out, w_up, k_0, v_0, middle_0, active_0, slope_0, p0, p1, p2, p3,
    output, state, g_vec, x_norm, context, x_mlp, active, d_hidden_0, d_hidden, d_z, d_y, d_mixed, k_grad_0, v_grad_0,
    w_down, q, k_all, v_all, probs_1, probs_2, entry, middle, k_grad, v_grad, extra, d_context, scores, d_scores, sems,
):
    probs = (None, probs_1, probs_2)
    length, width = state.shape
    inner = w_up.shape[1]
    pair_count = width // PAIR
    fetch(place_ref, (p0, p1, p2, p3), (w_down,), sems)
    g_vec[...] = jnp.zeros(g_vec.shape, F32)
    k_all[:length, :] = k_0[...]
    v_all[:length, :] = v_0[...]
    wait_whole(w_down, sems.at[0])
    feed_down(active_0, 0, length, w_down, vec, middle_0, 0, state)

    for r in range(1, PASSES):
        at, seen = (r - 1) * length, (r + 1) * length
        enter(state, r, vec, entry, at)
        norm_forward(entry, at, length, vec, GAIN_ATTN, SHIFT_ATTN, x_norm, at)
        project_in(x_norm, at, length, w_qkv, vec, (q, k_all, v_all), (at, r * length, r * length))

        def pair(j, _):
            attend(j, q, k_all, v_all, probs[r], scores, mask, context, at, seen)

        lax.fori_loop(0, pair_count, pair, None, unroll=2)
        project_out(context, at, length, w_out, vec, entry, middle)
        norm_forward(middle, at, length, vec, GAIN_MLP, SHIFT_MLP, x_mlp, at)
        feed_up(x_mlp, at, length, w_up, bias_up, active, d_hidden, at)
        feed_down(active, at, length, w_down, vec, middle, at, state)

    for b in range(0, length, 64):
        output[b : b + 64, :] = state[b : b + 64, :].astype(BF16)
        state[b : b + 64, :] = cotangent[b : b + 64, :].astype(F32)

    def through_down(r, slope, target, to):
        for b in range(0, length, 64):
            d_z[r * length + b : r * length + b + 64, :] = state[b : b + 64, :].astype(BF16)

        def step(j, _):
            c = cols(j, WIDE)
            acc = nt(d_z[r * length : (r + 1) * length, :], w_down[c, :])
            rows = pl.ds(to, length)
            target[rows, c] = (acc * slope[rows, c].astype(F32)).astype(BF16)

        lax.fori_loop(0, inner // WIDE, step, None, unroll=6)

    for r in reversed(range(1, PASSES)):
        at, seen = (r - 1) * length, (r + 1) * length
        mine = pl.ds(at, length)
        through_down(r, d_hidden, d_hidden, at)
        for c in range(0, width, WIDE):
            extra[:, c : c + WIDE] = nt(d_hidden[mine, :], w_up[c : c + WIDE, :])
        norm_backward(middle, at, extra, state, vec, GAIN_MLP, SHIFT_MLP, g_vec, d_y, at, None)
        for c in range(0, width, WIDE):
            d_context[:, c : c + WIDE] = nt(d_y[mine, :], w_out[c : c + WIDE, :]).astype(BF16)

        def pair_back(j, _):
            attend_back(
                j, q, k_all, v_all, probs[r], scores, d_scores, d_context, context, at, seen, d_mixed, k_grad, v_grad,
                r == PASSES - 1,
            )

        lax.fori_loop(0, pair_count, pair_back, None, unroll=2)
        for b in range(0, length, 64):
            part = slice(at + b, at + b + 64)
            made = slice(r * length + b, r * length + b + 64)
            d_mixed[part, width : 2 * width] = (k_grad[made, :] * SCALE).astype(BF16)
            d_mixed[part, 2 * width :] = v_grad[made, :].astype(BF16)
        for c in range(0, width, WIDE):
            extra[:, c : c + WIDE] = nt(d_mixed[mine, :], w_qkv[c : c + WIDE, :])
        norm_backward(entry, at, extra, state, vec, GAIN_ATTN, SHIFT_ATTN, g_vec, None, 0, EMBED + r)

    k_grad_0[...] = k_grad[:length, :]
    v_grad_0[...] = v_grad[:length, :]
    through_down(0, slope_0, d_hidden_0, 0)
    g_vec[BIAS_DOWN : BIAS_DOWN + 1, :] = nn(jnp.ones((16, PASSES * length), BF16), d_z[...])[:1]


def give_down_kernel(place_ref, active_0, active, d_z, give):
    down_half(place_ref, 1, active_0, active, d_z, give)


def keep_down_kernel(place_ref, active_0, active, d_z, keep):
    down_half(place_ref, 0, active_0, active, d_z, keep)


def up_half(place_ref, swapped, x_0, x, d_0, d, target, first_col, source_col, width):
    size = 384 if width % 384 == 0 else width
    start = half_start(place_ref, swapped, width)
    for c in range(0, width, size):
        part = pl.ds(pl.multiple_of(start + (source_col + c), 128), size)
        grad = tn(x_0[...], d_0[:, part]) + tn(x[...], d[:, part])
        put_blocks(place_ref, swapped, target, grad.astype(BF16), 0, first_col + c)


def give_up_kernel(
    place_ref, vec, w_up, w_out, x_mlp_0, x_mlp, d_hidden_0, d_hidden, middle_0, state_in, g_vec_in, context_0, context, d_y_1,
    give, state, g_vec, d_y, d_context,
    extra,
):
    width, inner = state.shape[1], w_up.shape[1]
    up_half(place_ref, 1, x_mlp_0, x_mlp, d_hidden_0, d_hidden, give, 0, 0, inner // 2)
    for c in range(0, width, WIDE):
        extra[:, c : c + WIDE] = nt(d_hidden_0[...], w_up[c : c + WIDE, :])
    state[...] = state_in[...]
    g_vec[...] = g_vec_in[...]
    norm_backward(middle_0, 0, extra, state, vec, GAIN_MLP, SHIFT_MLP, g_vec, d_y, 0, None)
    for c in range(0, width, WIDE):
        d_context[:, c : c + WIDE] = nt(d_y[...], w_out[c : c + WIDE, :]).astype(BF16)
    up_half(place_ref, 1, context_0, context, d_y, d_y_1, give, inner // 2, 0, width // 2)


def keep_up_kernel(
    place_ref, x_mlp_0, x_mlp, d_hidden_0, d_hidden, context_0, context, d_y_0, d_y, keep, g_bias_up
):
    width, inner = x_mlp.shape[1], d_hidden.shape[1]
    up_half(place_ref, 0, x_mlp_0, x_mlp, d_hidden_0, d_hidden, keep, 0, 0, inner // 2)
    up_half(place_ref, 0, context_0, context, d_y_0, d_y, keep, inner // 2, 0, width // 2)
    ones = jnp.ones((16, x_mlp.shape[0]), BF16)
    length = x_mlp_0.shape[0]

    def step(j, _):
        c = cols(j, 768)
        g_bias_up[:, c] = (nn(ones[:, :length], d_hidden_0[:, c]) + nn(ones, d_hidden[:, c]))[:1]

    lax.fori_loop(0, g_bias_up.shape[1] // 768, step, None)


def last_kernel(
    place_ref, vec, w_qkv, q, k, v, probs, context_0, d_context, d_y_0, d_y, d_mixed, entry, k_grad_0, v_grad_0, state_in,
    g_vec_in, g_bias_up,
    token_grad, d_mixed_0, small,
    k_grad, v_grad, state, g_vec, extra, scores, d_scores,
):
    length, width = state.shape
    k_grad[...] = k_grad_0[...]
    v_grad[...] = v_grad_0[...]
    state[...] = state_in[...]
    g_vec[...] = g_vec_in[...]

    def pair_back(j, _):
        attend_back(
            j, q, k, v, probs, scores, d_scores, d_context, context_0, 0, length, d_mixed_0, k_grad, v_grad, False
        )

    lax.fori_loop(0, width // PAIR, pair_back, None, unroll=2)
    for b in range(0, length, 64):
        part = slice(b, b + 64)
        d_mixed_0[part, width : 2 * width] = (k_grad[part, :] * SCALE).astype(BF16)
        d_mixed_0[part, 2 * width :] = v_grad[part, :].astype(BF16)
    for c in range(0, width, WIDE):
        extra[:, c : c + WIDE] = nt(d_mixed_0[...], w_qkv[c : c + WIDE, :])
    norm_backward(entry, 0, extra, state, vec, GAIN_ATTN, SHIFT_ATTN, g_vec, None, 0, EMBED)
    for b in range(0, length, 64):
        token_grad[b : b + 64, :] = state[b : b + 64, :].astype(BF16)

    ones = jnp.ones((16, 2 * length), BF16)

    def sums(d_0, d):
        return (nn(ones[:, :length], d_0) + nn(ones, d))[:1]

    g_vec[BIAS_Q : BIAS_Q + 1, :] = sums(d_mixed_0[:, :width], d_mixed[:, :width])
    g_vec[BIAS_V : BIAS_V + 1, :] = sums(d_mixed_0[:, 2 * width :], d_mixed[:, 2 * width :])
    g_vec[BIAS_OUT : BIAS_OUT + 1, :] = sums(d_y_0[...], d_y[...])
    vectors = g_vec[...].astype(BF16)
    four = []
    for b in range(g_bias_up.shape[1] // WIDE):
        four.append(jnp.where(own_lanes(), g_bias_up[:, b * WIDE : (b + 1) * WIDE], 0.0).astype(BF16))
    second = tn(vectors, pick_vectors(4 - EMBED, EMBED, EMBED + PASSES)) + nt(
        jnp.concatenate(four, axis=0), spread_four()
    )
    small[:, : SMALL // 2] = tn(vectors, pick_vectors(0, 0, EMBED)).astype(BF16)
    small[:, SMALL // 2 :] = second.astype(BF16)


def qkv_kernel(swapped, place_ref, x_norm_0, x_norm, d_mixed_0, d_mixed, small, target):
    wide = d_mixed.shape[1] // 2
    up_half(place_ref, swapped, x_norm_0, x_norm, d_mixed_0, d_mixed, target, 0, 0, wide)
    side = SMALL // 2
    put_blocks(place_ref, swapped, target, small[:, pl.ds(half_start(place_ref, swapped, side), side)], 0, wide)


def call(kernel, name, inputs, outputs, scratch, flops, touched):
    size = lambda shape, dtype: math.prod(shape) * jnp.dtype(dtype).itemsize
    need = sum(size(*s) for s in scratch if isinstance(s, tuple))
    results = [pltpu.VMEM(shape, dtype) if stays else jax.ShapeDtypeStruct(shape, dtype) for shape, dtype, stays in outputs]
    extra = sum(size(shape, dtype) for shape, dtype, stays in outputs if not stays)
    return pl.pallas_call(
        kernel,
        out_shape=results,
        in_specs=[pl.BlockSpec(memory_space=memory) for _, memory in inputs],
        out_specs=[pl.BlockSpec(memory_space=pltpu.VMEM)] * len(outputs),
        scratch_shapes=[pltpu.VMEM(*s) if isinstance(s, tuple) else s for s in scratch],
        compiler_params=pltpu.CompilerParams(vmem_limit_bytes=need + extra + 4 * 2**20),
        cost_estimate=pl.CostEstimate(flops=flops, bytes_accessed=touched, transcendentals=0),
        name=name,
    )(*[array for array, _ in inputs])


def layer(place, lengths, tokens, cotangent, chunks):
    length, width = tokens.shape
    inner = 16 * chunks[2][0].shape[2]
    rest = (PASSES - 1) * length
    heads = width // PAIR
    anywhere, local, scalars = pl.ANY, pltpu.VMEM, pltpu.SMEM
    place = (place, scalars)
    L = lambda *arrays: [(a, local) for a in arrays]

    G = lambda n: [(a, anywhere) for a in chunks[n]]
    low = lambda *shape: (shape, BF16)
    full = lambda *shape: (shape, F32)
    kept = lambda *specs: [(*s, True) for s in specs]
    out = lambda *specs: [(*s, False) for s in specs]
    semaphores = lambda n: pltpu.SemaphoreType.DMA((n,))
    row, row32 = low(length, width), full(length, width)
    part = 2 * length * width

    far_pieces(chunks[0])
    mate_pieces(chunks[0])
    far_pieces(chunks[1])
    w_qkv, vec, bias_up, mask, x_norm_0, q_0, k_0, v_0, probs_0, context_0, entry_0 = call(
        start_kernel, "start",
        [place, (lengths, scalars)] + L(tokens) + G(0),
        kept(
            low(width, 3 * width), full(VECTORS, width), full(1, inner), full(length, PASSES * length), row, row, row, row,
            low(heads, 2 * length, length), row, row32,
        ),
        [low(width, SMALL), full(2 * length, length), semaphores(2)],
        20 * 10**9, 70 * 2**20,
    )
    far_pieces(chunks[2])
    mate_pieces(chunks[1])
    w_up, w_out, middle_0, x_mlp_0, active_0, slope_0 = call(
        up_kernel, "up",
        [place] + L(context_0, vec, bias_up, entry_0) + G(1),
        kept(low(width, inner), low(width, width), row32, row, low(length, inner), low(length, inner)),
        [semaphores(2)],
        12 * 10**9, 40 * 2**20,
    )
    mate_pieces(chunks[2], context_0)
    (
        output, state, g_vec, x_norm, context, x_mlp, active, d_hidden_0, d_hidden, d_z, d_y, d_mixed, k_grad, v_grad,
    ) = call(
        main_kernel, "main",
        [place] + L(cotangent, vec, bias_up, mask, w_qkv, w_out, w_up, k_0, v_0, middle_0, active_0, slope_0) + G(2),
        out(row) + kept(
            row32, full(VECTORS, width), low(rest, width), low(rest, width), low(rest, width), low(rest, inner),
            low(length, inner), low(rest, inner), low(rest + length, width), low(rest, width), low(rest, 3 * width),
            row32, row32,
        ),
        [
            low(inner, width), low(rest, width), low(rest + length, width), low(rest + length, width),
            low(heads, 2 * length, 2 * length), low(heads, 2 * length, 3 * length), full(rest, width), full(rest, width),
            full(rest + length, width), full(rest + length, width), row32, row, full(2 * length, PASSES * length),
            low(2 * length, PASSES * length), semaphores(1),
        ],
        40 * part * inner, 60 * 2**20,
    )
    halves_ = []
    for kernel, name in ((give_down_kernel, "give_down"), (keep_down_kernel, "keep_down")):
        halves_ += call(
            kernel, name, [place] + L(active_0, active, after(d_z, *halves_)), kept(low(16, inner // 16, width // 2)), [],
            *COST,
        )
    begun = [begin_scatter(mate_step(halves_[0]), *halves_, MATE_WEIGHTS[0])]
    state = after(state, begun[0][0])
    begun[0] = far_step(begun[0])
    up_shape = low(16, width // 16, inner // 2 + width // 2)
    give_up, state, g_vec, d_y_0, d_context = call(
        give_up_kernel, "give_up",
        [place]
        + L(vec, w_up, w_out, x_mlp_0, x_mlp, d_hidden_0, d_hidden, middle_0, state, g_vec, context_0, context, d_y),
        kept(up_shape, row32, full(VECTORS, width), row, row), [row32],
        *COST,
    )
    keep_up, g_bias_up = call(
        keep_up_kernel, "keep_up",
        [place] + L(x_mlp_0, x_mlp, d_hidden_0, d_hidden, context_0, context, d_y_0, d_y),
        kept(up_shape, full(1, inner)), [],
        *COST,
    )
    up_got = mate_step(give_up)
    state = after(state, begun[0][0])
    token_grad, d_mixed_0, g_small = call(
        last_kernel, "last",
        [place]
        + L(
            vec, w_qkv, q_0, k_0, v_0, probs_0, context_0, d_context, d_y_0, d_y, d_mixed, entry_0, k_grad, v_grad, state,
            g_vec, g_bias_up,
        ),
        out(row) + kept(low(length, 3 * width), low(width, SMALL)),
        [
            row32, row32, row32, full(VECTORS, width), row32, full(2 * length, length), low(2 * length, length),
        ],
        40 * 10**9, 140 * 2**20,
    )
    begun.append(begin_scatter(after(up_got, g_small), give_up, keep_up, MATE_WEIGHTS[1]))
    g_small = after(g_small, begun[1][0])
    begun[1] = far_step(begun[1])
    near_0 = near_step(begun[0], FAR_WEIGHTS[0])
    last_shape = low(16, width // 16, 3 * width // 2 + SMALL // 2)
    ends = []
    for name, swapped in (("give_qkv", 1), ("keep_qkv", 0)):
        earlier = ends if ends else near_0[:1]
        ends += call(
            functools.partial(qkv_kernel, swapped), name,
            [place] + L(x_norm_0, x_norm, d_mixed_0, d_mixed, after(g_small, *earlier)), kept(last_shape), [], TINY, TINY,
        )
    near_0 = (near_0[0], after(near_0[1], ends[1]))
    return output, token_grad, (near_0, begun[1], far_step(begin_scatter(mate_step(ends[0]), *ends, MATE_WEIGHTS[2])))


def per_device(
    tokens,
    lengths,
    cotangent,
    w_qkv,
    bias_q,
    bias_v,
    w_out,
    bias_out,
    gain_attn,
    shift_attn,
    gain_mlp,
    shift_mlp,
    w_up,
    bias_up,
    w_down,
    bias_down,
    pass_embed,
):
    small = pack_small(
        [bias_q, bias_v, bias_out, gain_attn, shift_attn, gain_mlp, shift_mlp, bias_down], bias_up, pass_embed
    )
    place, chunks, last_z = gather_all(w_qkv, w_out, small, w_up, w_down)
    output, token_grad, parts = layer(place, lengths[0], tokens, cotangent, chunks)
    g_qkv, g_out, g_up, g_down, g_small = scatter_all(parts)
    (g_bq, g_bv, g_bo, g_ga, g_sa, g_gm, g_sm, g_bd), g_bu, g_pe = unpack_small(g_small)
    return (
        output,
        token_grad,
        g_qkv,
        g_bq,
        g_bv,
        g_out,
        g_bo,
        g_ga,
        g_sa,
        g_gm,
        g_sm,
        g_up,
        g_bu,
        g_down,
        g_bd,
        g_pe,
    )


def solution(mesh):
    placed = (
        P(("dp", "fsdp"), None),
        P(("dp", "fsdp"), None),
        P(("dp", "fsdp"), None),
        P(("dp", "fsdp"), None),
        P(("dp", "fsdp")),
        P(("dp", "fsdp")),
        P(("dp", "fsdp"), None),
        P(("dp", "fsdp")),
        P(("dp", "fsdp")),
        P(("dp", "fsdp")),
        P(("dp", "fsdp")),
        P(("dp", "fsdp")),
        P(("dp", "fsdp"), None),
        P(("dp", "fsdp")),
        P(("dp", "fsdp"), None),
        P(("dp", "fsdp")),
        P(None, ("dp", "fsdp")),
    )
    return jax.shard_map(
        per_device,
        mesh=mesh,
        in_specs=placed,
        out_specs=(
            P(("dp", "fsdp"), None),
            P(("dp", "fsdp"), None),
            P(("dp", "fsdp"), None),
            P(("dp", "fsdp")),
            P(("dp", "fsdp")),
            P(("dp", "fsdp"), None),
            P(("dp", "fsdp")),
            P(("dp", "fsdp")),
            P(("dp", "fsdp")),
            P(("dp", "fsdp")),
            P(("dp", "fsdp")),
            P(("dp", "fsdp"), None),
            P(("dp", "fsdp")),
            P(("dp", "fsdp"), None),
            P(("dp", "fsdp")),
            P(None, ("dp", "fsdp")),
        ),
        check_vma=False,
    )
```

```python
import functools
import math

import jax
import jax.numpy as jnp
from jax import lax
from jax.experimental import pallas as pl
from jax.experimental.pallas import tpu as pltpu
from jax.sharding import PartitionSpec as P

HEAD_DIM = 64
PASSES = 3
EPSILON = 1e-05
AXES = ("dp", "fsdp")
F32 = jnp.float32
BF16 = jnp.bfloat16


def pairs(partner):
    return [(i, partner(i)) for i in range(32)]


TO_MATE = pairs(lambda i: i ^ 1)
TO_Z = [pairs(lambda i, k=k: i ^ (8 * k)) for k in range(4)]
TO_NEAR = pairs(lambda i: i ^ (2 if i & 1 else 4))
TO_FAR = pairs(lambda i: i ^ (4 if i & 1 else 2))


def send(x, route):
    return lax.ppermute(x, AXES, route)


def after(x, *earlier):
    earlier = tuple(e for e in earlier if e is not None)
    return lax.optimization_barrier((x, earlier))[0] if earlier else x


def in_core_order(core, mine, other, axis):
    return jnp.where(
        core == 0,
        jnp.concatenate([mine, other], axis=axis),
        jnp.concatenate([other, mine], axis=axis),
    )


def stack_kernel(*refs):
    for n, ref in enumerate(refs[:-1]):
        refs[-1][n] = ref[...]


def stack_blocks(blocks, weight):
    if not weight:
        return jnp.stack(blocks)
    return pl.pallas_call(
        stack_kernel,
        out_shape=jax.ShapeDtypeStruct((len(blocks), *blocks[0].shape), BF16),
        in_specs=[pl.BlockSpec(memory_space=pltpu.VMEM)] * len(blocks),
        out_specs=pl.BlockSpec(memory_space=pltpu.VMEM),
        compiler_params=pltpu.CompilerParams(vmem_limit_bytes=8 * 2**20),
        cost_estimate=pl.CostEstimate(flops=weight * 10**9, bytes_accessed=weight * 35 * 10**5, transcendentals=0),
        name="stack",
    )(*blocks)


STACK_WEIGHTS = (0, 0, 10)
BOTH_WEIGHTS = (10, 0, 0)


def gather_chunks(blocks):
    chunks, earlier = [], None
    for n, block in enumerate(blocks):
        block = after(block, earlier)
        earlier = [send(block, TO_Z[k]) for k in (1, 2, 3)]
        stack = stack_blocks([block] + earlier, STACK_WEIGHTS[n])
        both = stack_blocks([stack, send(stack, TO_NEAR)], BOTH_WEIGHTS[n])
        chunks.append([both, None, send(both, TO_MATE), None])
    return chunks, earlier


def far_pieces(pieces, *earlier):
    if pieces[1] is None:
        pieces[1] = send(after(pieces[0], *earlier), TO_FAR)


def mate_pieces(pieces, *earlier):
    if pieces[3] is None:
        pieces[3] = send(after(pieces[1], *earlier), TO_MATE)


def chip_of(place, swapped, far, near, z):
    chip, core = place
    order = core ^ swapped
    near_bit = 2 - order
    far_bit = 1 + order
    return chip ^ (far * far_bit) ^ (near * near_bit) ^ (z * 4)


def add_low(a, b):
    return (a.astype(F32) + b.astype(F32)).astype(BF16)


def add_kernel(got, keep, give_out, keep_out):
    for n in range(got.shape[1]):
        give_out[n] = (keep[1, n].astype(F32) + got[1, n].astype(F32)).astype(BF16)
        keep_out[n] = (keep[0, n].astype(F32) + got[0, n].astype(F32)).astype(BF16)


def add_halves(got, keep, weight):
    if not weight:
        return add_low(keep[1], got[1]), add_low(keep[0], got[0])
    shape, merged = keep.shape[1:], (2, -1, keep.shape[-2], keep.shape[-1])
    got, keep = got.reshape(merged), keep.reshape(merged)
    give, keep = pl.pallas_call(
        add_kernel,
        out_shape=[jax.ShapeDtypeStruct(keep.shape[1:], BF16)] * 2,
        in_specs=[pl.BlockSpec(memory_space=pltpu.VMEM)] * 2,
        out_specs=[pl.BlockSpec(memory_space=pltpu.VMEM)] * 2,
        compiler_params=pltpu.CompilerParams(vmem_limit_bytes=8 * 2**20),
        cost_estimate=pl.CostEstimate(flops=weight * 10**9, bytes_accessed=weight * 35 * 10**5, transcendentals=0),
        name="add",
    )(got, keep)
    return give.reshape(shape), keep.reshape(shape)


def mate_step(give):
    return send(give, TO_MATE) if is_known_slice() else give


def begin_scatter(got, give, keep, weight):
    if not is_known_slice():
        return give, keep
    split = lambda a: a.reshape(2, 2, 4, *a.shape[1:])
    return add_halves(split(got), split(keep), weight)


def far_step(part):
    give, keep = part
    if not is_known_slice():
        return part
    return send(give, TO_FAR), keep


def near_step(part, weight):
    got, keep = part
    if not is_known_slice():
        return part
    give, keep = add_halves(got, keep, weight)
    return send(give, TO_NEAR), keep


def end_scatter(core, begun):
    begun = [(begun[0][0], after(begun[0][1], begun[1][0]))] + [near_step(begun[n], FAR_WEIGHTS[n]) for n in (1, 2)]
    results, earlier = [], None
    for n in range(len(begun)):
        near, keep = begun[n]
        z = [add_low(keep[k], near[k]) for k in (1, 2, 3)]
        z = [send(give, TO_Z[k + 1]) for k, give in enumerate(after(z, earlier))]
        earlier = z if n == 0 else None
        total = keep[0].astype(F32) + near[0].astype(F32)
        for part in z:
            total = total + part.astype(F32)
        total = total.reshape(2, total.shape[0] // 2, total.shape[1])
        mine = jnp.where(core == 0, total[0], total[1])
        theirs = jnp.where(core == 0, total[1], total[0])
        if n == 0:
            theirs = after(theirs, begun[1][0])
        other = send(theirs, TO_MATE)
        results.append((jnp.where(core == 0, mine, other), jnp.where(core == 0, other, mine)))
    return results


MATE_WEIGHTS = (0, 15, 0)
FAR_WEIGHTS = (40, 0, 0)
SMALL = 256


def pack_small(vectors, bias_up, pass_embed):
    rows = vectors[0].shape[0]
    first = jnp.stack(vectors, axis=1)
    second = jnp.concatenate([bias_up.reshape(rows, -1), pass_embed.T], axis=1)
    pad = lambda a: jnp.pad(a, ((0, 0), (0, SMALL // 2 - a.shape[1])))
    return jnp.concatenate([pad(first), pad(second)], axis=1)


def unpack_small(small):
    half = SMALL // 2
    vectors = [small[:, k] for k in range(8)]
    return vectors, small[:, half : half + 4].reshape(-1), small[:, half + 4 : half + 4 + PASSES].T


def is_known_slice():
    return lax.axis_size("dp") == 8 and lax.axis_size("fsdp") == 4


def place_of():
    if not is_known_slice():
        return jnp.zeros((2,), jnp.int32)
    index = lax.axis_index("dp") * 4 + lax.axis_index("fsdp")
    return jnp.stack([index >> 1, index & 1]).astype(jnp.int32)


def halves(*arrays):
    return [
        jnp.concatenate([a[:, h * (a.shape[1] // 2) : (h + 1) * (a.shape[1] // 2)] for a in arrays], axis=1)
        for h in range(2)
    ]


def slots(swapped):
    return [chip_of((0, 0), swapped, far, near, z) for far in range(2) for near in range(2) for z in range(4)]


def gather_all(w_qkv, w_out, small, w_up, w_down):
    place = place_of()
    groups = ((w_qkv, small), (w_up, w_out), (w_down,))
    if not is_known_slice():
        chunks = []
        for arrays in groups:
            whole = [lax.all_gather(a, AXES, axis=0, tiled=True) for a in arrays]
            pieces = []
            for swapped, part in enumerate(halves(*whole)):
                blocks = part.reshape(16, -1, part.shape[1])
                blocks = jnp.stack([blocks[chip] for chip in slots(swapped)])
                pieces += list(blocks.reshape(2, 2, 4, *blocks.shape[1:]))
            chunks.append(pieces)
        return place, chunks, ()
    core = place[1]
    blocks = []
    for arrays in groups:
        low, high = halves(*arrays)
        mine = jnp.where(core == 0, low, high)
        other = send(jnp.where(core == 0, high, low), TO_MATE)
        blocks.append(in_core_order(core, mine, other, 0))
    chunks, last_z = gather_chunks(blocks)
    return place, chunks, last_z


def scatter_all(parts):
    if is_known_slice():
        sums = end_scatter(place_of()[1], list(parts))
    else:
        sums = []
        for give, keep in parts:
            both = []
            for blocks, swapped in ((keep, 0), (give, 1)):
                order = slots(swapped)
                whole = jnp.concatenate([blocks[order.index(chip)] for chip in range(16)], axis=0)
                both.append(lax.psum_scatter(whole.astype(F32), AXES, scatter_dimension=0, tiled=True))
            sums.append(both)
    join = lambda n, first, width: jnp.concatenate([s[:, first : first + width] for s in sums[n]], axis=1)
    small_half = SMALL // 2
    qkv_half = sums[2][0].shape[1] - small_half
    out_half = qkv_half // 3
    up_half_ = sums[1][0].shape[1] - out_half
    return [
        join(2, 0, qkv_half),
        join(1, up_half_, out_half),
        join(1, 0, up_half_),
        join(0, 0, sums[0][0].shape[1]),
        join(2, qkv_half, small_half),
    ]


BIAS_Q, BIAS_V, BIAS_OUT, GAIN_ATTN, SHIFT_ATTN, GAIN_MLP, SHIFT_MLP, BIAS_DOWN, EMBED = range(9)
VECTORS = 16
PAIR = 2 * HEAD_DIM
SCALE = HEAD_DIM**-0.5
LOG2_E = 1.4426950408889634
GELU_A = 0.7978845608028654
GELU_B = 0.044715
LN_ROWS = 32
COST = (10 * 10**9, 35 * 2**20)
TINY = 1000
SOFT_ROWS = 64
WIDE = 256


def dot(a, b, a_dim, b_dim):
    return lax.dot_general(a, b, (((a_dim,), (b_dim,)), ((), ())), preferred_element_type=F32)


def nn(a, b):
    return dot(a, b, 1, 0)


def nt(a, b):
    return dot(a, b, 1, 1)


def tn(a, b):
    return dot(a, b, 0, 0)


def cols(n, size):
    return pl.ds(pl.multiple_of(n * size, size), size)


def row_mean(x):
    return jnp.sum(x, axis=1, keepdims=True) * (1.0 / x.shape[1])


def normalized(x):
    centred = x - row_mean(x)
    inverse = lax.rsqrt(row_mean(centred * centred) + EPSILON)
    return centred * inverse, inverse


def gelu_and_slope(v):
    square = v * v
    t = jnp.tanh(v * (GELU_A + (GELU_A * GELU_B) * square))
    half = 0.5 * (1.0 + t)
    slope = half + v * (1.0 - t * t) * (0.5 * GELU_A + (1.5 * GELU_A * GELU_B) * square)
    return v * half, slope


def iota(shape, dim):
    return lax.broadcasted_iota(jnp.int32, shape, dim)


def first_lanes():
    return iota((1, PAIR), 1) < HEAD_DIM


def stacked(x):
    low = first_lanes().astype(F32)
    return jnp.concatenate([x * low.astype(BF16), x * (1.0 - low).astype(BF16)], axis=0)


def unstacked(x):
    length = x.shape[0] // 2
    return jnp.where(first_lanes(), x[:length], x[length:])


def fetch(place_ref, pieces, targets, sems):
    place = (place_ref[0], place_ref[1])
    for source, swapped, far in zip(pieces, (0, 0, 1, 1), (0, 1, 0, 1)):
        half = place[1] ^ swapped
        rows = source.shape[2]
        for near in range(2):
            for z in range(4):
                chip = chip_of(place, swapped, far, near, z)
                first = 0
                for n, full in enumerate(targets):
                    width = full.shape[1] // 2
                    pltpu.make_async_copy(
                        source.at[near, z, :, pl.ds(first, width)],
                        full.at[
                            pl.ds(pl.multiple_of(chip * rows, 16), rows),
                            pl.ds(pl.multiple_of(half * width, 128), width),
                        ],
                        sems.at[n],
                    ).start()
                    first += width


def wait_whole(full, sem):
    pltpu.make_async_copy(full, full, sem).wait()


def slot_of(place_ref, swapped, chip):
    apart = chip ^ place_ref[0]
    order = place_ref[1] ^ swapped
    x, y = apart & 1, (apart >> 1) & 1
    far = x + order * (y - x)
    near = y + order * (x - y)
    return far * 8 + near * 4 + (apart >> 2)


def put_blocks(place_ref, swapped, target, value, first_chip, first_col):
    rows = target.shape[1]
    for n in range(value.shape[0] // rows):
        slot = slot_of(place_ref, swapped, first_chip + n)
        target[slot, :, first_col : first_col + value.shape[1]] = value[n * rows : (n + 1) * rows, :]


def half_start(place_ref, swapped, width):
    return pl.multiple_of((place_ref[1] ^ swapped) * width, 128)


def pick_vectors(offset, first, last):
    row, col = iota((VECTORS, SMALL // 2), 0), iota((VECTORS, SMALL // 2), 1)
    return ((col == row + offset) & (row >= first) & (row < last)).astype(F32).astype(BF16)


def spread_four():
    row, col = iota((SMALL // 2, WIDE), 0), iota((SMALL // 2, WIDE), 1)
    return ((row < 4) & ((col & 3) == row)).astype(F32).astype(BF16)


def own_lanes():
    return (iota((WIDE // 4, WIDE), 1) >> 2) == iota((WIDE // 4, WIDE), 0)


def norm_forward(source, at, length, vec, gain, shift, target, to):
    for b in range(0, length, LN_ROWS):
        n, _ = normalized(source[at + b : at + b + LN_ROWS, :])
        target[to + b : to + b + LN_ROWS, :] = (n * vec[gain : gain + 1, :] + vec[shift : shift + 1, :]).astype(BF16)


def norm_backward(source, at, extra, state, vec, gain, shift, g_vec, rounded, to, embed):
    for b in range(0, state.shape[0], LN_ROWS):
        part = slice(b, b + LN_ROWS)
        n, inverse = normalized(source[at + b : at + b + LN_ROWS, :])
        e = extra[part, :]
        g_vec[gain : gain + 1, :] += jnp.sum(e * n, axis=0, keepdims=True)
        g_vec[shift : shift + 1, :] += jnp.sum(e, axis=0, keepdims=True)
        eg = e * vec[gain : gain + 1, :]
        back = state[part, :] + inverse * (eg - row_mean(eg) - n * row_mean(eg * n))
        state[part, :] = back
        if rounded is not None:
            rounded[to + b : to + b + LN_ROWS, :] = back.astype(BF16)
        if embed is not None:
            g_vec[embed : embed + 1, :] += jnp.sum(back, axis=0, keepdims=True)


def attend(j, q, k, v, probs, scores, mask, context, at, seen):
    length = mask.shape[0]
    mine = pl.ds(at, length)
    c = cols(j, PAIR)
    scores[:, :seen] = nt(stacked(q[mine, c]), k[:seen, c])
    for b in range(0, 2 * length, SOFT_ROWS):
        part = slice(b, b + SOFT_ROWS)
        m = b % length
        s = scores[part, :seen] + mask[m : m + SOFT_ROWS, :seen]
        p = jnp.exp2((s - jnp.max(s, axis=1, keepdims=True)) * (SCALE * LOG2_E))
        p = p * (1.0 / jnp.sum(p, axis=1, keepdims=True))
        probs[j, part, :] = p.astype(BF16)
    context[mine, c] = unstacked(nn(probs[j], v[:seen, c])).astype(BF16)


def attend_back(j, q, k, v, probs, scores, d_scores, d_context, context, at, seen, d_query, k_grad, v_grad, fresh):
    length = d_context.shape[0]
    mine = pl.ds(at, length)
    c = cols(j, PAIR)
    dc = d_context[:, c]
    both = stacked(dc)
    scores[:, :seen] = nt(both, v[:seen, c])
    product = dc.astype(F32) * context[mine, c].astype(F32)
    inner_0 = jnp.sum(jnp.where(first_lanes(), product, 0.0), axis=1, keepdims=True)
    inner_1 = jnp.sum(jnp.where(first_lanes(), 0.0, product), axis=1, keepdims=True)
    for b in range(0, 2 * length, SOFT_ROWS):
        part = slice(b, b + SOFT_ROWS)
        m = b % length
        shift = (inner_0 if b < length else inner_1)[m : m + SOFT_ROWS]
        d_scores[part, :seen] = (probs[j, part, :].astype(F32) * (scores[part, :seen] - shift)).astype(BF16)
    ds = d_scores[:, :seen]
    d_query[mine, c] = (unstacked(nn(ds, k[:seen, c])) * SCALE).astype(BF16)
    k_more = tn(ds, stacked(q[mine, c]))
    v_more = tn(probs[j], both)
    if fresh:
        k_grad[:seen, c] = k_more
        v_grad[:seen, c] = v_more
    else:
        k_grad[:seen, c] += k_more
        v_grad[:seen, c] += v_more


def feed_up(x_mlp, at, length, w_up, bias_up, active, slope, to):
    def step(j, _):
        c = cols(j, WIDE)
        value, rise = gelu_and_slope(nn(x_mlp[pl.ds(at, length), :], w_up[:, c]) + bias_up[:, c])
        active[pl.ds(to, length), c] = value.astype(BF16)
        slope[pl.ds(to, length), c] = rise.astype(BF16)

    lax.fori_loop(0, w_up.shape[1] // WIDE, step, None, unroll=6)


def project_in(x_norm, at, length, w_qkv, vec, targets, to):
    width = w_qkv.shape[0]
    for part, (target, bias) in enumerate(zip(targets, (BIAS_Q, None, BIAS_V))):
        for c in range(0, width, WIDE):
            acc = nn(x_norm[at : at + length, :], w_qkv[:, part * width + c : part * width + c + WIDE])
            if bias is not None:
                acc = acc + vec[bias : bias + 1, c : c + WIDE]
            target[to[part] : to[part] + length, c : c + WIDE] = acc.astype(BF16)


def project_out(context, at, length, w_out, vec, entry, middle):
    for c in range(0, w_out.shape[1], WIDE):
        acc = nn(context[at : at + length, :], w_out[:, c : c + WIDE])
        middle[at : at + length, c : c + WIDE] = (
            entry[at : at + length, c : c + WIDE] + acc + vec[BIAS_OUT : BIAS_OUT + 1, c : c + WIDE]
        )


def feed_down(active, at, length, w_down, vec, middle, middle_at, state):
    for c in range(0, w_down.shape[1], WIDE):
        acc = nn(active[at : at + length, :], w_down[:, c : c + WIDE])
        state[:, c : c + WIDE] = (
            middle[middle_at : middle_at + length, c : c + WIDE] + acc + vec[BIAS_DOWN : BIAS_DOWN + 1, c : c + WIDE]
        )


def enter(state, r, vec, entry, at):
    for b in range(0, state.shape[0], LN_ROWS):
        entry[at + b : at + b + LN_ROWS, :] = state[b : b + LN_ROWS, :].astype(F32) + vec[EMBED + r : EMBED + r + 1, :]


def start_kernel(
    place_ref, lengths_ref, tokens, p0, p1, p2, p3,
    w_qkv, vec, bias_up, mask, x_norm, q, k, v, probs, context, entry,
    small, scores, sems,
):
    length, width = tokens.shape
    fetch(place_ref, (p0, p1, p2, p3), (w_qkv, small), sems)

    rows_at, keys_at = iota(mask.shape, 0), iota(mask.shape, 1)
    for _ in range(PASSES - 1):
        keys_at = jnp.where(keys_at >= length, keys_at - length, keys_at)
    same = keys_at <= rows_at
    end = 0
    for n in range(lengths_ref.shape[0]):
        end = end + lengths_ref[n]
        same = same & ((rows_at >= end) == (keys_at >= end))
    mask[...] = jnp.where(same, 0.0, -1e30)

    wait_whole(small, sems.at[1])
    side = SMALL // 2
    vec[...] = nt(pick_vectors(0, 0, EMBED), small[:, :side]) + nt(
        pick_vectors(4 - EMBED, EMBED, EMBED + PASSES), small[:, side:]
    )
    repeated = nn(small[:, side:], spread_four())
    for b in range(bias_up.shape[1] // WIDE):
        rows = repeated[b * (WIDE // 4) : (b + 1) * (WIDE // 4), :]
        bias_up[:, b * WIDE : (b + 1) * WIDE] = jnp.sum(jnp.where(own_lanes(), rows, 0.0), axis=0, keepdims=True)

    enter(tokens, 0, vec, entry, 0)
    norm_forward(entry, 0, length, vec, GAIN_ATTN, SHIFT_ATTN, x_norm, 0)
    wait_whole(w_qkv, sems.at[0])
    project_in(x_norm, 0, length, w_qkv, vec, (q, k, v), (0, 0, 0))

    def pair(j, _):
        attend(j, q, k, v, probs, scores, mask, context, 0, length)

    lax.fori_loop(0, width // PAIR, pair, None, unroll=2)


def up_kernel(
    place_ref, context, vec, bias_up, entry, p0, p1, p2, p3, w_up, w_out, middle, x_mlp, active, slope, sems
):
    length = context.shape[0]
    fetch(place_ref, (p0, p1, p2, p3), (w_up, w_out), sems)
    wait_whole(w_out, sems.at[1])
    project_out(context, 0, length, w_out, vec, entry, middle)
    norm_forward(middle, 0, length, vec, GAIN_MLP, SHIFT_MLP, x_mlp, 0)
    wait_whole(w_up, sems.at[0])
    feed_up(x_mlp, 0, length, w_up, bias_up, active, slope, 0)


def down_half(place_ref, swapped, active_0, active, d_z, target):
    length = active_0.shape[0]
    width = target.shape[2]
    step = 2 * target.shape[1]
    half = pl.ds(half_start(place_ref, swapped, width), width)

    def some(j, _):
        c = cols(j, step)
        grad = tn(active_0[:, c], d_z[:length, half]) + tn(active[:, c], d_z[length:, half])
        put_blocks(place_ref, swapped, target, grad.astype(BF16), 2 * j, 0)

    lax.fori_loop(0, active_0.shape[1] // step, some, None, unroll=2)


def main_kernel(
    place_ref, cotangent, vec, bias_up, mask, w_qkv, w_out, w_up, k_0, v_0, middle_0, active_0, slope_0, p0, p1, p2, p3,
    output, state, g_vec, x_norm, context, x_mlp, active, d_hidden_0, d_hidden, d_z, d_y, d_mixed, k_grad_0, v_grad_0,
    w_down, q, k_all, v_all, probs_1, probs_2, entry, middle, k_grad, v_grad, extra, d_context, scores, d_scores, sems,
):
    probs = (None, probs_1, probs_2)
    length, width = state.shape
    inner = w_up.shape[1]
    pair_count = width // PAIR
    fetch(place_ref, (p0, p1, p2, p3), (w_down,), sems)
    g_vec[...] = jnp.zeros(g_vec.shape, F32)
    k_all[:length, :] = k_0[...]
    v_all[:length, :] = v_0[...]
    wait_whole(w_down, sems.at[0])
    feed_down(active_0, 0, length, w_down, vec, middle_0, 0, state)

    for r in range(1, PASSES):
        at, seen = (r - 1) * length, (r + 1) * length
        enter(state, r, vec, entry, at)
        norm_forward(entry, at, length, vec, GAIN_ATTN, SHIFT_ATTN, x_norm, at)
        project_in(x_norm, at, length, w_qkv, vec, (q, k_all, v_all), (at, r * length, r * length))

        def pair(j, _):
            attend(j, q, k_all, v_all, probs[r], scores, mask, context, at, seen)

        lax.fori_loop(0, pair_count, pair, None, unroll=2)
        project_out(context, at, length, w_out, vec, entry, middle)
        norm_forward(middle, at, length, vec, GAIN_MLP, SHIFT_MLP, x_mlp, at)
        feed_up(x_mlp, at, length, w_up, bias_up, active, d_hidden, at)
        feed_down(active, at, length, w_down, vec, middle, at, state)

    for b in range(0, length, 64):
        output[b : b + 64, :] = state[b : b + 64, :].astype(BF16)
        state[b : b + 64, :] = cotangent[b : b + 64, :].astype(F32)

    def through_down(r, slope, target, to):
        for b in range(0, length, 64):
            d_z[r * length + b : r * length + b + 64, :] = state[b : b + 64, :].astype(BF16)

        def step(j, _):
            c = cols(j, WIDE)
            acc = nt(d_z[r * length : (r + 1) * length, :], w_down[c, :])
            rows = pl.ds(to, length)
            target[rows, c] = (acc * slope[rows, c].astype(F32)).astype(BF16)

        lax.fori_loop(0, inner // WIDE, step, None, unroll=6)

    for r in reversed(range(1, PASSES)):
        at, seen = (r - 1) * length, (r + 1) * length
        mine = pl.ds(at, length)
        through_down(r, d_hidden, d_hidden, at)
        for c in range(0, width, WIDE):
            extra[:, c : c + WIDE] = nt(d_hidden[mine, :], w_up[c : c + WIDE, :])
        norm_backward(middle, at, extra, state, vec, GAIN_MLP, SHIFT_MLP, g_vec, d_y, at, None)
        for c in range(0, width, WIDE):
            d_context[:, c : c + WIDE] = nt(d_y[mine, :], w_out[c : c + WIDE, :]).astype(BF16)

        def pair_back(j, _):
            attend_back(
                j, q, k_all, v_all, probs[r], scores, d_scores, d_context, context, at, seen, d_mixed, k_grad, v_grad,
                r == PASSES - 1,
            )

        lax.fori_loop(0, pair_count, pair_back, None, unroll=2)
        for b in range(0, length, 64):
            part = slice(at + b, at + b + 64)
            made = slice(r * length + b, r * length + b + 64)
            d_mixed[part, width : 2 * width] = (k_grad[made, :] * SCALE).astype(BF16)
            d_mixed[part, 2 * width :] = v_grad[made, :].astype(BF16)
        for c in range(0, width, WIDE):
            extra[:, c : c + WIDE] = nt(d_mixed[mine, :], w_qkv[c : c + WIDE, :])
        norm_backward(entry, at, extra, state, vec, GAIN_ATTN, SHIFT_ATTN, g_vec, None, 0, EMBED + r)

    k_grad_0[...] = k_grad[:length, :]
    v_grad_0[...] = v_grad[:length, :]
    through_down(0, slope_0, d_hidden_0, 0)
    g_vec[BIAS_DOWN : BIAS_DOWN + 1, :] = nn(jnp.ones((16, PASSES * length), BF16), d_z[...])[:1]


def give_down_kernel(place_ref, active_0, active, d_z, give):
    down_half(place_ref, 1, active_0, active, d_z, give)


def keep_down_kernel(place_ref, active_0, active, d_z, keep):
    down_half(place_ref, 0, active_0, active, d_z, keep)


def up_half(place_ref, swapped, x_0, x, d_0, d, target, first_col, source_col, width):
    size = 384 if width % 384 == 0 else width
    start = half_start(place_ref, swapped, width)
    for c in range(0, width, size):
        part = pl.ds(pl.multiple_of(start + (source_col + c), 128), size)
        grad = tn(x_0[...], d_0[:, part]) + tn(x[...], d[:, part])
        put_blocks(place_ref, swapped, target, grad.astype(BF16), 0, first_col + c)


def give_up_kernel(
    place_ref, vec, w_up, w_out, x_mlp_0, x_mlp, d_hidden_0, d_hidden, middle_0, state_in, g_vec_in, context_0, context, d_y_1,
    give, state, g_vec, d_y, d_context,
    extra,
):
    width, inner = state.shape[1], w_up.shape[1]
    up_half(place_ref, 1, x_mlp_0, x_mlp, d_hidden_0, d_hidden, give, 0, 0, inner // 2)
    for c in range(0, width, WIDE):
        extra[:, c : c + WIDE] = nt(d_hidden_0[...], w_up[c : c + WIDE, :])
    state[...] = state_in[...]
    g_vec[...] = g_vec_in[...]
    norm_backward(middle_0, 0, extra, state, vec, GAIN_MLP, SHIFT_MLP, g_vec, d_y, 0, None)
    for c in range(0, width, WIDE):
        d_context[:, c : c + WIDE] = nt(d_y[...], w_out[c : c + WIDE, :]).astype(BF16)
    up_half(place_ref, 1, context_0, context, d_y, d_y_1, give, inner // 2, 0, width // 2)


def keep_up_kernel(
    place_ref, x_mlp_0, x_mlp, d_hidden_0, d_hidden, context_0, context, d_y_0, d_y, keep, g_bias_up
):
    width, inner = x_mlp.shape[1], d_hidden.shape[1]
    up_half(place_ref, 0, x_mlp_0, x_mlp, d_hidden_0, d_hidden, keep, 0, 0, inner // 2)
    up_half(place_ref, 0, context_0, context, d_y_0, d_y, keep, inner // 2, 0, width // 2)
    ones = jnp.ones((16, x_mlp.shape[0]), BF16)
    length = x_mlp_0.shape[0]

    def step(j, _):
        c = cols(j, 768)
        g_bias_up[:, c] = (nn(ones[:, :length], d_hidden_0[:, c]) + nn(ones, d_hidden[:, c]))[:1]

    lax.fori_loop(0, g_bias_up.shape[1] // 768, step, None)


def last_kernel(
    place_ref, vec, w_qkv, q, k, v, probs, context_0, d_context, d_y_0, d_y, d_mixed, entry, k_grad_0, v_grad_0, state_in,
    g_vec_in, g_bias_up,
    token_grad, d_mixed_0, small,
    k_grad, v_grad, state, g_vec, extra, scores, d_scores,
):
    length, width = state.shape
    k_grad[...] = k_grad_0[...]
    v_grad[...] = v_grad_0[...]
    state[...] = state_in[...]
    g_vec[...] = g_vec_in[...]

    def pair_back(j, _):
        attend_back(
            j, q, k, v, probs, scores, d_scores, d_context, context_0, 0, length, d_mixed_0, k_grad, v_grad, False
        )

    lax.fori_loop(0, width // PAIR, pair_back, None, unroll=2)
    for b in range(0, length, 64):
        part = slice(b, b + 64)
        d_mixed_0[part, width : 2 * width] = (k_grad[part, :] * SCALE).astype(BF16)
        d_mixed_0[part, 2 * width :] = v_grad[part, :].astype(BF16)
    for c in range(0, width, WIDE):
        extra[:, c : c + WIDE] = nt(d_mixed_0[...], w_qkv[c : c + WIDE, :])
    norm_backward(entry, 0, extra, state, vec, GAIN_ATTN, SHIFT_ATTN, g_vec, None, 0, EMBED)
    for b in range(0, length, 64):
        token_grad[b : b + 64, :] = state[b : b + 64, :].astype(BF16)

    ones = jnp.ones((16, 2 * length), BF16)

    def sums(d_0, d):
        return (nn(ones[:, :length], d_0) + nn(ones, d))[:1]

    g_vec[BIAS_Q : BIAS_Q + 1, :] = sums(d_mixed_0[:, :width], d_mixed[:, :width])
    g_vec[BIAS_V : BIAS_V + 1, :] = sums(d_mixed_0[:, 2 * width :], d_mixed[:, 2 * width :])
    g_vec[BIAS_OUT : BIAS_OUT + 1, :] = sums(d_y_0[...], d_y[...])
    vectors = g_vec[...].astype(BF16)
    four = []
    for b in range(g_bias_up.shape[1] // WIDE):
        four.append(jnp.where(own_lanes(), g_bias_up[:, b * WIDE : (b + 1) * WIDE], 0.0).astype(BF16))
    second = tn(vectors, pick_vectors(4 - EMBED, EMBED, EMBED + PASSES)) + nt(
        jnp.concatenate(four, axis=0), spread_four()
    )
    small[:, : SMALL // 2] = tn(vectors, pick_vectors(0, 0, EMBED)).astype(BF16)
    small[:, SMALL // 2 :] = second.astype(BF16)


def qkv_kernel(swapped, place_ref, x_norm_0, x_norm, d_mixed_0, d_mixed, small, target):
    wide = d_mixed.shape[1] // 2
    up_half(place_ref, swapped, x_norm_0, x_norm, d_mixed_0, d_mixed, target, 0, 0, wide)
    side = SMALL // 2
    put_blocks(place_ref, swapped, target, small[:, pl.ds(half_start(place_ref, swapped, side), side)], 0, wide)


def call(kernel, name, inputs, outputs, scratch, flops, touched):
    size = lambda shape, dtype: math.prod(shape) * jnp.dtype(dtype).itemsize
    need = sum(size(*s) for s in scratch if isinstance(s, tuple))
    results = [pltpu.VMEM(shape, dtype) if stays else jax.ShapeDtypeStruct(shape, dtype) for shape, dtype, stays in outputs]
    extra = sum(size(shape, dtype) for shape, dtype, stays in outputs if not stays)
    return pl.pallas_call(
        kernel,
        out_shape=results,
        in_specs=[pl.BlockSpec(memory_space=memory) for _, memory in inputs],
        out_specs=[pl.BlockSpec(memory_space=pltpu.VMEM)] * len(outputs),
        scratch_shapes=[pltpu.VMEM(*s) if isinstance(s, tuple) else s for s in scratch],
        compiler_params=pltpu.CompilerParams(vmem_limit_bytes=need + extra + 4 * 2**20),
        cost_estimate=pl.CostEstimate(flops=flops, bytes_accessed=touched, transcendentals=0),
        name=name,
    )(*[array for array, _ in inputs])


def layer(place, lengths, tokens, cotangent, chunks):
    length, width = tokens.shape
    inner = 16 * chunks[2][0].shape[2]
    rest = (PASSES - 1) * length
    heads = width // PAIR
    anywhere, local, scalars = pl.ANY, pltpu.VMEM, pltpu.SMEM
    place = (place, scalars)
    L = lambda *arrays: [(a, local) for a in arrays]

    G = lambda n: [(a, anywhere) for a in chunks[n]]
    low = lambda *shape: (shape, BF16)
    full = lambda *shape: (shape, F32)
    kept = lambda *specs: [(*s, True) for s in specs]
    out = lambda *specs: [(*s, False) for s in specs]
    semaphores = lambda n: pltpu.SemaphoreType.DMA((n,))
    row, row32 = low(length, width), full(length, width)
    part = 2 * length * width

    far_pieces(chunks[0])
    mate_pieces(chunks[0])
    far_pieces(chunks[1])
    w_qkv, vec, bias_up, mask, x_norm_0, q_0, k_0, v_0, probs_0, context_0, entry_0 = call(
        start_kernel, "start",
        [place, (lengths, scalars)] + L(tokens) + G(0),
        kept(
            low(width, 3 * width), full(VECTORS, width), full(1, inner), full(length, PASSES * length), row, row, row, row,
            low(heads, 2 * length, length), row, row32,
        ),
        [low(width, SMALL), full(2 * length, length), semaphores(2)],
        20 * 10**9, 70 * 2**20,
    )
    far_pieces(chunks[2])
    mate_pieces(chunks[1])
    w_up, w_out, middle_0, x_mlp_0, active_0, slope_0 = call(
        up_kernel, "up",
        [place] + L(context_0, vec, bias_up, entry_0) + G(1),
        kept(low(width, inner), low(width, width), row32, row, low(length, inner), low(length, inner)),
        [semaphores(2)],
        12 * 10**9, 40 * 2**20,
    )
    mate_pieces(chunks[2], context_0)
    (
        output, state, g_vec, x_norm, context, x_mlp, active, d_hidden_0, d_hidden, d_z, d_y, d_mixed, k_grad, v_grad,
    ) = call(
        main_kernel, "main",
        [place] + L(cotangent, vec, bias_up, mask, w_qkv, w_out, w_up, k_0, v_0, middle_0, active_0, slope_0) + G(2),
        out(row) + kept(
            row32, full(VECTORS, width), low(rest, width), low(rest, width), low(rest, width), low(rest, inner),
            low(length, inner), low(rest, inner), low(rest + length, width), low(rest, width), low(rest, 3 * width),
            row32, row32,
        ),
        [
            low(inner, width), low(rest, width), low(rest + length, width), low(rest + length, width),
            low(heads, 2 * length, 2 * length), low(heads, 2 * length, 3 * length), full(rest, width), full(rest, width),
            full(rest + length, width), full(rest + length, width), row32, row, full(2 * length, PASSES * length),
            low(2 * length, PASSES * length), semaphores(1),
        ],
        40 * part * inner, 60 * 2**20,
    )
    halves_ = []
    for kernel, name in ((give_down_kernel, "give_down"), (keep_down_kernel, "keep_down")):
        halves_ += call(
            kernel, name, [place] + L(active_0, active, after(d_z, *halves_)), kept(low(16, inner // 16, width // 2)), [],
            *COST,
        )
    begun = [begin_scatter(mate_step(halves_[0]), *halves_, MATE_WEIGHTS[0])]
    state = after(state, begun[0][0])
    begun[0] = far_step(begun[0])
    up_shape = low(16, width // 16, inner // 2 + width // 2)
    give_up, state, g_vec, d_y_0, d_context = call(
        give_up_kernel, "give_up",
        [place]
        + L(vec, w_up, w_out, x_mlp_0, x_mlp, d_hidden_0, d_hidden, middle_0, state, g_vec, context_0, context, d_y),
        kept(up_shape, row32, full(VECTORS, width), row, row), [row32],
        *COST,
    )
    keep_up, g_bias_up = call(
        keep_up_kernel, "keep_up",
        [place] + L(x_mlp_0, x_mlp, d_hidden_0, d_hidden, context_0, context, d_y_0, d_y),
        kept(up_shape, full(1, inner)), [],
        *COST,
    )
    begun.append(begin_scatter(mate_step(give_up), give_up, keep_up, MATE_WEIGHTS[1]))
    state = after(state, begun[0][0])
    near_0 = near_step(begun[0], FAR_WEIGHTS[0])
    state = after(state, begun[1][0])
    begun[1] = far_step(begun[1])
    token_grad, d_mixed_0, g_small = call(
        last_kernel, "last",
        [place]
        + L(
            vec, w_qkv, q_0, k_0, v_0, probs_0, context_0, d_context, d_y_0, d_y, d_mixed, entry_0, k_grad, v_grad, state,
            g_vec, g_bias_up,
        ),
        out(row) + kept(low(length, 3 * width), low(width, SMALL)),
        [
            row32, row32, row32, full(VECTORS, width), row32, full(2 * length, length), low(2 * length, length),
        ],
        40 * 10**9, 140 * 2**20,
    )
    last_shape = low(16, width // 16, 3 * width // 2 + SMALL // 2)
    ends = []
    for name, swapped in (("give_qkv", 1), ("keep_qkv", 0)):
        earlier = ends if ends else near_0[:1]
        ends += call(
            functools.partial(qkv_kernel, swapped), name,
            [place] + L(x_norm_0, x_norm, d_mixed_0, d_mixed, after(g_small, *earlier)), kept(last_shape), [], TINY, TINY,
        )
    give, keep = begin_scatter(mate_step(ends[0]), *ends, MATE_WEIGHTS[2])
    near_0 = (near_0[0], after(near_0[1], give))
    return output, token_grad, (near_0, begun[1], far_step((give, keep)))


def per_device(
    tokens,
    lengths,
    cotangent,
    w_qkv,
    bias_q,
    bias_v,
    w_out,
    bias_out,
    gain_attn,
    shift_attn,
    gain_mlp,
    shift_mlp,
    w_up,
    bias_up,
    w_down,
    bias_down,
    pass_embed,
):
    small = pack_small(
        [bias_q, bias_v, bias_out, gain_attn, shift_attn, gain_mlp, shift_mlp, bias_down], bias_up, pass_embed
    )
    place, chunks, last_z = gather_all(w_qkv, w_out, small, w_up, w_down)
    output, token_grad, parts = layer(place, lengths[0], tokens, cotangent, chunks)
    g_qkv, g_out, g_up, g_down, g_small = scatter_all(parts)
    (g_bq, g_bv, g_bo, g_ga, g_sa, g_gm, g_sm, g_bd), g_bu, g_pe = unpack_small(g_small)
    return (
        output,
        token_grad,
        g_qkv,
        g_bq,
        g_bv,
        g_out,
        g_bo,
        g_ga,
        g_sa,
        g_gm,
        g_sm,
        g_up,
        g_bu,
        g_down,
        g_bd,
        g_pe,
    )


def solution(mesh):
    placed = (
        P(("dp", "fsdp"), None),
        P(("dp", "fsdp"), None),
        P(("dp", "fsdp"), None),
        P(("dp", "fsdp"), None),
        P(("dp", "fsdp")),
        P(("dp", "fsdp")),
        P(("dp", "fsdp"), None),
        P(("dp", "fsdp")),
        P(("dp", "fsdp")),
        P(("dp", "fsdp")),
        P(("dp", "fsdp")),
        P(("dp", "fsdp")),
        P(("dp", "fsdp"), None),
        P(("dp", "fsdp")),
        P(("dp", "fsdp"), None),
        P(("dp", "fsdp")),
        P(None, ("dp", "fsdp")),
    )
    return jax.shard_map(
        per_device,
        mesh=mesh,
        in_specs=placed,
        out_specs=(
            P(("dp", "fsdp"), None),
            P(("dp", "fsdp"), None),
            P(("dp", "fsdp"), None),
            P(("dp", "fsdp")),
            P(("dp", "fsdp")),
            P(("dp", "fsdp"), None),
            P(("dp", "fsdp")),
            P(("dp", "fsdp")),
            P(("dp", "fsdp")),
            P(("dp", "fsdp")),
            P(("dp", "fsdp")),
            P(("dp", "fsdp"), None),
            P(("dp", "fsdp")),
            P(("dp", "fsdp"), None),
            P(("dp", "fsdp")),
            P(None, ("dp", "fsdp")),
        ),
        check_vma=False,
    )
```

```python
import functools
import math

import jax
import jax.numpy as jnp
from jax import lax
from jax.experimental import pallas as pl
from jax.experimental.pallas import tpu as pltpu
from jax.sharding import PartitionSpec as P

HEAD_DIM = 64
PASSES = 3
EPSILON = 1e-05
AXES = ("dp", "fsdp")
F32 = jnp.float32
BF16 = jnp.bfloat16


def pairs(partner):
    return [(i, partner(i)) for i in range(32)]


TO_MATE = pairs(lambda i: i ^ 1)
TO_Z = [pairs(lambda i, k=k: i ^ (8 * k)) for k in range(4)]
TO_NEAR = pairs(lambda i: i ^ (2 if i & 1 else 4))
TO_FAR = pairs(lambda i: i ^ (4 if i & 1 else 2))


def send(x, route):
    return lax.ppermute(x, AXES, route)


def after(x, *earlier):
    earlier = tuple(e for e in earlier if e is not None)
    return lax.optimization_barrier((x, earlier))[0] if earlier else x


def in_core_order(core, mine, other, axis):
    return jnp.where(
        core == 0,
        jnp.concatenate([mine, other], axis=axis),
        jnp.concatenate([other, mine], axis=axis),
    )


def stack_kernel(*refs):
    for n, ref in enumerate(refs[:-1]):
        refs[-1][n] = ref[...]


def stack_blocks(blocks, weight):
    if not weight:
        return jnp.stack(blocks)
    return pl.pallas_call(
        stack_kernel,
        out_shape=jax.ShapeDtypeStruct((len(blocks), *blocks[0].shape), BF16),
        in_specs=[pl.BlockSpec(memory_space=pltpu.VMEM)] * len(blocks),
        out_specs=pl.BlockSpec(memory_space=pltpu.VMEM),
        compiler_params=pltpu.CompilerParams(vmem_limit_bytes=8 * 2**20),
        cost_estimate=pl.CostEstimate(flops=weight * 10**9, bytes_accessed=weight * 35 * 10**5, transcendentals=0),
        name="stack",
    )(*blocks)


STACK_WEIGHTS = (0, 0, 10)
BOTH_WEIGHTS = (10, 0, 0)


def gather_chunks(blocks):
    chunks, earlier = [], None
    for n, block in enumerate(blocks):
        block = after(block, earlier)
        earlier = [send(block, TO_Z[k]) for k in (1, 2, 3)]
        stack = stack_blocks([block] + earlier, STACK_WEIGHTS[n])
        both = stack_blocks([stack, send(stack, TO_NEAR)], BOTH_WEIGHTS[n])
        chunks.append([both, None, send(both, TO_MATE), None])
    return chunks, earlier


def far_pieces(pieces, *earlier):
    if pieces[1] is None:
        pieces[1] = send(after(pieces[0], *earlier), TO_FAR)


def mate_pieces(pieces, *earlier):
    if pieces[3] is None:
        pieces[3] = send(after(pieces[1], *earlier), TO_MATE)


def chip_of(place, swapped, far, near, z):
    chip, core = place
    order = core ^ swapped
    near_bit = 2 - order
    far_bit = 1 + order
    return chip ^ (far * far_bit) ^ (near * near_bit) ^ (z * 4)


def add_low(a, b):
    return (a.astype(F32) + b.astype(F32)).astype(BF16)


def add_kernel(got, keep, give_out, keep_out):
    for n in range(got.shape[1]):
        give_out[n] = (keep[1, n].astype(F32) + got[1, n].astype(F32)).astype(BF16)
        keep_out[n] = (keep[0, n].astype(F32) + got[0, n].astype(F32)).astype(BF16)


def add_halves(got, keep, weight):
    if not weight:
        return add_low(keep[1], got[1]), add_low(keep[0], got[0])
    shape, merged = keep.shape[1:], (2, -1, keep.shape[-2], keep.shape[-1])
    got, keep = got.reshape(merged), keep.reshape(merged)
    give, keep = pl.pallas_call(
        add_kernel,
        out_shape=[jax.ShapeDtypeStruct(keep.shape[1:], BF16)] * 2,
        in_specs=[pl.BlockSpec(memory_space=pltpu.VMEM)] * 2,
        out_specs=[pl.BlockSpec(memory_space=pltpu.VMEM)] * 2,
        compiler_params=pltpu.CompilerParams(vmem_limit_bytes=8 * 2**20),
        cost_estimate=pl.CostEstimate(flops=weight * 10**9, bytes_accessed=weight * 35 * 10**5, transcendentals=0),
        name="add",
    )(got, keep)
    return give.reshape(shape), keep.reshape(shape)


def mate_step(give):
    return send(give, TO_MATE) if is_known_slice() else give


def begin_scatter(got, give, keep, weight):
    if not is_known_slice():
        return give, keep
    split = lambda a: a.reshape(2, 2, 4, *a.shape[1:])
    return add_halves(split(got), split(keep), weight)


def far_step(part):
    give, keep = part
    if not is_known_slice():
        return part
    return send(give, TO_FAR), keep


def near_step(part, weight):
    got, keep = part
    if not is_known_slice():
        return part
    give, keep = add_halves(got, keep, weight)
    return send(give, TO_NEAR), keep


def end_scatter(core, begun):
    begun = [(begun[0][0], after(begun[0][1], begun[1][0]))] + [near_step(begun[n], FAR_WEIGHTS[n]) for n in (1, 2)]
    results, earlier = [], None
    for n in range(len(begun)):
        near, keep = begun[n]
        z = [add_low(keep[k], near[k]) for k in (1, 2, 3)]
        z = [send(give, TO_Z[k + 1]) for k, give in enumerate(after(z, earlier))]
        earlier = z if n == 0 else None
        total = keep[0].astype(F32) + near[0].astype(F32)
        for part in z:
            total = total + part.astype(F32)
        total = total.reshape(2, total.shape[0] // 2, total.shape[1])
        mine = jnp.where(core == 0, total[0], total[1])
        theirs = jnp.where(core == 0, total[1], total[0])
        if n == 0:
            theirs = after(theirs, begun[1][0])
        other = send(theirs, TO_MATE)
        results.append((jnp.where(core == 0, mine, other), jnp.where(core == 0, other, mine)))
    return results


MATE_WEIGHTS = (0, 15, 0)
FAR_WEIGHTS = (40, 0, 0)
SMALL = 256


def pack_small(vectors, bias_up, pass_embed):
    rows = vectors[0].shape[0]
    first = jnp.stack(vectors, axis=1)
    second = jnp.concatenate([bias_up.reshape(rows, -1), pass_embed.T], axis=1)
    pad = lambda a: jnp.pad(a, ((0, 0), (0, SMALL // 2 - a.shape[1])))
    return jnp.concatenate([pad(first), pad(second)], axis=1)


def unpack_small(small):
    half = SMALL // 2
    vectors = [small[:, k] for k in range(8)]
    return vectors, small[:, half : half + 4].reshape(-1), small[:, half + 4 : half + 4 + PASSES].T


def is_known_slice():
    return lax.axis_size("dp") == 8 and lax.axis_size("fsdp") == 4


def place_of():
    if not is_known_slice():
        return jnp.zeros((2,), jnp.int32)
    index = lax.axis_index("dp") * 4 + lax.axis_index("fsdp")
    return jnp.stack([index >> 1, index & 1]).astype(jnp.int32)


def halves(*arrays):
    return [
        jnp.concatenate([a[:, h * (a.shape[1] // 2) : (h + 1) * (a.shape[1] // 2)] for a in arrays], axis=1)
        for h in range(2)
    ]


def slots(swapped):
    return [chip_of((0, 0), swapped, far, near, z) for far in range(2) for near in range(2) for z in range(4)]


def gather_all(w_qkv, w_out, small, w_up, w_down):
    place = place_of()
    groups = ((w_qkv, small), (w_up, w_out), (w_down,))
    if not is_known_slice():
        chunks = []
        for arrays in groups:
            whole = [lax.all_gather(a, AXES, axis=0, tiled=True) for a in arrays]
            pieces = []
            for swapped, part in enumerate(halves(*whole)):
                blocks = part.reshape(16, -1, part.shape[1])
                blocks = jnp.stack([blocks[chip] for chip in slots(swapped)])
                pieces += list(blocks.reshape(2, 2, 4, *blocks.shape[1:]))
            chunks.append(pieces)
        return place, chunks, ()
    core = place[1]
    blocks = []
    for arrays in groups:
        low, high = halves(*arrays)
        mine = jnp.where(core == 0, low, high)
        other = send(jnp.where(core == 0, high, low), TO_MATE)
        blocks.append(in_core_order(core, mine, other, 0))
    chunks, last_z = gather_chunks(blocks)
    return place, chunks, last_z


def scatter_all(parts):
    if is_known_slice():
        sums = end_scatter(place_of()[1], list(parts))
    else:
        sums = []
        for give, keep in parts:
            both = []
            for blocks, swapped in ((keep, 0), (give, 1)):
                order = slots(swapped)
                whole = jnp.concatenate([blocks[order.index(chip)] for chip in range(16)], axis=0)
                both.append(lax.psum_scatter(whole.astype(F32), AXES, scatter_dimension=0, tiled=True))
            sums.append(both)
    join = lambda n, first, width: jnp.concatenate([s[:, first : first + width] for s in sums[n]], axis=1)
    small_half = SMALL // 2
    qkv_half = sums[2][0].shape[1] - small_half
    out_half = qkv_half // 3
    up_half_ = sums[1][0].shape[1] - out_half
    return [
        join(2, 0, qkv_half),
        join(1, up_half_, out_half),
        join(1, 0, up_half_),
        join(0, 0, sums[0][0].shape[1]),
        join(2, qkv_half, small_half),
    ]


BIAS_Q, BIAS_V, BIAS_OUT, GAIN_ATTN, SHIFT_ATTN, GAIN_MLP, SHIFT_MLP, BIAS_DOWN, EMBED = range(9)
VECTORS = 16
PAIR = 2 * HEAD_DIM
SCALE = HEAD_DIM**-0.5
LOG2_E = 1.4426950408889634
GELU_A = 0.7978845608028654
GELU_B = 0.044715
LN_ROWS = 32
COST = (10 * 10**9, 35 * 2**20)
TINY = 1000
SOFT_ROWS = 64
WIDE = 256


def dot(a, b, a_dim, b_dim):
    return lax.dot_general(a, b, (((a_dim,), (b_dim,)), ((), ())), preferred_element_type=F32)


def nn(a, b):
    return dot(a, b, 1, 0)


def nt(a, b):
    return dot(a, b, 1, 1)


def tn(a, b):
    return dot(a, b, 0, 0)


def cols(n, size):
    return pl.ds(pl.multiple_of(n * size, size), size)


def row_mean(x):
    return jnp.sum(x, axis=1, keepdims=True) * (1.0 / x.shape[1])


def normalized(x):
    centred = x - row_mean(x)
    inverse = lax.rsqrt(row_mean(centred * centred) + EPSILON)
    return centred * inverse, inverse


def gelu_and_slope(v):
    square = v * v
    t = jnp.tanh(v * (GELU_A + (GELU_A * GELU_B) * square))
    half = 0.5 * (1.0 + t)
    slope = half + v * (1.0 - t * t) * (0.5 * GELU_A + (1.5 * GELU_A * GELU_B) * square)
    return v * half, slope


def iota(shape, dim):
    return lax.broadcasted_iota(jnp.int32, shape, dim)


def first_lanes():
    return iota((1, PAIR), 1) < HEAD_DIM


def stacked(x):
    low = first_lanes().astype(F32)
    return jnp.concatenate([x * low.astype(BF16), x * (1.0 - low).astype(BF16)], axis=0)


def unstacked(x):
    length = x.shape[0] // 2
    return jnp.where(first_lanes(), x[:length], x[length:])


def fetch(place_ref, pieces, targets, sems):
    place = (place_ref[0], place_ref[1])
    for source, swapped, far in zip(pieces, (0, 0, 1, 1), (0, 1, 0, 1)):
        half = place[1] ^ swapped
        rows = source.shape[2]
        for near in range(2):
            for z in range(4):
                chip = chip_of(place, swapped, far, near, z)
                first = 0
                for n, full in enumerate(targets):
                    width = full.shape[1] // 2
                    pltpu.make_async_copy(
                        source.at[near, z, :, pl.ds(first, width)],
                        full.at[
                            pl.ds(pl.multiple_of(chip * rows, 16), rows),
                            pl.ds(pl.multiple_of(half * width, 128), width),
                        ],
                        sems.at[n],
                    ).start()
                    first += width


def wait_whole(full, sem):
    pltpu.make_async_copy(full, full, sem).wait()


def slot_of(place_ref, swapped, chip):
    apart = chip ^ place_ref[0]
    order = place_ref[1] ^ swapped
    x, y = apart & 1, (apart >> 1) & 1
    far = x + order * (y - x)
    near = y + order * (x - y)
    return far * 8 + near * 4 + (apart >> 2)


def put_blocks(place_ref, swapped, target, value, first_chip, first_col):
    rows = target.shape[1]
    for n in range(value.shape[0] // rows):
        slot = slot_of(place_ref, swapped, first_chip + n)
        target[slot, :, first_col : first_col + value.shape[1]] = value[n * rows : (n + 1) * rows, :]


def half_start(place_ref, swapped, width):
    return pl.multiple_of((place_ref[1] ^ swapped) * width, 128)


def pick_vectors(offset, first, last):
    row, col = iota((VECTORS, SMALL // 2), 0), iota((VECTORS, SMALL // 2), 1)
    return ((col == row + offset) & (row >= first) & (row < last)).astype(F32).astype(BF16)


def spread_four():
    row, col = iota((SMALL // 2, WIDE), 0), iota((SMALL // 2, WIDE), 1)
    return ((row < 4) & ((col & 3) == row)).astype(F32).astype(BF16)


def own_lanes():
    return (iota((WIDE // 4, WIDE), 1) >> 2) == iota((WIDE // 4, WIDE), 0)


def norm_forward(source, at, length, vec, gain, shift, target, to):
    for b in range(0, length, LN_ROWS):
        n, _ = normalized(source[at + b : at + b + LN_ROWS, :])
        target[to + b : to + b + LN_ROWS, :] = (n * vec[gain : gain + 1, :] + vec[shift : shift + 1, :]).astype(BF16)


def norm_backward(source, at, extra, state, vec, gain, shift, g_vec, rounded, to, embed):
    for b in range(0, state.shape[0], LN_ROWS):
        part = slice(b, b + LN_ROWS)
        n, inverse = normalized(source[at + b : at + b + LN_ROWS, :])
        e = extra[part, :]
        g_vec[gain : gain + 1, :] += jnp.sum(e * n, axis=0, keepdims=True)
        g_vec[shift : shift + 1, :] += jnp.sum(e, axis=0, keepdims=True)
        eg = e * vec[gain : gain + 1, :]
        back = state[part, :] + inverse * (eg - row_mean(eg) - n * row_mean(eg * n))
        state[part, :] = back
        if rounded is not None:
            rounded[to + b : to + b + LN_ROWS, :] = back.astype(BF16)
        if embed is not None:
            g_vec[embed : embed + 1, :] += jnp.sum(back, axis=0, keepdims=True)


def attend(j, q, k, v, probs, scores, mask, context, at, seen):
    length = mask.shape[0]
    mine = pl.ds(at, length)
    c = cols(j, PAIR)
    scores[:, :seen] = nt(stacked(q[mine, c]), k[:seen, c])
    for b in range(0, 2 * length, SOFT_ROWS):
        part = slice(b, b + SOFT_ROWS)
        m = b % length
        s = scores[part, :seen] + mask[m : m + SOFT_ROWS, :seen]
        p = jnp.exp2((s - jnp.max(s, axis=1, keepdims=True)) * (SCALE * LOG2_E))
        p = p * (1.0 / jnp.sum(p, axis=1, keepdims=True))
        probs[j, part, :] = p.astype(BF16)
    context[mine, c] = unstacked(nn(probs[j], v[:seen, c])).astype(BF16)


def attend_back(j, q, k, v, probs, scores, d_scores, d_context, context, at, seen, d_query, k_grad, v_grad, fresh):
    length = d_context.shape[0]
    mine = pl.ds(at, length)
    c = cols(j, PAIR)
    dc = d_context[:, c]
    both = stacked(dc)
    scores[:, :seen] = nt(both, v[:seen, c])
    product = dc.astype(F32) * context[mine, c].astype(F32)
    inner_0 = jnp.sum(jnp.where(first_lanes(), product, 0.0), axis=1, keepdims=True)
    inner_1 = jnp.sum(jnp.where(first_lanes(), 0.0, product), axis=1, keepdims=True)
    for b in range(0, 2 * length, SOFT_ROWS):
        part = slice(b, b + SOFT_ROWS)
        m = b % length
        shift = (inner_0 if b < length else inner_1)[m : m + SOFT_ROWS]
        d_scores[part, :seen] = (probs[j, part, :].astype(F32) * (scores[part, :seen] - shift)).astype(BF16)
    ds = d_scores[:, :seen]
    d_query[mine, c] = (unstacked(nn(ds, k[:seen, c])) * SCALE).astype(BF16)
    k_more = tn(ds, stacked(q[mine, c]))
    v_more = tn(probs[j], both)
    if fresh:
        k_grad[:seen, c] = k_more
        v_grad[:seen, c] = v_more
    else:
        k_grad[:seen, c] += k_more
        v_grad[:seen, c] += v_more


def feed_up(x_mlp, at, length, w_up, bias_up, active, slope, to):
    def step(j, _):
        c = cols(j, WIDE)
        value, rise = gelu_and_slope(nn(x_mlp[pl.ds(at, length), :], w_up[:, c]) + bias_up[:, c])
        active[pl.ds(to, length), c] = value.astype(BF16)
        slope[pl.ds(to, length), c] = rise.astype(BF16)

    lax.fori_loop(0, w_up.shape[1] // WIDE, step, None, unroll=6)


def project_in(x_norm, at, length, w_qkv, vec, targets, to):
    width = w_qkv.shape[0]
    for part, (target, bias) in enumerate(zip(targets, (BIAS_Q, None, BIAS_V))):
        for c in range(0, width, WIDE):
            acc = nn(x_norm[at : at + length, :], w_qkv[:, part * width + c : part * width + c + WIDE])
            if bias is not None:
                acc = acc + vec[bias : bias + 1, c : c + WIDE]
            target[to[part] : to[part] + length, c : c + WIDE] = acc.astype(BF16)


def project_out(context, at, length, w_out, vec, entry, middle):
    for c in range(0, w_out.shape[1], WIDE):
        acc = nn(context[at : at + length, :], w_out[:, c : c + WIDE])
        middle[at : at + length, c : c + WIDE] = (
            entry[at : at + length, c : c + WIDE] + acc + vec[BIAS_OUT : BIAS_OUT + 1, c : c + WIDE]
        )


def feed_down(active, at, length, w_down, vec, middle, middle_at, state):
    for c in range(0, w_down.shape[1], WIDE):
        acc = nn(active[at : at + length, :], w_down[:, c : c + WIDE])
        state[:, c : c + WIDE] = (
            middle[middle_at : middle_at + length, c : c + WIDE] + acc + vec[BIAS_DOWN : BIAS_DOWN + 1, c : c + WIDE]
        )


def enter(state, r, vec, entry, at):
    for b in range(0, state.shape[0], LN_ROWS):
        entry[at + b : at + b + LN_ROWS, :] = state[b : b + LN_ROWS, :].astype(F32) + vec[EMBED + r : EMBED + r + 1, :]


def start_kernel(
    place_ref, lengths_ref, tokens, p0, p1, p2, p3,
    w_qkv, vec, bias_up, mask, x_norm, q, k, v, probs, context, entry,
    small, scores, sems,
):
    length, width = tokens.shape
    fetch(place_ref, (p0, p1, p2, p3), (w_qkv, small), sems)

    rows_at, keys_at = iota(mask.shape, 0), iota(mask.shape, 1)
    for _ in range(PASSES - 1):
        keys_at = jnp.where(keys_at >= length, keys_at - length, keys_at)
    same = keys_at <= rows_at
    end = 0
    for n in range(lengths_ref.shape[0]):
        end = end + lengths_ref[n]
        same = same & ((rows_at >= end) == (keys_at >= end))
    mask[...] = jnp.where(same, 0.0, -1e30)

    wait_whole(small, sems.at[1])
    side = SMALL // 2
    vec[...] = nt(pick_vectors(0, 0, EMBED), small[:, :side]) + nt(
        pick_vectors(4 - EMBED, EMBED, EMBED + PASSES), small[:, side:]
    )
    repeated = nn(small[:, side:], spread_four())
    for b in range(bias_up.shape[1] // WIDE):
        rows = repeated[b * (WIDE // 4) : (b + 1) * (WIDE // 4), :]
        bias_up[:, b * WIDE : (b + 1) * WIDE] = jnp.sum(jnp.where(own_lanes(), rows, 0.0), axis=0, keepdims=True)

    enter(tokens, 0, vec, entry, 0)
    norm_forward(entry, 0, length, vec, GAIN_ATTN, SHIFT_ATTN, x_norm, 0)
    wait_whole(w_qkv, sems.at[0])
    project_in(x_norm, 0, length, w_qkv, vec, (q, k, v), (0, 0, 0))

    def pair(j, _):
        attend(j, q, k, v, probs, scores, mask, context, 0, length)

    lax.fori_loop(0, width // PAIR, pair, None, unroll=3)


def up_kernel(
    place_ref, context, vec, bias_up, entry, p0, p1, p2, p3, w_up, w_out, middle, x_mlp, active, slope, sems
):
    length = context.shape[0]
    fetch(place_ref, (p0, p1, p2, p3), (w_up, w_out), sems)
    wait_whole(w_out, sems.at[1])
    project_out(context, 0, length, w_out, vec, entry, middle)
    norm_forward(middle, 0, length, vec, GAIN_MLP, SHIFT_MLP, x_mlp, 0)
    wait_whole(w_up, sems.at[0])
    feed_up(x_mlp, 0, length, w_up, bias_up, active, slope, 0)


def down_half(place_ref, swapped, active_0, active, d_z, target):
    length = active_0.shape[0]
    width = target.shape[2]
    step = 2 * target.shape[1]
    half = pl.ds(half_start(place_ref, swapped, width), width)

    def some(j, _):
        c = cols(j, step)
        grad = tn(active_0[:, c], d_z[:length, half]) + tn(active[:, c], d_z[length:, half])
        put_blocks(place_ref, swapped, target, grad.astype(BF16), 2 * j, 0)

    lax.fori_loop(0, active_0.shape[1] // step, some, None, unroll=2)


def main_kernel(
    place_ref, cotangent, vec, bias_up, mask, w_qkv, w_out, w_up, k_0, v_0, middle_0, active_0, slope_0, p0, p1, p2, p3,
    output, state, g_vec, x_norm, context, x_mlp, active, d_hidden_0, d_hidden, d_z, d_y, d_mixed, k_grad_0, v_grad_0,
    w_down, q, k_all, v_all, probs_1, probs_2, entry, middle, k_grad, v_grad, extra, d_context, scores, d_scores, sems,
):
    probs = (None, probs_1, probs_2)
    length, width = state.shape
    inner = w_up.shape[1]
    pair_count = width // PAIR
    fetch(place_ref, (p0, p1, p2, p3), (w_down,), sems)
    g_vec[...] = jnp.zeros(g_vec.shape, F32)
    k_all[:length, :] = k_0[...]
    v_all[:length, :] = v_0[...]
    wait_whole(w_down, sems.at[0])
    feed_down(active_0, 0, length, w_down, vec, middle_0, 0, state)

    for r in range(1, PASSES):
        at, seen = (r - 1) * length, (r + 1) * length
        enter(state, r, vec, entry, at)
        norm_forward(entry, at, length, vec, GAIN_ATTN, SHIFT_ATTN, x_norm, at)
        project_in(x_norm, at, length, w_qkv, vec, (q, k_all, v_all), (at, r * length, r * length))

        def pair(j, _):
            attend(j, q, k_all, v_all, probs[r], scores, mask, context, at, seen)

        lax.fori_loop(0, pair_count, pair, None, unroll=3)
        project_out(context, at, length, w_out, vec, entry, middle)
        norm_forward(middle, at, length, vec, GAIN_MLP, SHIFT_MLP, x_mlp, at)
        feed_up(x_mlp, at, length, w_up, bias_up, active, d_hidden, at)
        feed_down(active, at, length, w_down, vec, middle, at, state)

    for b in range(0, length, 64):
        output[b : b + 64, :] = state[b : b + 64, :].astype(BF16)
        state[b : b + 64, :] = cotangent[b : b + 64, :].astype(F32)

    def through_down(r, slope, target, to):
        for b in range(0, length, 64):
            d_z[r * length + b : r * length + b + 64, :] = state[b : b + 64, :].astype(BF16)

        def step(j, _):
            c = cols(j, WIDE)
            acc = nt(d_z[r * length : (r + 1) * length, :], w_down[c, :])
            rows = pl.ds(to, length)
            target[rows, c] = (acc * slope[rows, c].astype(F32)).astype(BF16)

        lax.fori_loop(0, inner // WIDE, step, None, unroll=6)

    for r in reversed(range(1, PASSES)):
        at, seen = (r - 1) * length, (r + 1) * length
        mine = pl.ds(at, length)
        through_down(r, d_hidden, d_hidden, at)
        for c in range(0, width, WIDE):
            extra[:, c : c + WIDE] = nt(d_hidden[mine, :], w_up[c : c + WIDE, :])
        norm_backward(middle, at, extra, state, vec, GAIN_MLP, SHIFT_MLP, g_vec, d_y, at, None)
        for c in range(0, width, WIDE):
            d_context[:, c : c + WIDE] = nt(d_y[mine, :], w_out[c : c + WIDE, :]).astype(BF16)

        def pair_back(j, _):
            attend_back(
                j, q, k_all, v_all, probs[r], scores, d_scores, d_context, context, at, seen, d_mixed, k_grad, v_grad,
                r == PASSES - 1,
            )

        lax.fori_loop(0, pair_count, pair_back, None, unroll=3)
        for b in range(0, length, 64):
            part = slice(at + b, at + b + 64)
            made = slice(r * length + b, r * length + b + 64)
            d_mixed[part, width : 2 * width] = (k_grad[made, :] * SCALE).astype(BF16)
            d_mixed[part, 2 * width :] = v_grad[made, :].astype(BF16)
        for c in range(0, width, WIDE):
            extra[:, c : c + WIDE] = nt(d_mixed[mine, :], w_qkv[c : c + WIDE, :])
        norm_backward(entry, at, extra, state, vec, GAIN_ATTN, SHIFT_ATTN, g_vec, None, 0, EMBED + r)

    k_grad_0[...] = k_grad[:length, :]
    v_grad_0[...] = v_grad[:length, :]
    through_down(0, slope_0, d_hidden_0, 0)
    g_vec[BIAS_DOWN : BIAS_DOWN + 1, :] = nn(jnp.ones((16, PASSES * length), BF16), d_z[...])[:1]


def give_down_kernel(place_ref, active_0, active, d_z, give):
    down_half(place_ref, 1, active_0, active, d_z, give)


def keep_down_kernel(place_ref, active_0, active, d_z, keep):
    down_half(place_ref, 0, active_0, active, d_z, keep)


def up_half(place_ref, swapped, x_0, x, d_0, d, target, first_col, source_col, width):
    size = 384 if width % 384 == 0 else width
    start = half_start(place_ref, swapped, width)
    for c in range(0, width, size):
        part = pl.ds(pl.multiple_of(start + (source_col + c), 128), size)
        grad = tn(x_0[...], d_0[:, part]) + tn(x[...], d[:, part])
        put_blocks(place_ref, swapped, target, grad.astype(BF16), 0, first_col + c)


def give_up_kernel(
    place_ref, vec, w_up, w_out, x_mlp_0, x_mlp, d_hidden_0, d_hidden, middle_0, state_in, g_vec_in, context_0, context, d_y_1,
    give, state, g_vec, d_y, d_context,
    extra,
):
    width, inner = state.shape[1], w_up.shape[1]
    up_half(place_ref, 1, x_mlp_0, x_mlp, d_hidden_0, d_hidden, give, 0, 0, inner // 2)
    for c in range(0, width, WIDE):
        extra[:, c : c + WIDE] = nt(d_hidden_0[...], w_up[c : c + WIDE, :])
    state[...] = state_in[...]
    g_vec[...] = g_vec_in[...]
    norm_backward(middle_0, 0, extra, state, vec, GAIN_MLP, SHIFT_MLP, g_vec, d_y, 0, None)
    for c in range(0, width, WIDE):
        d_context[:, c : c + WIDE] = nt(d_y[...], w_out[c : c + WIDE, :]).astype(BF16)
    up_half(place_ref, 1, context_0, context, d_y, d_y_1, give, inner // 2, 0, width // 2)


def keep_up_kernel(
    place_ref, x_mlp_0, x_mlp, d_hidden_0, d_hidden, context_0, context, d_y_0, d_y, keep, g_bias_up
):
    width, inner = x_mlp.shape[1], d_hidden.shape[1]
    up_half(place_ref, 0, x_mlp_0, x_mlp, d_hidden_0, d_hidden, keep, 0, 0, inner // 2)
    up_half(place_ref, 0, context_0, context, d_y_0, d_y, keep, inner // 2, 0, width // 2)
    ones = jnp.ones((16, x_mlp.shape[0]), BF16)
    length = x_mlp_0.shape[0]

    def step(j, _):
        c = cols(j, 768)
        g_bias_up[:, c] = (nn(ones[:, :length], d_hidden_0[:, c]) + nn(ones, d_hidden[:, c]))[:1]

    lax.fori_loop(0, g_bias_up.shape[1] // 768, step, None)


def last_kernel(
    place_ref, vec, w_qkv, q, k, v, probs, context_0, d_context, d_y_0, d_y, d_mixed, entry, k_grad_0, v_grad_0, state_in,
    g_vec_in, g_bias_up,
    token_grad, d_mixed_0, small,
    k_grad, v_grad, state, g_vec, extra, scores, d_scores,
):
    length, width = state.shape
    k_grad[...] = k_grad_0[...]
    v_grad[...] = v_grad_0[...]
    state[...] = state_in[...]
    g_vec[...] = g_vec_in[...]

    def pair_back(j, _):
        attend_back(
            j, q, k, v, probs, scores, d_scores, d_context, context_0, 0, length, d_mixed_0, k_grad, v_grad, False
        )

    lax.fori_loop(0, width // PAIR, pair_back, None, unroll=3)
    for b in range(0, length, 64):
        part = slice(b, b + 64)
        d_mixed_0[part, width : 2 * width] = (k_grad[part, :] * SCALE).astype(BF16)
        d_mixed_0[part, 2 * width :] = v_grad[part, :].astype(BF16)
    for c in range(0, width, WIDE):
        extra[:, c : c + WIDE] = nt(d_mixed_0[...], w_qkv[c : c + WIDE, :])
    norm_backward(entry, 0, extra, state, vec, GAIN_ATTN, SHIFT_ATTN, g_vec, None, 0, EMBED)
    for b in range(0, length, 64):
        token_grad[b : b + 64, :] = state[b : b + 64, :].astype(BF16)

    ones = jnp.ones((16, 2 * length), BF16)

    def sums(d_0, d):
        return (nn(ones[:, :length], d_0) + nn(ones, d))[:1]

    g_vec[BIAS_Q : BIAS_Q + 1, :] = sums(d_mixed_0[:, :width], d_mixed[:, :width])
    g_vec[BIAS_V : BIAS_V + 1, :] = sums(d_mixed_0[:, 2 * width :], d_mixed[:, 2 * width :])
    g_vec[BIAS_OUT : BIAS_OUT + 1, :] = sums(d_y_0[...], d_y[...])
    vectors = g_vec[...].astype(BF16)
    four = []
    for b in range(g_bias_up.shape[1] // WIDE):
        four.append(jnp.where(own_lanes(), g_bias_up[:, b * WIDE : (b + 1) * WIDE], 0.0).astype(BF16))
    second = tn(vectors, pick_vectors(4 - EMBED, EMBED, EMBED + PASSES)) + nt(
        jnp.concatenate(four, axis=0), spread_four()
    )
    small[:, : SMALL // 2] = tn(vectors, pick_vectors(0, 0, EMBED)).astype(BF16)
    small[:, SMALL // 2 :] = second.astype(BF16)


def qkv_kernel(swapped, place_ref, x_norm_0, x_norm, d_mixed_0, d_mixed, small, target):
    wide = d_mixed.shape[1] // 2
    up_half(place_ref, swapped, x_norm_0, x_norm, d_mixed_0, d_mixed, target, 0, 0, wide)
    side = SMALL // 2
    put_blocks(place_ref, swapped, target, small[:, pl.ds(half_start(place_ref, swapped, side), side)], 0, wide)


def call(kernel, name, inputs, outputs, scratch, flops, touched):
    size = lambda shape, dtype: math.prod(shape) * jnp.dtype(dtype).itemsize
    need = sum(size(*s) for s in scratch if isinstance(s, tuple))
    results = [pltpu.VMEM(shape, dtype) if stays else jax.ShapeDtypeStruct(shape, dtype) for shape, dtype, stays in outputs]
    extra = sum(size(shape, dtype) for shape, dtype, stays in outputs if not stays)
    return pl.pallas_call(
        kernel,
        out_shape=results,
        in_specs=[pl.BlockSpec(memory_space=memory) for _, memory in inputs],
        out_specs=[pl.BlockSpec(memory_space=pltpu.VMEM)] * len(outputs),
        scratch_shapes=[pltpu.VMEM(*s) if isinstance(s, tuple) else s for s in scratch],
        compiler_params=pltpu.CompilerParams(vmem_limit_bytes=need + extra + 4 * 2**20),
        cost_estimate=pl.CostEstimate(flops=flops, bytes_accessed=touched, transcendentals=0),
        name=name,
    )(*[array for array, _ in inputs])


def layer(place, lengths, tokens, cotangent, chunks):
    length, width = tokens.shape
    inner = 16 * chunks[2][0].shape[2]
    rest = (PASSES - 1) * length
    heads = width // PAIR
    anywhere, local, scalars = pl.ANY, pltpu.VMEM, pltpu.SMEM
    place = (place, scalars)
    L = lambda *arrays: [(a, local) for a in arrays]

    G = lambda n: [(a, anywhere) for a in chunks[n]]
    low = lambda *shape: (shape, BF16)
    full = lambda *shape: (shape, F32)
    kept = lambda *specs: [(*s, True) for s in specs]
    out = lambda *specs: [(*s, False) for s in specs]
    semaphores = lambda n: pltpu.SemaphoreType.DMA((n,))
    row, row32 = low(length, width), full(length, width)
    part = 2 * length * width

    far_pieces(chunks[0])
    mate_pieces(chunks[0])
    far_pieces(chunks[1])
    w_qkv, vec, bias_up, mask, x_norm_0, q_0, k_0, v_0, probs_0, context_0, entry_0 = call(
        start_kernel, "start",
        [place, (lengths, scalars)] + L(tokens) + G(0),
        kept(
            low(width, 3 * width), full(VECTORS, width), full(1, inner), full(length, PASSES * length), row, row, row, row,
            low(heads, 2 * length, length), row, row32,
        ),
        [low(width, SMALL), full(2 * length, length), semaphores(2)],
        20 * 10**9, 70 * 2**20,
    )
    far_pieces(chunks[2])
    mate_pieces(chunks[1])
    w_up, w_out, middle_0, x_mlp_0, active_0, slope_0 = call(
        up_kernel, "up",
        [place] + L(context_0, vec, bias_up, entry_0) + G(1),
        kept(low(width, inner), low(width, width), row32, row, low(length, inner), low(length, inner)),
        [semaphores(2)],
        12 * 10**9, 40 * 2**20,
    )
    mate_pieces(chunks[2], context_0)
    (
        output, state, g_vec, x_norm, context, x_mlp, active, d_hidden_0, d_hidden, d_z, d_y, d_mixed, k_grad, v_grad,
    ) = call(
        main_kernel, "main",
        [place] + L(cotangent, vec, bias_up, mask, w_qkv, w_out, w_up, k_0, v_0, middle_0, active_0, slope_0) + G(2),
        out(row) + kept(
            row32, full(VECTORS, width), low(rest, width), low(rest, width), low(rest, width), low(rest, inner),
            low(length, inner), low(rest, inner), low(rest + length, width), low(rest, width), low(rest, 3 * width),
            row32, row32,
        ),
        [
            low(inner, width), low(rest, width), low(rest + length, width), low(rest + length, width),
            low(heads, 2 * length, 2 * length), low(heads, 2 * length, 3 * length), full(rest, width), full(rest, width),
            full(rest + length, width), full(rest + length, width), row32, row, full(2 * length, PASSES * length),
            low(2 * length, PASSES * length), semaphores(1),
        ],
        40 * part * inner, 60 * 2**20,
    )
    halves_ = []
    for kernel, name in ((give_down_kernel, "give_down"), (keep_down_kernel, "keep_down")):
        halves_ += call(
            kernel, name, [place] + L(active_0, active, after(d_z, *halves_)), kept(low(16, inner // 16, width // 2)), [],
            *COST,
        )
    begun = [begin_scatter(mate_step(halves_[0]), *halves_, MATE_WEIGHTS[0])]
    state = after(state, begun[0][0])
    begun[0] = far_step(begun[0])
    up_shape = low(16, width // 16, inner // 2 + width // 2)
    give_up, state, g_vec, d_y_0, d_context = call(
        give_up_kernel, "give_up",
        [place]
        + L(vec, w_up, w_out, x_mlp_0, x_mlp, d_hidden_0, d_hidden, middle_0, state, g_vec, context_0, context, d_y),
        kept(up_shape, row32, full(VECTORS, width), row, row), [row32],
        *COST,
    )
    keep_up, g_bias_up = call(
        keep_up_kernel, "keep_up",
        [place] + L(x_mlp_0, x_mlp, d_hidden_0, d_hidden, context_0, context, d_y_0, d_y),
        kept(up_shape, full(1, inner)), [],
        *COST,
    )
    begun.append(begin_scatter(mate_step(give_up), give_up, keep_up, MATE_WEIGHTS[1]))
    state = after(state, begun[0][0])
    near_0 = near_step(begun[0], FAR_WEIGHTS[0])
    state = after(state, begun[1][0])
    begun[1] = far_step(begun[1])
    token_grad, d_mixed_0, g_small = call(
        last_kernel, "last",
        [place]
        + L(
            vec, w_qkv, q_0, k_0, v_0, probs_0, context_0, d_context, d_y_0, d_y, d_mixed, entry_0, k_grad, v_grad, state,
            g_vec, g_bias_up,
        ),
        out(row) + kept(low(length, 3 * width), low(width, SMALL)),
        [
            row32, row32, row32, full(VECTORS, width), row32, full(2 * length, length), low(2 * length, length),
        ],
        40 * 10**9, 140 * 2**20,
    )
    last_shape = low(16, width // 16, 3 * width // 2 + SMALL // 2)
    ends = []
    for name, swapped in (("give_qkv", 1), ("keep_qkv", 0)):
        earlier = ends if ends else near_0[:1]
        ends += call(
            functools.partial(qkv_kernel, swapped), name,
            [place] + L(x_norm_0, x_norm, d_mixed_0, d_mixed, after(g_small, *earlier)), kept(last_shape), [], TINY, TINY,
        )
    give, keep = begin_scatter(mate_step(ends[0]), *ends, MATE_WEIGHTS[2])
    near_0 = (near_0[0], after(near_0[1], give))
    return output, token_grad, (near_0, begun[1], far_step((give, keep)))


def per_device(
    tokens,
    lengths,
    cotangent,
    w_qkv,
    bias_q,
    bias_v,
    w_out,
    bias_out,
    gain_attn,
    shift_attn,
    gain_mlp,
    shift_mlp,
    w_up,
    bias_up,
    w_down,
    bias_down,
    pass_embed,
):
    small = pack_small(
        [bias_q, bias_v, bias_out, gain_attn, shift_attn, gain_mlp, shift_mlp, bias_down], bias_up, pass_embed
    )
    place, chunks, last_z = gather_all(w_qkv, w_out, small, w_up, w_down)
    output, token_grad, parts = layer(place, lengths[0], tokens, cotangent, chunks)
    g_qkv, g_out, g_up, g_down, g_small = scatter_all(parts)
    (g_bq, g_bv, g_bo, g_ga, g_sa, g_gm, g_sm, g_bd), g_bu, g_pe = unpack_small(g_small)
    return (
        output,
        token_grad,
        g_qkv,
        g_bq,
        g_bv,
        g_out,
        g_bo,
        g_ga,
        g_sa,
        g_gm,
        g_sm,
        g_up,
        g_bu,
        g_down,
        g_bd,
        g_pe,
    )


def solution(mesh):
    placed = (
        P(("dp", "fsdp"), None),
        P(("dp", "fsdp"), None),
        P(("dp", "fsdp"), None),
        P(("dp", "fsdp"), None),
        P(("dp", "fsdp")),
        P(("dp", "fsdp")),
        P(("dp", "fsdp"), None),
        P(("dp", "fsdp")),
        P(("dp", "fsdp")),
        P(("dp", "fsdp")),
        P(("dp", "fsdp")),
        P(("dp", "fsdp")),
        P(("dp", "fsdp"), None),
        P(("dp", "fsdp")),
        P(("dp", "fsdp"), None),
        P(("dp", "fsdp")),
        P(None, ("dp", "fsdp")),
    )
    return jax.shard_map(
        per_device,
        mesh=mesh,
        in_specs=placed,
        out_specs=(
            P(("dp", "fsdp"), None),
            P(("dp", "fsdp"), None),
            P(("dp", "fsdp"), None),
            P(("dp", "fsdp")),
            P(("dp", "fsdp")),
            P(("dp", "fsdp"), None),
            P(("dp", "fsdp")),
            P(("dp", "fsdp")),
            P(("dp", "fsdp")),
            P(("dp", "fsdp")),
            P(("dp", "fsdp")),
            P(("dp", "fsdp"), None),
            P(("dp", "fsdp")),
            P(("dp", "fsdp"), None),
            P(("dp", "fsdp")),
            P(None, ("dp", "fsdp")),
        ),
        check_vma=False,
    )
```
